128 devices in a mesh: dp: 32 (over x, y_lo, z), tensor: 4 (over y_hi, core).
Axes of the slice: x: 4, y: 4 (y_hi: 2, y_lo: 2; y = y_hi * 2 + y_lo), z: 4, core: 2. Of those that a mesh axis runs over, the one named last changes fastest.
Arguments:
- tokens: bfloat16 [32768, 1536], P('dp'), may hold values from -6 to 6
- segment: int32 [32, 1024], P('dp'), may hold values from 0 to 3, never falling along the last dimension, each value on 1 to 512 neighbouring positions
- gate_proj: bfloat16 [1536, 3072], P(None, 'tensor'), may hold values from -0.15625 to 0.15625
- value_proj: bfloat16 [1536, 3072], P(None, 'tensor'), may hold values from -0.15625 to 0.15625
- state_proj: bfloat16 [1536, 256], replicated, may hold values from -0.15625 to 0.15625
- step_proj: bfloat16 [1536, 48], P(None, 'tensor'), may hold values from -0.15625 to 0.15625
- value_conv: float32 [4, 3072], P(None, 'tensor'), may hold values from -3 to 3
- value_conv_bias: float32 [3072], P('tensor'), may hold values from -3 to 3
- state_conv: float32 [4, 256], replicated, may hold values from -3 to 3
- state_conv_bias: float32 [256], replicated, may hold values from -3 to 3
- step_bias: float32 [48], P('tensor'), may hold values from -7 to -3
- log_rate: float32 [48], P('tensor'), may hold values from 0 to 2.3
- bypass_gain: float32 [48], P('tensor'), may hold values from 0.5 to 1.5
- norm_gain: float32 [1536], replicated, may hold values from 0.5 to 1.5
- gated_norm_gain: float32 [3072], P('tensor'), may hold values from 0.5 to 1.5
- out_proj: bfloat16 [3072, 1536], P('tensor'), may hold values from -0.109375 to 0.109375
- cotangent: bfloat16 [32768, 1536], P('dp'), may hold values from -6 to 6
Outputs:
- mixed_out: bfloat16 [32768, 1536], P('dp')
- grad_tokens: float32 [32768, 1536], P('dp')
- grad_gate_proj: float32 [1536, 3072], P(None, 'tensor')
- grad_value_proj: float32 [1536, 3072], P(None, 'tensor')
- grad_state_proj: float32 [1536, 256], replicated
- grad_step_proj: float32 [1536, 48], P(None, 'tensor')
- grad_value_conv: float32 [4, 3072], P(None, 'tensor')
- grad_value_conv_bias: float32 [3072], P('tensor')
- grad_state_conv: float32 [4, 256], replicated
- grad_state_conv_bias: float32 [256], replicated
- grad_step_bias: float32 [48], P('tensor')
- grad_log_rate: float32 [48], P('tensor')
- gradient_bypass_gain: float32 [48], P('tensor')
- grad_norm_gain: float32 [1536], replicated
- grad_mixer_gain: float32 [3072], P('tensor')
- grad_out_proj: float32 [3072, 1536], P('tensor')
The draws below stay inside these ranges and needn't reach their ends.
Inputs may be any that keep to these rules, and one draw needn't show every extreme that they name: `segment`: within each row of 1024 tokens the numbers never fall; each document has 1 to 512 tokens, and one has exactly that many.
All inputs are finite; a program needn't handle non-finite values.
Results may differ from the reference program's by a relative error of at most 0.025.
Values may be sent and summed in bfloat16 or wider, within the bound.
A program may use at most 192 MiB of HBM per device.

```python
import math
import jax
import jax.numpy as jnp
import numpy as np
from jax import lax

D = 1536
H = 48
P_SIZE = 64
N = 128
CONV = 4
SPAN = 256
SEQ_LEN = 1024
SEQS = 1
TOKENS = 32768
N_DP = 32


def level_of(own_key, shape, pieces, least, largest):
    loudness = 1.0
    for dim, parts in pieces:
        draws = jax.random.uniform(jax.random.fold_in(jax.random.fold_in(own_key, 6), dim), (parts,), jnp.float32, least / len(pieces), largest / len(pieces))
        loudness = loudness * jnp.repeat(jnp.exp(draws), shape[dim] // parts).reshape((-1,) + (1,) * (len(shape) - 1 - dim))
    return loudness


def split_up(amount, total, reach, lean):
    portions = [(1 << 20) // math.isqrt(rank ** lean) + 1 for rank in range(2, amount + 1)]
    spare, counts = total - reach - (amount - 1), [1] * (amount - 1)
    while spare > 0:
        free = [i for i in range(amount - 1) if counts[i] < reach]
        mass, remaining = sum([portions[i] for i in free]), spare
        for i in free:
            more = min(reach - counts[i], max(1, remaining * portions[i] // mass), spare)
            counts[i] = counts[i] + more
            spare = spare - more
    return np.array([reach] + counts)


def ragged_sizes(rng, amount, total, bound, slope):
    if amount == 2:
        one = jax.random.randint(rng, (), max(1, total - bound), min(bound, total - 1) + 1)
        return jnp.stack([one, total - one])
    lengths = jnp.asarray(split_up(amount, total, bound, slope), jnp.int32)
    pairs = (amount - 1) // 2
    donor, receiver = lengths[1:1 + 2 * pairs:2], lengths[2:2 + 2 * pairs:2]
    room = jnp.minimum(donor - 1, bound - receiver)
    passed = jax.random.randint(jax.random.fold_in(rng, 1), (pairs,), 0, 1 << 20) % (room + 1)
    lengths = lengths.at[1:1 + 2 * pairs:2].set(donor - passed).at[2:2 + 2 * pairs:2].set(receiver + passed)
    return lengths[jax.random.permutation(jax.random.fold_in(rng, 2), amount)]


def gaussian(stream_key, dims, spread, reach, split=(), kind=jnp.bfloat16):
    values = spread * jax.random.normal(stream_key, dims, jnp.float32)
    if split:
        values = values * level_of(stream_key, dims, split, -0.22, 0.18)
    return jnp.clip(values, -reach, reach).astype(kind)


def setup_inputs(seed: int = 0) -> dict:
    streams_of = jax.random.split(jax.random.key(seed), 18)
    tokens = gaussian(streams_of[0], (TOKENS, D), 1.0, 6.0, ((0, 32),))
    segment = jax.vmap(lambda own: jnp.searchsorted(jnp.cumsum(ragged_sizes(own, 4, SEQ_LEN, SEQ_LEN // 2, 0)), jnp.arange(SEQ_LEN), side="right"))(jax.random.split(streams_of[1], (SEQS * N_DP))).reshape((SEQS * N_DP, SEQ_LEN)).astype(jnp.int32)
    gate_proj = gaussian(streams_of[2], (D, H * P_SIZE), D ** -0.5, 0.15625, ((1, 4),))
    value_proj = gaussian(streams_of[3], (D, H * P_SIZE), D ** -0.5, 0.15625, ((1, 4),))
    state_proj = gaussian(streams_of[4], (D, 2 * N), D ** -0.5, 0.15625)
    step_proj = gaussian(streams_of[5], (D, H), D ** -0.5, 0.15625, ((1, 4),))
    value_conv = gaussian(streams_of[6], (CONV, H * P_SIZE), CONV ** -0.5, 3.0, ((1, 4),), jnp.float32)
    value_conv_bias = gaussian(streams_of[7], (H * P_SIZE,), 0.5, 3.0, ((0, 4),), jnp.float32)
    state_conv = gaussian(streams_of[8], (CONV, 2 * N), CONV ** -0.5, 3.0, (), jnp.float32)
    state_conv_bias = gaussian(streams_of[9], (2 * N,), 0.5, 3.0, (), jnp.float32)
    step_bias = jnp.clip(-7.0 + 4.0 * jax.random.uniform(streams_of[10], (H,), jnp.float32) ** level_of(streams_of[10], (H,), ((0, 4),), -0.2, 0.2), -7.0, -3.0)
    log_rate = jnp.clip(2.3 * jax.random.uniform(streams_of[11], (H,), jnp.float32) ** level_of(streams_of[11], (H,), ((0, 4),), -0.2, 0.2), 0.0, 2.3)
    bypass_gain = jnp.clip(0.5 + 1.0 * jax.random.uniform(streams_of[12], (H,), jnp.float32) ** level_of(streams_of[12], (H,), ((0, 4),), -0.2, 0.2), 0.5, 1.5)
    norm_gain = jnp.clip(1.0 + 0.1 * jax.random.normal(streams_of[13], (D,), jnp.float32), 0.5, 1.5)
    gated_norm_gain = jnp.clip(1.0 + 0.1 * jax.random.normal(streams_of[14], (H * P_SIZE,), jnp.float32), 0.5, 1.5)
    out_proj = gaussian(streams_of[15], (H * P_SIZE, D), (H * P_SIZE) ** -0.5, 0.109375, ((0, 4),))
    cotangent = gaussian(streams_of[16], (TOKENS, D), 1.0, 6.0, ((0, 32),))
    return {"tokens": tokens, "segment": segment, "gate_proj": gate_proj, "value_proj": value_proj, "state_proj": state_proj, "step_proj": step_proj, "value_conv": value_conv, "value_conv_bias": value_conv_bias, "state_conv": state_conv, "state_conv_bias": state_conv_bias, "step_bias": step_bias, "log_rate": log_rate, "bypass_gain": bypass_gain, "norm_gain": norm_gain, "gated_norm_gain": gated_norm_gain, "out_proj": out_proj, "cotangent": cotangent}


EPS = 1e-05
HIGH_ACCURACY = lax.Precision.HIGHEST

@jax.custom_vjp
def low(v):
    return lax.optimization_barrier(v.astype(jnp.bfloat16)).astype(jnp.float32)

@jax.custom_vjp
def low_back(v):
    return v

def low_keep(v):
    return (low(v), None)

def low_pass(kept, grad):
    return (grad,)

def back_keep(v):
    return (v, None)

def back_low(kept, grad):
    return (low(grad),)
low.defvjp(low_keep, low_pass)
low_back.defvjp(back_keep, back_low)

def causal_conv(values, kernel, offset, segment):
    length = values.shape[0]
    summed = offset + kernel[0] * values
    for lag_count in range(1, kernel.shape[0]):
        shifted = jnp.pad(values, ((lag_count, 0), (0, 0)))[:length]
        earlier = jnp.pad(segment, (lag_count, 0), constant_values=-1)[:length]
        keeper = (earlier == segment).astype(jnp.float32)[:, None]
        summed = summed + kernel[lag_count] * shifted * keeper
    return jax.nn.silu(summed)

def state_space(values, step_sizes, decay_rate, in_state, final_state, segment):
    length, head_count, head_dim = values.shape
    blocks = length // SPAN
    blocked = values.reshape(blocks, SPAN, head_count, head_dim)
    step_blocks = jnp.transpose(step_sizes.reshape(blocks, SPAN, head_count), (0, 2, 1))
    log_decay = step_blocks * decay_rate[None, :, None]
    row_index = lax.broadcasted_iota(jnp.int32, (SPAN, SPAN), 0)
    column_position = lax.broadcasted_iota(jnp.int32, (SPAN, SPAN), 1)
    lower_ones = (row_index >= column_position).astype(jnp.float32)
    cumulative = jnp.einsum('khs,ts->kht', log_decay, lower_ones, precision=HIGH_ACCURACY)
    seg_blocks = segment.reshape(blocks, SPAN)
    same_doc = (seg_blocks[:, :, None] == seg_blocks[:, None, :]) & (row_index >= column_position)[None]
    log_gap = cumulative[:, :, :, None] - cumulative[:, :, None, :]
    decay_mat = jnp.exp(jnp.where(same_doc[:, None], log_gap, -1e+30))
    in_blocks = in_state.reshape(blocks, SPAN, -1)
    out_blocks = final_state.reshape(blocks, SPAN, -1)
    scores = jnp.einsum('ktn,ksn->kts', out_blocks, in_blocks, precision=HIGH_ACCURACY)
    weights = scores[:, None] * decay_mat * step_blocks[:, :, None, :]
    inside = jnp.einsum('khts,kshp->kthp', weights, blocked, precision=HIGH_ACCURACY)
    last_doc = seg_blocks[:, -1]
    keep_end = (seg_blocks == last_doc[:, None]).astype(jnp.float32)
    tail_weight = jnp.exp(cumulative[:, :, -1:] - cumulative) * step_blocks * keep_end[:, None, :]
    states = jnp.einsum('khs,kshp,ksn->khpn', tail_weight, blocked, in_blocks, precision=HIGH_ACCURACY)
    through = jnp.exp(cumulative[:, :, -1])
    carried = jnp.zeros((head_count, head_dim, in_state.shape[1]), jnp.float32)
    entering = []
    for block_id in range(blocks):
        entering.append(carried)
        if block_id == 0:
            carried = states[0]
        else:
            continues = last_doc[block_id] == last_doc[block_id - 1]
            carried = states[block_id] + jnp.where(continues, through[block_id][:, None, None] * carried, 0.0)
    before = jnp.stack(entering)
    prev_last = jnp.concatenate([jnp.full((1,), -1, jnp.int32), last_doc[:-1].astype(jnp.int32)])
    keep_start = (seg_blocks == prev_last[:, None]).astype(jnp.float32)
    growth = jnp.exp(cumulative) * keep_start[:, None, :]
    outside = jnp.einsum('ktn,khpn,kht->kthp', out_blocks, before, growth, precision=HIGH_ACCURACY)
    return (inside + outside).reshape(length, head_count, head_dim)

def mixer(value_in, state_in, step_in, value_kernel, value_offset, state_kernel, state_offset, step_offset, rate_log, skip_weight, segment):
    length = value_in.shape[0]
    conv_values = causal_conv(value_in, value_kernel, value_offset, segment)
    conv_state = causal_conv(state_in, state_kernel, state_offset, segment)
    head_count = step_offset.shape[0]
    state_size = conv_state.shape[1] // 2
    step_sizes = jax.nn.softplus(step_in + step_offset)
    decay_rate = -jnp.exp(rate_log)
    heads_view = conv_values.reshape(length, head_count, -1)
    result = state_space(heads_view, step_sizes, decay_rate, conv_state[:, :state_size], conv_state[:, state_size:], segment)
    result = result + skip_weight[None, :, None] * heads_view
    return result.reshape(length, -1)

def apply_mixer(value_in, state_in, step_in, value_kernel, value_offset, state_kernel, state_offset, step_offset, rate_log, skip_weight, segment):
    mapped = jax.vmap(mixer, in_axes=(0, 0, 0, None, None, None, None, None, None, None, 0))
    return mapped(value_in, state_in, step_in, value_kernel, value_offset, state_kernel, state_offset, step_offset, rate_log, skip_weight, segment)

def project(left_operand, right_operand):
    return jnp.einsum('yav,vt->yat', left_operand, right_operand, precision=HIGH_ACCURACY)

def layer(tokens, gate_proj, value_proj, state_proj, step_proj, value_conv, value_conv_bias, state_conv, state_conv_bias, step_bias, log_rate, bypass_gain, norm_gain, gated_norm_gain, out_proj, segment):
    inverse = lax.rsqrt(lax.optimization_barrier(jnp.mean(tokens * tokens, -1, keepdims=True)) + EPS)
    normed = low(tokens * inverse * norm_gain)
    gate_raw = low_back(project(normed, gate_proj))
    value_raw = low_back(project(normed, value_proj))
    state_raw = low_back(project(normed, state_proj))
    step_raw = low_back(project(normed, step_proj))
    mixed_y = apply_mixer(value_raw, state_raw, step_raw, value_conv, value_conv_bias, state_conv, state_conv_bias, step_bias, log_rate, bypass_gain, segment)
    gated = mixed_y * jax.nn.silu(gate_raw)
    gate_scale = lax.rsqrt(lax.optimization_barrier(jnp.mean(gated * gated, -1, keepdims=True)) + EPS)
    gate_normed = low(gated * gate_scale * gated_norm_gain)
    branch = low_back(project(gate_normed, out_proj))
    return tokens + branch

def reference(tokens, segment, gate_proj, value_proj, state_proj, step_proj, value_conv, value_conv_bias, state_conv, state_conv_bias, step_bias, log_rate, bypass_gain, norm_gain, gated_norm_gain, out_proj, cotangent):
    params = tuple((weight_arg.astype(jnp.float32) for weight_arg in (gate_proj, value_proj, state_proj, step_proj, value_conv, value_conv_bias, state_conv, state_conv_bias, step_bias, log_rate, bypass_gain, norm_gain, gated_norm_gain, out_proj)))
    whole = tokens.astype(jnp.float32).reshape(N_DP, SEQS, SEQ_LEN, D)
    documents = segment.astype(jnp.int32).reshape(N_DP, SEQS, SEQ_LEN)
    upstream = cotangent.astype(jnp.float32).reshape(N_DP, SEQS, SEQ_LEN, D)
    zeros_start = tuple((jnp.zeros(weight_arg.shape, jnp.float32) for weight_arg in params))

    def group(totals, group_item):
        group_tokens, group_docs, group_up = group_item

        def forward(*inputs):
            return layer(*inputs, group_docs)
        result, pullback = jax.vjp(forward, group_tokens, *params)
        grads = pullback(group_up)
        totals = tuple((running + low(partial_grad) for running, partial_grad in zip(totals, grads[1:])))
        return (totals, (result.astype(jnp.bfloat16), grads[0]))
    totals, outputs = lax.scan(group, zeros_start, (whole, documents, upstream))
    results = outputs[0].reshape(TOKENS, D)
    input_grads = outputs[1].reshape(TOKENS, D)
    return (results, input_grads, totals[0], totals[1], totals[2], totals[3], totals[4], totals[5], totals[6], totals[7], totals[8], totals[9], totals[10], totals[11], totals[12], totals[13])
```

```python
import functools

import jax
import jax.numpy as jnp
from jax import lax
from jax.experimental import pallas as pl
from jax.experimental.pallas import tpu as pltpu
from jax.sharding import PartitionSpec as P

H = 48
P_SIZE = 64
SPAN = 256


EPS = 1e-05
HIGH_ACCURACY = lax.Precision.HIGHEST


MESH_ID = pl.DeviceIdType.MESH


def place():
    dp = lax.axis_index("dp")
    tensor = lax.axis_index("tensor")
    return {"x": dp // 8, "y": (dp // 4) % 2, "z": dp % 4, "t": tensor}


def device_at(at, **moved):
    spot = dict(at, **moved)
    return (spot["x"] * 8 + spot["y"] * 4 + spot["z"], spot["t"])


def greet(peers):
    barrier = pltpu.get_barrier_semaphore()
    for peer in peers:
        pl.semaphore_signal(barrier, inc=1, device_id=peer, device_id_type=MESH_ID)
    pl.semaphore_wait(barrier, len(peers))


def dp_peers(at):
    return [
        device_at(at, x=(at["x"] + 1) % 4),
        device_at(at, x=(at["x"] + 3) % 4),
        device_at(at, z=(at["z"] + 1) % 4),
        device_at(at, z=(at["z"] + 3) % 4),
        device_at(at, y=1 - at["y"]),
    ]


def tensor_peers(at):
    return [device_at(at, t=(at["t"] + step) % 4) for step in (1, 2, 3)]


def added(*refs):
    total = refs[0][...].astype(jnp.float32)
    for ref in refs[1:]:
        total = total + ref[...].astype(jnp.float32)
    return total.astype(jnp.bfloat16)


class SumOverDp:
    def __init__(self, at, buf, res, tmps, send, recv, first, order, tensor_rows=None, tensor_tmp=None):
        self.at, self.buf, self.res, self.tmps = at, buf, res, tmps
        self.send, self.recv, self.next = send, recv, first
        self.a_axis, self.b_axis = order
        self.tensor_rows, self.tensor_tmp = tensor_rows, tensor_tmp
        self.stage = 0
        self.flying = []

    def copy(self, src, dst, peer):
        cp = pltpu.make_async_remote_copy(
            src_ref=src,
            dst_ref=dst,
            send_sem=self.send.at[self.next],
            recv_sem=self.recv.at[self.next],
            device_id=peer,
            device_id_type=MESH_ID,
        )
        self.next += 1
        cp.start()
        self.flying.append(cp)

    def start(self):
        at, buf, res = self.at, self.buf, self.res
        a, b, y = at[self.a_axis], at[self.b_axis], at["y"]
        a_up, a_down, a_far = (a + 1) % 4, (a + 3) % 4, (a + 2) % 4
        b_up, b_down, b_far = (b + 1) % 4, (b + 3) % 4, (b + 2) % 4
        a_right, a_left = device_at(at, **{self.a_axis: a_up}), device_at(at, **{self.a_axis: a_down})
        b_right, b_left = device_at(at, **{self.b_axis: b_up}), device_at(at, **{self.b_axis: b_down})
        other = device_at(at, y=1 - y)
        ta1, ta2, tb1, tb2, ty = self.tmps
        low, high = pl.ds(0, 2), pl.ds(2, 2)
        if self.stage == 0:
            self.copy(buf.at[a_far, low], ta1.at[0], a_right)
            self.copy(buf.at[a_far, high], ta1.at[1], a_left)
        elif self.stage == 1:
            self.copy(buf.at[a_up], ta2.at[0], a_right)
            self.copy(buf.at[a_down], ta2.at[1], a_left)
        elif self.stage == 2:
            self.copy(buf.at[a, b_far, 0], tb1.at[0], b_right)
            self.copy(buf.at[a, b_far, 1], tb1.at[1], b_left)
        elif self.stage == 3:
            self.copy(buf.at[a, b_up], tb2.at[0], b_right)
            self.copy(buf.at[a, b_down], tb2.at[1], b_left)
        elif self.stage == 4:
            self.copy(buf.at[a, b, 1 - y], ty, other)
        elif self.stage == 5:
            if self.tensor_rows is not None:
                for peer in tensor_peers(at):
                    self.copy(res.at[a, b, y, self.tensor_rows], self.tensor_tmp.at[at["t"]], peer)
        elif self.stage == 6:
            self.copy(res.at[a, b, y], res.at[a, b, y], other)
        elif self.stage == 7:
            self.copy(res.at[a, b], res.at[a, b], b_right)
            self.copy(res.at[a, b], res.at[a, b], b_left)
        elif self.stage == 8:
            self.copy(res.at[a, b_down, 0], res.at[a, b_down, 0], b_right)
            self.copy(res.at[a, b_up, 1], res.at[a, b_up, 1], b_left)
        elif self.stage == 9:
            self.copy(res.at[a], res.at[a], a_right)
            self.copy(res.at[a], res.at[a], a_left)
        elif self.stage == 10:
            self.copy(res.at[a_down, low], res.at[a_down, low], a_right)
            self.copy(res.at[a_up, high], res.at[a_up, high], a_left)

    def finish(self):
        for cp in self.flying:
            cp.wait()
        self.flying = []
        at, buf, res = self.at, self.buf, self.res
        a, b, y = at[self.a_axis], at[self.b_axis], at["y"]
        a_up, a_down = (a + 1) % 4, (a + 3) % 4
        b_up, b_down = (b + 1) % 4, (b + 3) % 4
        ta1, ta2, tb1, tb2, ty = self.tmps
        if self.stage == 0:
            for j in range(2):
                for k in range(2):
                    buf[a_up, j, k] = added(buf.at[a_up, j, k], ta1.at[0, j, k])
                    buf[a_down, 2 + j, k] = added(buf.at[a_down, 2 + j, k], ta1.at[1, j, k])
        elif self.stage == 1:
            for j in range(4):
                for k in range(2):
                    buf[a, j, k] = added(buf.at[a, j, k], ta2.at[0, j, k], ta2.at[1, j, k])
        elif self.stage == 2:
            buf[a, b_up, 0] = added(buf.at[a, b_up, 0], tb1.at[0])
            buf[a, b_down, 1] = added(buf.at[a, b_down, 1], tb1.at[1])
        elif self.stage == 3:
            for k in range(2):
                buf[a, b, k] = added(buf.at[a, b, k], tb2.at[0, k], tb2.at[1, k])
        elif self.stage == 4:
            res[a, b, y] = added(buf.at[a, b, y], ty)
        elif self.stage == 5 and self.tensor_rows is not None:
            self.tensor_tmp[at["t"]] = res[a, b, y, self.tensor_rows]
            res[a, b, y, self.tensor_rows] = added(*(self.tensor_tmp.at[k] for k in range(4)))
        self.stage += 1


STAGES = 11


def dp_tmps(rows, width):
    block = (rows, width)
    return [
        pltpu.VMEM((2, 2, 2) + block, jnp.bfloat16),
        pltpu.VMEM((2, 4, 2) + block, jnp.bfloat16),
        pltpu.VMEM((2,) + block, jnp.bfloat16),
        pltpu.VMEM((2, 2) + block, jnp.bfloat16),
        pltpu.VMEM(block, jnp.bfloat16),
    ]


def sum_kernel(rows, kept, width, tensor_rows, big_in, small_in, big_out, small_out, buf, small, res, small_res, sa1, sa2, sb1, sb2, sy, ta1, ta2, tb1, tb2, ty, ua1, ua2, ub1, ub2, uy, tt0, tt1, tts, send, recv, local):
    at = place()
    greet(dp_peers(at) + tensor_peers(at))
    loads = [pltpu.make_async_copy(big_in, buf, local.at[0]), pltpu.make_async_copy(small_in, small, local.at[1])]
    for cp in loads:
        cp.start()
    for cp in loads:
        cp.wait()
    engines = [
        SumOverDp(at, buf.at[0], res.at[0], (ta1, ta2, tb1, tb2, ty), send, recv, 0, ("x", "z"), pl.ds(kept, rows - kept), tt0),
        SumOverDp(at, buf.at[1], res.at[1], (ua1, ua2, ub1, ub2, uy), send, recv, 32, ("z", "x"), pl.ds(kept, rows - kept), tt1),
        SumOverDp(at, small, small_res, (sa1, sa2, sb1, sb2, sy), send, recv, 64, ("x", "z"), pl.ds(tensor_rows, 16), tts),
    ]
    for _ in range(STAGES):
        for engine in engines:
            engine.start()
        for engine in engines:
            engine.finish()
    stores = [pltpu.make_async_copy(res, big_out, local.at[0]), pltpu.make_async_copy(small_res, small_out, local.at[1])]
    for cp in stores:
        cp.start()
    for cp in stores:
        cp.wait()


def summed_over_dp(big, small, kept):
    rows, width = big.shape[4:]
    return pl.pallas_call(
        functools.partial(sum_kernel, rows, kept, width, 16),
        out_shape=(jax.ShapeDtypeStruct(big.shape, big.dtype), jax.ShapeDtypeStruct(small.shape, small.dtype)),
        in_specs=[pl.BlockSpec(memory_space=pl.ANY)] * 2,
        out_specs=[pl.BlockSpec(memory_space=pl.ANY)] * 2,
        scratch_shapes=[pltpu.VMEM(big.shape, big.dtype), pltpu.VMEM(small.shape, small.dtype)] * 2
        + dp_tmps(32, 128) + dp_tmps(rows, width) + dp_tmps(rows, width)
        + [pltpu.VMEM((4, rows - kept, width), jnp.bfloat16)] * 2
        + [pltpu.VMEM((4, 16, 128), jnp.bfloat16)]
        + [pltpu.SemaphoreType.DMA((96,)), pltpu.SemaphoreType.DMA((96,)), pltpu.SemaphoreType.DMA((2,))],
        compiler_params=pltpu.CompilerParams(collective_id=0, has_side_effects=True, vmem_limit_bytes=48 * 2**20),
        name="sum_over_dp",
    )(big, small)


def sent_to_all(shard, axis):
    copies = jnp.broadcast_to(shard, (lax.axis_size(axis), *shard.shape))
    return lax.all_to_all(copies, axis, split_axis=0, concat_axis=0, tiled=True)


def over_copies(shard, axis):
    everything = sent_to_all(shard, axis)
    return jnp.sum(everything, axis=0)


def in_blocks_2(shard, dim, count):
    lengths = shard.shape
    pieces = shard.reshape(*lengths[:dim], count, lengths[dim] // count, *lengths[dim + 1 :])
    return jnp.moveaxis(pieces, dim, 0)


def sum_at_owner(shard, axis, dim):
    pieces = in_blocks_2(shard, dim, lax.axis_size(axis))
    arrived = lax.all_to_all(pieces, axis, split_axis=0, concat_axis=0, tiled=True)
    return arrived.astype(jnp.float32).sum(axis=0)


def taken_together(shard, axis):
    return sent_to_all(shard, axis).astype(jnp.float32).sum(axis=0)


def causal_conv(values, kernel, offset, segment):
    length = values.shape[0]
    summed = offset + kernel[0] * values
    for lag_count in range(1, kernel.shape[0]):
        shifted = jnp.pad(values, ((lag_count, 0), (0, 0)))[:length]
        earlier = jnp.pad(segment, (lag_count, 0), constant_values=-1)[:length]
        keeper = (earlier == segment).astype(jnp.float32)[:, None]
        summed = summed + kernel[lag_count] * shifted * keeper
    return jax.nn.silu(summed)


def state_space(values, step_sizes, decay_rate, in_state, final_state, segment):
    length, head_count, head_dim = values.shape
    blocks = length // SPAN
    blocked = values.reshape(blocks, SPAN, head_count, head_dim)
    step_blocks = jnp.transpose(step_sizes.reshape(blocks, SPAN, head_count), (0, 2, 1))
    log_decay = step_blocks * decay_rate[None, :, None]
    row_index = lax.broadcasted_iota(jnp.int32, (SPAN, SPAN), 0)
    column_position = lax.broadcasted_iota(jnp.int32, (SPAN, SPAN), 1)
    lower_ones = (row_index >= column_position).astype(jnp.float32)
    cumulative = jnp.einsum("khs,ts->kht", log_decay, lower_ones, precision=HIGH_ACCURACY)
    seg_blocks = segment.reshape(blocks, SPAN)
    same_doc = (seg_blocks[:, :, None] == seg_blocks[:, None, :]) & (row_index >= column_position)[
        None
    ]
    log_gap = cumulative[:, :, :, None] - cumulative[:, :, None, :]
    decay_mat = jnp.exp(jnp.where(same_doc[:, None], log_gap, -1e30))
    in_blocks = in_state.reshape(blocks, SPAN, -1)
    out_blocks = final_state.reshape(blocks, SPAN, -1)
    scores = jnp.einsum("ktn,ksn->kts", out_blocks, in_blocks, precision=HIGH_ACCURACY)
    weights = scores[:, None] * decay_mat * step_blocks[:, :, None, :]
    inside = jnp.einsum("khts,kshp->kthp", weights, blocked, precision=HIGH_ACCURACY)
    last_doc = seg_blocks[:, -1]
    keep_end = (seg_blocks == last_doc[:, None]).astype(jnp.float32)
    tail_weight = jnp.exp(cumulative[:, :, -1:] - cumulative) * step_blocks * keep_end[:, None, :]
    states = jnp.einsum(
        "khs,kshp,ksn->khpn", tail_weight, blocked, in_blocks, precision=HIGH_ACCURACY
    )
    through = jnp.exp(cumulative[:, :, -1])
    carried = jnp.zeros((head_count, head_dim, in_state.shape[1]), jnp.float32)
    entering = []
    for block_id in range(blocks):
        entering.append(carried)
        if block_id == 0:
            carried = states[0]
        else:
            continues = last_doc[block_id] == last_doc[block_id - 1]
            carried = states[block_id] + jnp.where(
                continues, through[block_id][:, None, None] * carried, 0.0
            )
    before = jnp.stack(entering)
    prev_last = jnp.concatenate([jnp.full((1,), -1, jnp.int32), last_doc[:-1]])
    keep_start = (seg_blocks == prev_last[:, None]).astype(jnp.float32)
    growth = jnp.exp(cumulative) * keep_start[:, None, :]
    outside = jnp.einsum("ktn,khpn,kht->kthp", out_blocks, before, growth, precision=HIGH_ACCURACY)
    return (inside + outside).reshape(length, head_count, head_dim)


def mixer(
    value_in,
    state_in,
    step_in,
    value_kernel,
    value_offset,
    state_kernel,
    state_offset,
    step_offset,
    rate_log,
    skip_weight,
    segment,
):
    length = value_in.shape[0]
    conv_values = causal_conv(value_in, value_kernel, value_offset, segment)
    conv_state = causal_conv(state_in, state_kernel, state_offset, segment)
    head_count = step_offset.shape[0]
    state_size = conv_state.shape[1] // 2
    step_sizes = jax.nn.softplus(step_in + step_offset)
    decay_rate = -jnp.exp(rate_log)
    heads_view = conv_values.reshape(length, head_count, -1)
    result = state_space(
        heads_view,
        step_sizes,
        decay_rate,
        conv_state[:, :state_size],
        conv_state[:, state_size:],
        segment,
    )
    result = result + skip_weight[None, :, None] * heads_view
    return result.reshape(length, -1)


def apply_mixer(
    value_in,
    state_in,
    step_in,
    value_kernel,
    value_offset,
    state_kernel,
    state_offset,
    step_offset,
    rate_log,
    skip_weight,
    segment,
):
    mapped = jax.vmap(mixer, in_axes=(0, 0, 0, None, None, None, None, None, None, None, 0))
    return mapped(
        value_in,
        state_in,
        step_in,
        value_kernel,
        value_offset,
        state_kernel,
        state_offset,
        step_offset,
        rate_log,
        skip_weight,
        segment,
    )


def local(
    tokens,
    segment,
    gate_proj,
    value_proj,
    state_proj,
    step_proj,
    value_conv,
    value_conv_bias,
    state_conv,
    state_conv_bias,
    step_bias,
    log_rate,
    bypass_gain,
    norm_gain,
    gated_norm_gain,
    out_proj,
    cotangent,
):
    seq_count, length = segment.shape
    row_count, model_width = tokens.shape
    inner_width = H * P_SIZE
    hidden = tokens.astype(jnp.float32)
    inverse = lax.rsqrt(jnp.mean(hidden * hidden, -1, keepdims=True) + EPS)
    normed = (hidden * inverse * norm_gain).astype(jnp.bfloat16)
    gate_raw = jnp.dot(normed, gate_proj, preferred_element_type=jnp.float32)
    value_raw = jnp.dot(normed, value_proj, preferred_element_type=jnp.float32)
    state_raw = jnp.dot(normed, state_proj, preferred_element_type=jnp.float32)
    step_raw = jnp.dot(normed, step_proj, preferred_element_type=jnp.float32)

    def run_mixer(
        value_in,
        state_in,
        step_in,
        value_kernel,
        value_offset,
        state_kernel,
        state_offset,
        step_offset,
        rate_log,
        skip_weight,
    ):
        return apply_mixer(
            value_in,
            state_in,
            step_in,
            value_kernel,
            value_offset,
            state_kernel,
            state_offset,
            step_offset,
            rate_log,
            skip_weight,
            segment,
        )

    mixed_y, pull_mixer = jax.vjp(
        run_mixer,
        value_raw.reshape(seq_count, length, -1),
        state_raw.reshape(seq_count, length, -1),
        step_raw.reshape(seq_count, length, -1),
        value_conv,
        value_conv_bias,
        state_conv,
        state_conv_bias,
        step_bias,
        log_rate,
        bypass_gain,
    )
    mixed_y = mixed_y.reshape(row_count, -1)
    gate_act = jax.nn.silu(gate_raw)
    gated = mixed_y * gate_act
    grad_gate_normed = jnp.dot(cotangent, out_proj.T, preferred_element_type=jnp.float32)
    scaled = grad_gate_normed * gated_norm_gain
    sums = over_copies(jnp.stack([jnp.sum(gated * gated, -1), jnp.sum(scaled * gated, -1)]), "tensor")
    squares, cross = sums[0], sums[1]
    gate_scale = lax.rsqrt(squares[:, None] / inner_width + EPS)
    gate_normed = (gated * gate_scale * gated_norm_gain).astype(jnp.bfloat16)
    branch_part = jnp.dot(gate_normed, out_proj, preferred_element_type=jnp.float32)
    shared = sum_at_owner(branch_part.astype(jnp.bfloat16), "tensor", 0)
    share_rows = shared.shape[0]
    own_rows = lax.dynamic_slice_in_dim(
        hidden, lax.axis_index("tensor") * share_rows, share_rows, 0
    )
    mixed_out = lax.all_gather(
        (own_rows + shared).astype(jnp.bfloat16), "tensor", axis=0, tiled=True
    )
    upstream = cotangent.astype(jnp.float32)
    grad_out_proj = jnp.dot(gate_normed.T, cotangent, preferred_element_type=jnp.float32)
    grad_mixer_gain = jnp.sum(grad_gate_normed * gated * gate_scale, 0)
    grad_gated = (
        gate_scale * scaled
        - gated * gate_scale * gate_scale * gate_scale * cross[:, None] / inner_width
    )
    grad_y = grad_gated * gate_act
    logistic = jax.nn.sigmoid(gate_raw)
    grad_gate_raw = grad_gated * mixed_y * logistic * (1.0 + gate_raw * (1.0 - logistic))
    pulled = pull_mixer(grad_y.reshape(seq_count, length, -1))
    grad_value_raw, grad_state_part, grad_step_raw = (pulled[0], pulled[1], pulled[2])
    grad_value_conv, grad_value_conv_bias = (pulled[3], pulled[4])
    grad_step_bias, grad_log_rate, gradient_bypass_gain = (pulled[7], pulled[8], pulled[9])
    grad_state_raw, grad_state_conv, grad_state_conv_bias = grad_state_part.reshape(row_count, -1), pulled[5], pulled[6]
    gate_low = grad_gate_raw.astype(jnp.bfloat16)
    value_low = grad_value_raw.reshape(row_count, -1).astype(jnp.bfloat16)
    state_low = grad_state_raw.astype(jnp.bfloat16)
    step_low = grad_step_raw.reshape(row_count, -1).astype(jnp.bfloat16)
    grad_gate_proj = jnp.dot(normed.T, gate_low, preferred_element_type=jnp.float32)
    grad_value_proj = jnp.dot(normed.T, value_low, preferred_element_type=jnp.float32)
    grad_state_proj = jnp.dot(normed.T, state_low, preferred_element_type=jnp.float32)
    grad_step_proj = jnp.dot(normed.T, step_low, preferred_element_type=jnp.float32)
    normed_part = jnp.dot(gate_low, gate_proj.T, preferred_element_type=jnp.float32)
    normed_part = normed_part + jnp.dot(value_low, value_proj.T, preferred_element_type=jnp.float32)
    normed_part = normed_part + jnp.dot(step_low, step_proj.T, preferred_element_type=jnp.float32)
    normed_part = normed_part + jnp.dot(state_low, state_proj.T, preferred_element_type=jnp.float32)
    grad_norm_gain = jnp.sum(normed_part * hidden * inverse, 0)
    grad_normed = lax.psum(normed_part.astype(jnp.bfloat16), "tensor").astype(jnp.float32)
    scaled_in = grad_normed * norm_gain
    grad_tokens = (
        upstream
        + inverse * scaled_in
        - hidden
        * inverse
        * inverse
        * inverse
        * jnp.sum(scaled_in * hidden, -1, keepdims=True)
        / model_width
    )
    big = jnp.concatenate(
        [
            piece.astype(jnp.bfloat16).reshape(32, -1, 2, 384)
            for piece in (grad_gate_proj, grad_value_proj, grad_out_proj, grad_state_proj)
        ],
        axis=1,
    )
    big = jnp.transpose(big, (2, 0, 1, 3)).reshape(2, 4, 4, 2, 160, 384)
    own = (grad_step_proj, grad_value_conv, grad_value_conv_bias, grad_step_bias, grad_log_rate, gradient_bypass_gain, grad_mixer_gain)
    shared_by_all = (grad_state_conv, grad_state_conv_bias, grad_norm_gain)
    small = jnp.concatenate([packed(own), packed(shared_by_all)], axis=1).reshape(4, 4, 2, 32, 128)
    big, small = summed_over_dp(big, small, 144)
    big = jnp.transpose(big.reshape(2, 32, 160, 384), (1, 2, 0, 3)).astype(jnp.float32)
    small = small.reshape(32, 32, 128).astype(jnp.float32)
    sum_own = unpacked(small[:, :16], own)
    sum_shared = unpacked(small[:, 16:], shared_by_all)
    return (
        mixed_out,
        grad_tokens,
        big[:, :48].reshape(grad_gate_proj.shape),
        big[:, 48:96].reshape(grad_value_proj.shape),
        big[:, 144:].reshape(grad_state_proj.shape),
        sum_own[0],
        sum_own[1],
        sum_own[2],
        sum_shared[0],
        sum_shared[1],
        sum_own[3],
        sum_own[4],
        sum_own[5],
        sum_shared[2],
        sum_own[6],
        big[:, 96:144].reshape(grad_out_proj.shape),
    )


def packed(pieces):
    flat = jnp.concatenate([piece.reshape(-1).astype(jnp.bfloat16) for piece in pieces])
    return jnp.pad(flat, (0, 65536 - flat.shape[0])).reshape(32, 16, 128)


def unpacked(rows, like):
    flat, at, pieces = rows.reshape(-1), 0, []
    for piece in like:
        pieces.append(flat[at : at + piece.size].reshape(piece.shape))
        at += piece.size
    return pieces


def solution(mesh):
    placed = (
        P("dp", None),
        P("dp", None),
        P(None, "tensor"),
        P(None, "tensor"),
        P(),
        P(None, "tensor"),
        P(None, "tensor"),
        P("tensor"),
        P(),
        P(),
        P("tensor"),
        P("tensor"),
        P("tensor"),
        P(),
        P("tensor"),
        P("tensor", None),
        P("dp", None),
    )
    return jax.shard_map(
        local,
        mesh=mesh,
        in_specs=placed,
        out_specs=(
            P("dp", None),
            P("dp", None),
            P(None, "tensor"),
            P(None, "tensor"),
            P(),
            P(None, "tensor"),
            P(None, "tensor"),
            P("tensor"),
            P(),
            P(),
            P("tensor"),
            P("tensor"),
            P("tensor"),
            P(),
            P("tensor"),
            P("tensor", None),
        ),
        check_vma=False,
    )
```

```python
import jax
import jax.numpy as jnp
from jax import lax
from jax.experimental import pallas as pl
from jax.experimental.pallas import tpu as pltpu
from jax.sharding import PartitionSpec as P

EPS = 1e-05
MESH_ID = pl.DeviceIdType.MESH


def place():
    dp = lax.axis_index("dp")
    tensor = lax.axis_index("tensor")
    return {"x": dp // 8, "y": (dp // 4) % 2, "z": dp % 4, "t": tensor}


def device_at(at, **moved):
    spot = dict(at, **moved)
    return (spot["x"] * 8 + spot["y"] * 4 + spot["z"], spot["t"])


def dp_peers(at):
    return [
        device_at(at, x=(at["x"] + 1) % 4),
        device_at(at, x=(at["x"] + 3) % 4),
        device_at(at, z=(at["z"] + 1) % 4),
        device_at(at, z=(at["z"] + 3) % 4),
        device_at(at, y=1 - at["y"]),
    ]


def tensor_peers(at):
    return [device_at(at, t=(at["t"] + step) % 4) for step in (1, 2, 3)]


def greet(peers):
    barrier = pltpu.get_barrier_semaphore()
    for peer in peers:
        pl.semaphore_signal(barrier, inc=1, device_id=peer, device_id_type=MESH_ID)
    pl.semaphore_wait(barrier, len(peers))


def added(*refs):
    total = refs[0][...].astype(jnp.float32)
    for ref in refs[1:]:
        total = total + ref[...].astype(jnp.float32)
    return total.astype(jnp.bfloat16)


class Staged:
    def __init__(self, send, recv, first):
        self.send, self.recv, self.first = send, recv, first

    def made(self, stage):
        at = self.first + sum(self.counts[:stage])
        for n, (src, dst, peer) in enumerate(self.copies(stage)):
            if peer is None:
                yield pltpu.make_async_copy(src, dst, self.recv.at[at + n])
            else:
                yield pltpu.make_async_remote_copy(
                    src_ref=src,
                    dst_ref=dst,
                    send_sem=self.send.at[at + n],
                    recv_sem=self.recv.at[at + n],
                    device_id=peer,
                    device_id_type=MESH_ID,
                )

    def start(self, stage):
        for cp in self.made(stage):
            cp.start()

    def finish(self, stage):
        for cp in self.made(stage):
            cp.wait()
        self.settle(stage)


class SumOverDp(Staged):
    counts = (2, 2, 2, 2, 1, 3, 2, 2, 2, 2, 2)

    def __init__(self, at, order, buf, res, scratch, sems, tensor_from=None):
        super().__init__(*sems)
        self.at, self.buf, self.res, self.tensor_from = at, buf, res, tensor_from
        self.ta1, self.ta2, self.tb1, self.tb2, self.ty, self.own, self.tt = scratch
        a_axis, b_axis = order
        self.a, self.b, self.y = at[a_axis], at[b_axis], at["y"]
        self.a_up, self.a_down, self.a_far = [(self.a + n) % 4 for n in (1, 3, 2)]
        self.b_up, self.b_down, self.b_far = [(self.b + n) % 4 for n in (1, 3, 2)]
        self.a_right, self.a_left = [device_at(at, **{a_axis: n}) for n in (self.a_up, self.a_down)]
        self.b_right, self.b_left = [device_at(at, **{b_axis: n}) for n in (self.b_up, self.b_down)]
        self.other = device_at(at, y=1 - self.y)
        self.peers = tensor_peers(at)

    def copies(self, stage):
        buf, res, a, b, y = self.buf, self.res, self.a, self.b, self.y
        near, far = pl.ds(0, 2), pl.ds(2, 2)
        if stage == 0:
            return [(buf.at[self.a_far, near], self.ta1.at[0], self.a_right), (buf.at[self.a_far, far], self.ta1.at[1], self.a_left)]
        if stage == 1:
            return [(buf.at[self.a_up], self.ta2.at[0], self.a_right), (buf.at[self.a_down], self.ta2.at[1], self.a_left)]
        if stage == 2:
            return [(buf.at[a, self.b_far, 0], self.tb1.at[0], self.b_right), (buf.at[a, self.b_far, 1], self.tb1.at[1], self.b_left)]
        if stage == 3:
            return [(buf.at[a, self.b_up], self.tb2.at[0], self.b_right), (buf.at[a, self.b_down], self.tb2.at[1], self.b_left)]
        if stage == 4:
            return [(buf.at[a, b, 1 - y], self.ty, self.other)]
        if stage == 5:
            if self.tensor_from is None:
                return []
            rows = pl.ds(self.tensor_from, self.own.shape[0] - self.tensor_from)
            return [(self.own.at[rows], self.tt.at[self.at["t"]], peer) for peer in self.peers]
        if stage == 6:
            return [(self.own, res.at[a, b, y], self.other), (self.own, res.at[a, b, y], None)]
        if stage == 7:
            return [(res.at[a, b], res.at[a, b], self.b_right), (res.at[a, b], res.at[a, b], self.b_left)]
        if stage == 8:
            return [
                (res.at[a, self.b_down, 0], res.at[a, self.b_down, 0], self.b_right),
                (res.at[a, self.b_up, 1], res.at[a, self.b_up, 1], self.b_left),
            ]
        if stage == 9:
            return [(res.at[a], res.at[a], self.a_right), (res.at[a], res.at[a], self.a_left)]
        return [
            (res.at[self.a_down, near], res.at[self.a_down, near], self.a_right),
            (res.at[self.a_up, far], res.at[self.a_up, far], self.a_left),
        ]

    def settle(self, stage):
        buf, a, b, y = self.buf, self.a, self.b, self.y
        if stage == 0:
            for j in range(2):
                for k in range(2):
                    buf[self.a_up, j, k] = added(buf.at[self.a_up, j, k], self.ta1.at[0, j, k])
                    buf[self.a_down, 2 + j, k] = added(buf.at[self.a_down, 2 + j, k], self.ta1.at[1, j, k])
        elif stage == 1:
            for j in range(4):
                for k in range(2):
                    buf[a, j, k] = added(buf.at[a, j, k], self.ta2.at[0, j, k], self.ta2.at[1, j, k])
        elif stage == 2:
            buf[a, self.b_up, 0] = added(buf.at[a, self.b_up, 0], self.tb1.at[0])
            buf[a, self.b_down, 1] = added(buf.at[a, self.b_down, 1], self.tb1.at[1])
        elif stage == 3:
            for k in range(2):
                buf[a, b, k] = added(buf.at[a, b, k], self.tb2.at[0, k], self.tb2.at[1, k])
        elif stage == 4:
            self.own[...] = added(buf.at[a, b, y], self.ty)
        elif stage == 5 and self.tensor_from is not None:
            rows = pl.ds(self.tensor_from, self.own.shape[0] - self.tensor_from)
            self.tt[self.at["t"]] = self.own[rows]
            self.own[rows] = added(*(self.tt.at[n] for n in range(4)))


DP_STAGES = 11
DP_SEMS = sum(SumOverDp.counts)


def dp_scratch(rows, width, tensor_rows):
    shapes = [(2, 2, 2, rows, width), (2, 4, 2, rows, width), (2, rows, width), (2, 2, rows, width), (rows, width), (rows, width)]
    return [pltpu.VMEM(shape, jnp.bfloat16) for shape in shapes + [(4, max(tensor_rows, 16), width)]]


class SumOverTensor(Staged):
    counts = (1, 1, 2, 1)

    def __init__(self, at, buf, res, scratch, sems):
        super().__init__(*sems)
        self.buf, self.res = buf, res
        self.t0, self.t1, self.own = scratch
        self.c, self.h = at["t"] % 2, at["t"] // 2
        self.sibling = device_at(at, t=self.h * 2 + 1 - self.c)
        self.partner = device_at(at, t=(1 - self.h) * 2 + self.c)

    def copies(self, stage):
        buf, res, c, h = self.buf, self.res, self.c, self.h
        if stage == 0:
            return [(buf.at[1 - c], self.t0, self.sibling)]
        if stage == 1:
            return [(buf.at[c, 1 - h], self.t1, self.partner)]
        if stage == 2:
            return [(self.own, res.at[c, h], self.partner), (self.own, res.at[c, h], None)]
        return [(res.at[c], res.at[c], self.sibling)]

    def settle(self, stage):
        buf, c, h = self.buf, self.c, self.h
        if stage == 0:
            for n in range(2):
                buf[c, n] = added(buf.at[c, n], self.t0.at[n])
        elif stage == 1:
            self.own[...] = added(buf.at[c, h], self.t1)


TENSOR_STAGES = 4
TENSOR_SEMS = sum(SumOverTensor.counts)


def tensor_scratch(rows, width):
    return [pltpu.VMEM(shape, jnp.bfloat16) for shape in ((2, rows, width), (rows, width), (rows, width))]


def wide(tile, count=6):
    return jnp.concatenate([tile] * count, axis=1)


def mul(left, right):
    return jnp.dot(left, right, preferred_element_type=jnp.float32)


def mul_nt(left, right):
    return lax.dot_general(left, right, (((1,), (1,)), ((), ())), preferred_element_type=jnp.float32)


def mul_tn(left, right):
    return lax.dot_general(left, right, (((0,), (0,)), ((), ())), preferred_element_type=jnp.float32)


def low(value):
    return value.astype(jnp.bfloat16)


def iota(shape, dim):
    return lax.broadcasted_iota(jnp.int32, shape, dim)


def in_three(value):
    high = low(value).astype(jnp.float32)
    rest = value - high
    middle = low(rest).astype(jnp.float32)
    lane = iota(value.shape, 1)
    return low(jnp.where(lane < 16, high, jnp.where(lane < 32, middle, rest - middle)))


def exact_sum(ones, value):
    high = low(value)
    rest = value - high.astype(jnp.float32)
    middle = low(rest)
    return mul(ones, high) + mul(ones, middle) + mul(ones, low(rest - middle.astype(jnp.float32)))


def softplus(value):
    return jnp.maximum(value, 0.0) + jnp.log1p(jnp.exp(-jnp.abs(value)))


def sigmoid(value):
    return 1.0 / (1.0 + jnp.exp(-value))


def columns_of_segments(seg_ref, segc):
    segc[0:8, :] = jnp.full((8, 128), -1.0, jnp.float32)
    segc[1032:1040, :] = jnp.full((8, 128), -1.0, jnp.float32)

    def fill(k, carry):
        row = jnp.broadcast_to(seg_ref[pl.ds(k, 1), :].astype(jnp.float32), (128, 128))
        segc[pl.ds(pl.multiple_of(8 + k * 128, 8), 128), :] = row.T
        return carry

    lax.fori_loop(0, 8, fill, 0)


def kept(segc, start):
    around = segc[pl.ds(start, 144), :]
    here = around[8:, :]
    return [(pltpu.roll(around, lag, 0)[8:, :] == here).astype(jnp.float32) for lag in (1, 2, 3)]


def lagged(padded, start, keeps):
    around = padded[pl.ds(start, 136), :]
    count = around.shape[1] // 128
    return [around[8:, :]] + [pltpu.roll(around, lag, 0)[8:, :] * wide(keep[:128], count) for lag, keep in zip((1, 2, 3), keeps)]


def convolved(shifted, taps):
    total = taps[4:5, :] + taps[0:1, :] * shifted[0]
    for lag in (1, 2, 3):
        total = total + taps[lag : lag + 1, :] * shifted[lag]
    return total


def decay(k, start, segc, seg_ref, step_raw, heads):
    step = softplus(step_raw[pl.ds(start, 128), :] + heads[0:1, :])
    tri = (iota((128, 128), 0) >= iota((128, 128), 1)).astype(jnp.bfloat16)
    cum = exact_sum(tri, step * heads[1:2, :])
    seg_column = segc[pl.ds(start + 8, 128), :]
    seg_row = seg_ref[pl.ds(k, 1), :].astype(jnp.float32)
    before = segc[pl.ds(start, 8), :][7:8, :]
    last = seg_column[127:128, :]
    growth = jnp.exp(cum)
    tail = jnp.exp(cum[127:128, :] - cum) * (seg_column == last).astype(jnp.float32)
    return step, cum, seg_column, seg_row, before, last, growth, tail


def forward_kernel(
    tokens, cot, seg_ref, w_gate, w_value, w_state, w_step, w_out, taps, state_taps, heads, expand, norm_gain, gated_gain, bypass,
    normed, gate, vpad, spad, step_raw, y_out, q_out, states, sums, segc, carried,
):
    columns_of_segments(seg_ref, segc)
    vpad[0:8, :] = jnp.zeros((8, 768), jnp.float32)
    spad[0:8, :] = jnp.zeros((8, 256), jnp.float32)
    carried[...] = jnp.zeros((128, 768), jnp.float32)

    def project(k, carry):
        rows = pl.ds(pl.multiple_of(k * 256, 256), 256)
        padded = pl.ds(pl.multiple_of(8 + k * 256, 8), 256)
        hidden = tokens[rows, :].astype(jnp.float32)
        inverse = lax.rsqrt(jnp.sum(hidden * hidden, 1, keepdims=True) / 1536 + EPS)
        normal = low(hidden * inverse * norm_gain[...])
        normed[rows, :] = normal
        gate[rows, :] = mul(normal, w_gate[...])
        vpad[padded, :] = mul(normal, w_value[...])
        spad[padded, :] = mul(normal, w_state[...])
        step_raw[rows, :] = mul(normal, w_step[...])
        q_out[rows, :] = mul_nt(cot[rows, :], w_out[...])
        return carry

    lax.fori_loop(0, 4, project, 0)

    def block(k, carry):
        start = pl.multiple_of(k * 128, 128)
        rows = pl.ds(start, 128)
        keeps = kept(segc, start)
        pre = convolved(lagged(vpad, start, keeps), taps)
        x = pre * sigmoid(pre)
        pre = convolved(lagged(spad, start, keeps), state_taps)
        state = low(pre * sigmoid(pre))
        b_in, c_out = state[:, :128], state[:, 128:]
        step, cum, seg_column, seg_row, before, last, growth, tail = decay(k, start, segc, seg_ref, step_raw, heads)
        spread = mul(jnp.concatenate([in_three(step), in_three(growth), in_three(tail)], 0), expand[...])
        xs = x * spread[:128]
        start_keep = (seg_column == before).astype(jnp.float32)
        entering = carried[...]
        states[k] = low(entering)
        outside = mul(c_out, low(entering)) * (spread[128:256] * wide(start_keep))
        through = spread[255:256] * wide((last == before).astype(jnp.float32))
        carried[...] = through * entering + mul_tn(b_in, low(xs * spread[256:]))
        scores = mul_nt(c_out, b_in)
        bias = jnp.where((seg_column == seg_row) & (iota((128, 128), 0) >= iota((128, 128), 1)), 0.0, -1e30)
        cum_rows = cum.T
        first = iota((128, 128), 1) < 64
        inside = []
        for pair in range(6):
            own = xs[:, pair * 128 : (pair + 1) * 128]
            right = low(jnp.concatenate([jnp.where(first, own, 0.0), jnp.where(first, 0.0, own)], 0))
            left = [
                low(scores * jnp.exp(cum[:, h : h + 1] - cum_rows[h : h + 1, :] + bias)) for h in (2 * pair, 2 * pair + 1)
            ]
            inside.append(mul(jnp.concatenate(left, 1), right))
        y = jnp.concatenate(inside, 1) + outside + bypass[...] * x
        y_out[rows, :] = y
        raw = gate[rows, :]
        gated = y * (raw * sigmoid(raw))
        squares = jnp.sum(gated * gated, 1, keepdims=True)
        cross = jnp.sum(q_out[rows, :] * gated_gain[...] * gated, 1, keepdims=True)
        lane = iota((128, 128), 1)
        sums[k] = jnp.where(lane == 0, squares, jnp.where(lane == 1, cross, 0.0)).T[0:8, :]
        return carry

    lax.fori_loop(0, 8, block, 0)


def forward(*operands):
    f32, bf16 = jnp.float32, jnp.bfloat16
    outs = [
        ((1024, 1536), bf16),
        ((1024, 768), f32),
        ((1032, 768), f32),
        ((1032, 256), f32),
        ((1024, 128), f32),
        ((1024, 768), f32),
        ((1024, 768), f32),
        ((8, 128, 768), bf16),
        ((8, 8, 128), f32),
    ]
    return pl.pallas_call(
        forward_kernel,
        out_shape=[jax.ShapeDtypeStruct(shape, kind) for shape, kind in outs],
        in_specs=[pl.BlockSpec(memory_space=pltpu.VMEM)] * len(operands),
        out_specs=[pl.BlockSpec(memory_space=pltpu.VMEM)] * len(outs),
        scratch_shapes=[pltpu.VMEM((1040, 128), f32), pltpu.VMEM((128, 768), f32)],
        compiler_params=pltpu.CompilerParams(vmem_limit_bytes=58 * 2**20),
        name="forward",
    )(*operands)


def per_head_lanes(values):
    padded = jnp.pad(values, [(0, 0)] * (values.ndim - 1) + [(0, 4)])
    return jnp.pad(jnp.concatenate([padded] * 3, -1), [(0, 0)] * (values.ndim - 1) + [(0, 80)])


def expansion():
    row, column = iota((128, 768), 0), iota((128, 768), 1)
    return ((row < 48) & (row % 16 == column // 64)).astype(jnp.bfloat16)


def head_sums(value, expand):
    high = low(value)
    return mul_nt(high, expand) + mul_nt(low(value - high.astype(jnp.float32)), expand)


def slope(pre, sig):
    return sig * (1.0 + pre * (1.0 - sig))


def middle_block(k, total, slot, gated_gain, dy, gate_low, gate_normed, acc_v):
    rows = pl.ds(pl.multiple_of(k * 128, 128), 128)
    columns = jnp.concatenate([total] * 16, 0).T
    scale = lax.rsqrt(columns[:, 0:1] / 3072 + EPS)
    pull = columns[:, 1:2] * scale * scale * scale / 3072
    raw, y, q = slot[0], slot[1], slot[2]
    sig = sigmoid(raw)
    act = raw * sig
    gated = y * act
    scaled = gated * scale
    gate_normed[rows, :] = low(scaled * gated_gain[...])
    acc_v[5:6, :] += jnp.sum(q * scaled, 0, keepdims=True)
    grad_gated = scale * (q * gated_gain[...]) - gated * pull
    dy[rows, :] = grad_gated * act
    gate_low[rows, :] = low(grad_gated * y * slope(raw, sig))


def put(buf, i, first, count, value):
    pieces = low(value.reshape(4, 2, count, 768))
    for stream in range(2):
        buf[stream, i, :, :, first : first + count, :] = pieces[..., stream * 384 : (stream + 1) * 384]


def backward_block(
    k, vpad, spad, step_raw, seg_ref, segc, taps, state_taps, heads, expand, bypass, states, dy,
    dstate, du, dus, head_rows, value_low, state_low, step_low, acc_v, acc_s, acc_h,
):
    start = pl.multiple_of(k * 128, 128)
    rows = pl.ds(start, 128)
    keeps = kept(segc, start)
    values = lagged(vpad, start, keeps)
    pre = convolved(values, taps)
    sig = sigmoid(pre)
    x = pre * sig
    state_values = lagged(spad, start, keeps)
    state_pre = convolved(state_values, state_taps)
    state_sig = sigmoid(state_pre)
    state = low(state_pre * state_sig)
    b_in, c_out = state[:, :128], state[:, 128:]
    step, cum, seg_column, seg_row, before, last, growth, tail = decay(k, start, segc, seg_ref, step_raw, heads)
    spread = mul(jnp.concatenate([in_three(step), in_three(growth), in_three(tail)], 0), expand[...])
    step_wide, tail_wide = spread[:128], spread[256:]
    growth_wide = spread[128:256] * wide((seg_column == before).astype(jnp.float32))
    through = spread[255:256] * wide((last == before).astype(jnp.float32))
    xs = x * step_wide
    entering = states[k]
    grad_state = dstate[...]
    grad_state_low = low(grad_state)
    dyk = dy[rows, :]
    grown = low(dyk * growth_wide)
    outside = mul(c_out, entering) * growth_wide
    dxs_after = mul(b_in, grad_state_low) * tail_wide
    grad_c = mul_nt(grown, entering)
    grad_b = mul_nt(low(xs * tail_wide), grad_state_low)
    end = jnp.sum(entering.astype(jnp.float32) * grad_state, 0, keepdims=True) * through
    dstate[...] = through * grad_state + mul_tn(c_out, grown)
    scores = mul_nt(b_in, c_out)
    row, column = iota((128, 128), 0), iota((128, 128), 1)
    bias = jnp.where((seg_column == seg_row) & (row <= column), 0.0, -1e30)
    tri = (row >= column).astype(jnp.bfloat16)
    strict = row < column
    cum_rows = cum.T
    first = column < 64
    grad_scores = jnp.zeros((128, 128), jnp.float32)
    inside = []
    for pair in range(6):
        lanes = slice(pair * 128, (pair + 1) * 128)
        own = dyk[:, lanes]
        both = low(jnp.concatenate([jnp.where(first, own, 0.0), jnp.where(first, 0.0, own)], 0))
        grad_weights = mul_nt(low(xs[:, lanes]), both)
        weights, moved = [], []
        for side in range(2):
            h = 2 * pair + side
            faded = jnp.exp(cum_rows[h : h + 1, :] - cum[:, h : h + 1] + bias)
            pulled = grad_weights[:, side * 128 : (side + 1) * 128] * faded
            grad_scores = grad_scores + pulled
            moved.append(low(pulled * scores))
            weights.append(low(scores * faded))
        inside.append(mul(jnp.concatenate(weights, 1), both))
        later = mul(jnp.concatenate(moved, 0), tri)
        for side in range(2):
            h = 2 * pair + side
            part = jnp.where(strict, later[side * 128 : (side + 1) * 128], 0.0)
            head_rows[h : h + 1, :] = jnp.sum(part, 0, keepdims=True)
    grad_scores = low(grad_scores)
    grad_b = grad_b + mul(grad_scores, c_out)
    grad_c = grad_c + mul_tn(grad_scores, b_in)
    dxs = jnp.concatenate(inside, 1) + dxs_after
    dx = dxs * step_wide + bypass[...] * dyk
    summed = head_sums(jnp.concatenate([dxs * x, dyk * outside, xs * dxs_after], 0), expand[...])
    end = head_sums(jnp.broadcast_to(end, (16, 768)), expand[...])
    upper = (row <= column).astype(jnp.bfloat16)
    below = (row > column).astype(jnp.bfloat16)
    grad_decay = exact_sum(upper, summed[128:256]) + exact_sum(below, summed[256:]) + end[0:1, :] + head_rows[...].T
    grad_step = summed[:128] + heads[1:2, :] * grad_decay
    grad_raw = grad_step * sigmoid(step_raw[rows, :] + heads[0:1, :])
    step_low[rows, :] = low(jnp.where(column < 16, grad_raw, 0.0))
    acc_h[0:1, :] += jnp.sum(grad_raw, 0, keepdims=True)
    acc_h[1:2, :] += jnp.sum(step * grad_decay, 0, keepdims=True) * heads[1:2, :]
    for grad, grads, shifted, taps_ref, acc, result in (
        (dx * slope(pre, sig), du, values, taps, acc_v, value_low),
        (jnp.concatenate([grad_b, grad_c], 1) * slope(state_pre, state_sig), dus, state_values, state_taps, acc_s, state_low),
    ):
        grads[128:136, :] = grads[0:8, :]
        grads[0:128, :] = grad
        for lag in range(4):
            acc[lag : lag + 1, :] += jnp.sum(grad * shifted[lag], 0, keepdims=True)
        acc[4:5, :] += jnp.sum(grad, 0, keepdims=True)
        around = grads[...]
        count = around.shape[1] // 128
        total = grad * taps_ref[0:1, :]
        for lag, keep in zip((1, 2, 3), keeps):
            total = total + taps_ref[lag : lag + 1, :] * pltpu.roll(around * wide(keep, count), 136 - lag, 0)[:128, :]
        result[rows, :] = low(total)
    acc_v[6:7, :] += jnp.sum(dyk * x, 0, keepdims=True)


def put_small(small, acc_v, acc_s, acc_h, acc_n, step_grad):
    def block(j):
        return (j // 8, (j // 2) % 4, j % 2)

    small[...] = jnp.zeros_like(small)
    pad = jnp.zeros((8, 128), jnp.float32)
    for j in range(12):
        small[block(j) + (slice(0, 16), slice(None))] = low(step_grad[:, j * 128 : (j + 1) * 128])
    for j in range(6):
        small[block(12 + j) + (slice(0, 16), slice(None))] = low(jnp.concatenate([acc_v[:, j * 128 : (j + 1) * 128], pad], 0))
    small[block(18) + (slice(0, 16), slice(None))] = low(jnp.concatenate([acc_h[...], pad], 0))
    for j in range(2):
        small[block(j) + (slice(16, 32), slice(None))] = low(jnp.concatenate([acc_s[:, j * 128 : (j + 1) * 128], pad], 0))
    gains = [acc_n[0:1, j * 128 : (j + 1) * 128] for j in range(12)] + [jnp.zeros((4, 128), jnp.float32)]
    small[block(2) + (slice(16, 32), slice(None))] = low(jnp.concatenate(gains, 0))


class Loads:
    def __init__(self, sems):
        self.sems, self.used = sems, 0

    def make(self, src, dst):
        self.used += 1
        return pltpu.make_async_copy(src, dst, self.sems.at[self.used - 1])


def stream_copies(k, slot, sources, slots, sems):
    rows = pl.ds(pl.multiple_of(k * 128, 128), 128)
    return [pltpu.make_async_copy(src.at[rows], slots.at[slot, n], sems.at[slot, n]) for n, src in enumerate(sources)]


def backward_kernel(
    tokens, cot_in, normed_in, seg_ref, w_gate_in, w_value_in, w_state_in, w_step_in, w_out_in, taps, state_taps, heads, expand, gated_gain, bypass,
    gate, vpad, spad, step_raw, y_in, q_in, states, sums,
    big, small, branch, dx_part,
    segc, dy, gate_low, gate_normed, value_low, state_low, step_low, du, dus, dstate, head_rows, acc_v, acc_s, acc_h, acc_n,
    normed, cot, w_gate, w_value, w_state, w_step, w_out, slots, token_rows, slot_sems, sems,
):
    loads = Loads(sems)
    early_loads = [loads.make(*pair) for pair in ((normed_in, normed), (cot_in, cot), (w_out_in, w_out))]
    late_loads = [
        loads.make(*pair)
        for pair in ((w_gate_in, w_gate), (w_value_in, w_value), (w_state_in, w_state), (w_step_in, w_step))
    ]
    streamed = (gate, y_in, q_in)
    for cp in stream_copies(0, 0, streamed, slots, slot_sems) + early_loads + late_loads:
        cp.start()
    columns_of_segments(seg_ref, segc)
    for ref in (du, dus, dstate, head_rows, acc_v, acc_s, acc_h, acc_n):
        ref[...] = jnp.zeros_like(ref)

    def middle(k, carry):
        slot = k % 2

        @pl.when(k < 7)
        def _():
            for cp in stream_copies(k + 1, 1 - slot, streamed, slots, slot_sems):
                cp.start()

        for cp in stream_copies(k, slot, streamed, slots, slot_sems):
            cp.wait()
        middle_block(k, sums[k], slots.at[slot], gated_gain, dy, gate_low, gate_normed, acc_v)
        return carry

    lax.fori_loop(0, 8, middle, 0)
    for cp in early_loads:
        cp.wait()

    def early(i, carry):
        wide_columns = pl.ds(pl.multiple_of(i * 384, 128), 384)
        out_rows = pl.ds(pl.multiple_of((i % 2) * 384, 128), 384)
        out_columns = pl.ds(pl.multiple_of((i // 2) * 768, 128), 768)
        put(big, i, 0, 48, mul_tn(normed[:, wide_columns], gate_low[...]))
        put(big, i, 96, 48, mul_tn(gate_normed[:, out_rows], cot[:, out_columns]))
        rows = pl.ds(pl.multiple_of(i * 256, 256), 256)
        branch[rows, :] = low(mul(gate_normed[rows, :], w_out[...]))
        return carry

    lax.fori_loop(0, 4, early, 0)

    def scan(i, carry):
        backward_block(
            7 - i, vpad, spad, step_raw, seg_ref, segc, taps, state_taps, heads, expand, bypass, states, dy,
            dstate, du, dus, head_rows, value_low, state_low, step_low, acc_v, acc_s, acc_h,
        )
        return carry

    lax.fori_loop(0, 8, scan, 0)
    for cp in late_loads:
        cp.wait()

    def late(i, carry):
        rows = pl.ds(pl.multiple_of(i * 256, 256), 256)
        fetch = pltpu.make_async_copy(tokens.at[rows], token_rows, sems.at[7])
        fetch.start()
        wide_columns = pl.ds(pl.multiple_of(i * 384, 128), 384)
        put(big, i, 48, 48, mul_tn(normed[:, wide_columns], value_low[...]))
        thirds = [
            mul_tn(normed[:, pl.ds(pl.multiple_of(q * 512 + i * 128, 128), 128)], state_low[...]) for q in range(3)
        ]
        put(big, i, 144, 16, jnp.concatenate(thirds, 1))
        part = mul_nt(gate_low[rows, :], w_gate[...]) + mul_nt(value_low[rows, :], w_value[...])
        part = part + mul_nt(state_low[rows, :], w_state[...]) + mul_nt(step_low[rows, :], w_step[...])
        dx_part[rows, :] = low(part)
        fetch.wait()
        hidden = token_rows[...].astype(jnp.float32)
        inverse = lax.rsqrt(jnp.sum(hidden * hidden, 1, keepdims=True) / 1536 + EPS)
        acc_n[0:1, :] += jnp.sum(part * (hidden * inverse), 0, keepdims=True)
        return carry

    lax.fori_loop(0, 4, late, 0)
    step_grad = mul_tn(step_low[...], normed[...])[0:16, :]
    put_small(small, acc_v, acc_s, acc_h, acc_n, step_grad)


def backward(*operands):
    f32, bf16 = jnp.float32, jnp.bfloat16
    outs = [((2, 4, 4, 2, 160, 384), bf16), ((4, 4, 2, 32, 128), bf16), ((1024, 1536), bf16), ((1024, 1536), bf16)]
    scratch = [
        ((1040, 128), f32), ((1024, 768), f32), ((1024, 768), bf16), ((1024, 768), bf16), ((1024, 768), bf16),
        ((1024, 256), bf16), ((1024, 128), bf16), ((136, 768), f32), ((136, 256), f32), ((128, 768), f32),
        ((128, 128), f32), ((8, 768), f32), ((8, 256), f32), ((8, 128), f32), ((8, 1536), f32),
        ((1024, 1536), bf16), ((1024, 1536), bf16), ((1536, 768), bf16), ((1536, 768), bf16), ((1536, 256), bf16),
        ((1536, 128), bf16), ((768, 1536), bf16), ((2, 3, 128, 768), f32), ((256, 1536), bf16),
    ]
    vmem, hbm = pl.BlockSpec(memory_space=pltpu.VMEM), pl.BlockSpec(memory_space=pl.ANY)
    in_hbm = (0, 1, 2, 4, 5, 6, 7, 8, 15, 19, 20)
    return pl.pallas_call(
        backward_kernel,
        out_shape=[jax.ShapeDtypeStruct(shape, kind) for shape, kind in outs],
        in_specs=[hbm if n in in_hbm else vmem for n in range(len(operands))],
        out_specs=[vmem] * len(outs),
        scratch_shapes=[pltpu.VMEM(shape, kind) for shape, kind in scratch]
        + [pltpu.SemaphoreType.DMA((2, 3)), pltpu.SemaphoreType.DMA((8,))],
        compiler_params=pltpu.CompilerParams(vmem_limit_bytes=62 * 2**20),
        name="backward",
    )(*operands)


def exchange_kernel(sums, total, landed, send, recv):
    at = place()
    greet(tensor_peers(at))
    copies = [
        pltpu.make_async_remote_copy(
            src_ref=sums,
            dst_ref=landed.at[at["t"]],
            send_sem=send.at[n],
            recv_sem=recv.at[n],
            device_id=peer,
            device_id_type=MESH_ID,
        )
        for n, peer in enumerate(tensor_peers(at))
    ]
    for cp in copies:
        cp.start()
    landed[at["t"]] = sums[...]
    for cp in copies:
        cp.wait()
    total[...] = (landed[0] + landed[1]) + (landed[2] + landed[3])


def summed_over_tensor(sums):
    vmem = pl.BlockSpec(memory_space=pltpu.VMEM)
    return pl.pallas_call(
        exchange_kernel,
        out_shape=jax.ShapeDtypeStruct(sums.shape, sums.dtype),
        in_specs=[vmem],
        out_specs=vmem,
        scratch_shapes=[
            pltpu.VMEM((4,) + sums.shape, sums.dtype),
            pltpu.SemaphoreType.DMA((3,)),
            pltpu.SemaphoreType.DMA((3,)),
        ],
        compiler_params=pltpu.CompilerParams(collective_id=1, has_side_effects=True),
        name="exchange",
    )(sums)


def sum_kernel(big_in, small_in, branch_in, dx_in, big_out, small_out, branch_out, dx_out, big, small, branch, dx, *rest):
    dp0, dp1, dps, tb, td = rest[0:7], rest[7:14], rest[14:21], rest[21:24], rest[24:27]
    send, recv, local = rest[27:]
    at = place()
    loads = [
        pltpu.make_async_copy(src, dst, local.at[n])
        for n, (src, dst) in enumerate(((big_in, big), (small_in, small), (branch_in, branch), (dx_in, dx)))
    ]
    for cp in loads:
        cp.start()
    greet(dp_peers(at) + tensor_peers(at))
    for cp in loads:
        cp.wait()
    kept_rows = big.shape[4] - 16
    dp_sums = [
        SumOverDp(at, ("x", "z"), big.at[0], big_out.at[0], dp0, (send, recv, 0), kept_rows),
        SumOverDp(at, ("z", "x"), big.at[1], big_out.at[1], dp1, (send, recv, DP_SEMS), kept_rows),
        SumOverDp(at, ("x", "z"), small, small_out, dps, (send, recv, 2 * DP_SEMS), 16),
    ]
    tensor_sums = [
        SumOverTensor(at, branch, branch_out, tb, (send, recv, 3 * DP_SEMS)),
        SumOverTensor(at, dx, dx_out, td, (send, recv, 3 * DP_SEMS + TENSOR_SEMS)),
    ]
    pending = [(tensor_sums[0], n) for n in range(TENSOR_STAGES)] + [(tensor_sums[1], n) for n in range(TENSOR_STAGES)]
    for stage in range(DP_STAGES):
        for engine in dp_sums:
            engine.start(stage)
        if stage < len(pending):
            pending[stage][0].start(pending[stage][1])
        for engine in dp_sums:
            engine.finish(stage)
        if stage < len(pending):
            pending[stage][0].finish(pending[stage][1])


def summed(big, small, branch, dx):
    operands = (big, small, branch, dx)
    rows = big.shape[4]
    hbm = pl.BlockSpec(memory_space=pl.ANY)
    count = 3 * DP_SEMS + 2 * TENSOR_SEMS
    return pl.pallas_call(
        sum_kernel,
        out_shape=[jax.ShapeDtypeStruct(operand.shape, operand.dtype) for operand in operands],
        in_specs=[hbm] * 4,
        out_specs=[hbm] * 4,
        scratch_shapes=[pltpu.VMEM(operand.shape, operand.dtype) for operand in operands]
        + dp_scratch(rows, 384, 16)
        + dp_scratch(rows, 384, 16)
        + dp_scratch(32, 128, 16)
        + tensor_scratch(256, 1536)
        + tensor_scratch(256, 1536)
        + [pltpu.SemaphoreType.DMA((count,)), pltpu.SemaphoreType.DMA((count,)), pltpu.SemaphoreType.DMA((4,))],
        compiler_params=pltpu.CompilerParams(collective_id=0, has_side_effects=True, vmem_limit_bytes=56 * 2**20),
        name="sums",
    )(*operands)


def finish_kernel(tokens, cot, norm_gain, big, branch, dx, mixed, grad_tokens, gate, value, out, state):
    hidden = tokens[...].astype(jnp.float32)
    inverse = lax.rsqrt(jnp.sum(hidden * hidden, 1, keepdims=True) / 1536 + EPS)
    mixed[...] = low(hidden + branch[...].astype(jnp.float32))
    scaled = dx[...].astype(jnp.float32) * norm_gain[...]
    along = jnp.sum(scaled * hidden, 1, keepdims=True) * (inverse * inverse * inverse / 1536)
    grad_tokens[...] = cot[...].astype(jnp.float32) + inverse * scaled - hidden * along
    for stream in range(2):
        columns = slice(stream * 384, (stream + 1) * 384)
        for j in range(2):
            for y in range(2):
                part = big[stream, 0, j, y].astype(jnp.float32)
                rows = slice((j * 2 + y) * 48, (j * 2 + y + 1) * 48)
                gate[rows, columns] = part[0:48]
                value[rows, columns] = part[48:96]
                out[rows, columns] = part[96:144]
    for j in range(2):
        for y in range(2):
            rows = slice((j * 2 + y) * 16, (j * 2 + y + 1) * 16)
            left = big[0, 0, j, y, 144:160].astype(jnp.float32)
            right = big[1, 0, j, y, 144:160].astype(jnp.float32)
            state[0, rows, :] = left[:, 0:256]
            state[1, rows, 0:128] = left[:, 256:384]
            state[1, rows, 128:256] = right[:, 0:128]
            state[2, rows, :] = right[:, 128:384]


def finished(tokens, cot, norm_gain, big, branch, dx):
    f32 = jnp.float32
    by_rows = pl.BlockSpec((128, 1536), lambda g: (g, 0))
    weight = pl.BlockSpec((192, 768), lambda g: (g, 0))
    return pl.pallas_call(
        finish_kernel,
        grid=(8,),
        out_shape=[
            jax.ShapeDtypeStruct((1024, 1536), jnp.bfloat16),
            jax.ShapeDtypeStruct((1024, 1536), f32),
            jax.ShapeDtypeStruct((1536, 768), f32),
            jax.ShapeDtypeStruct((1536, 768), f32),
            jax.ShapeDtypeStruct((768, 1536), f32),
            jax.ShapeDtypeStruct((3, 512, 256), f32),
        ],
        in_specs=[
            by_rows,
            by_rows,
            pl.BlockSpec((1, 1536), lambda g: (0, 0)),
            pl.BlockSpec((2, 1, 2, 2, 160, 384), lambda g: (0, g // 2, g % 2, 0, 0, 0)),
            by_rows,
            by_rows,
        ],
        out_specs=[
            by_rows,
            by_rows,
            weight,
            weight,
            pl.BlockSpec((192, 768), lambda g: ((g // 2) % 2 * 2 + g % 2, g // 4)),
            pl.BlockSpec((3, 64, 256), lambda g: (0, g, 0)),
        ],
        compiler_params=pltpu.CompilerParams(vmem_limit_bytes=40 * 2**20),
        name="finish",
    )(tokens, cot, norm_gain, big, branch, dx)


def local(
    tokens,
    segment,
    gate_proj,
    value_proj,
    state_proj,
    step_proj,
    value_conv,
    value_conv_bias,
    state_conv,
    state_conv_bias,
    step_bias,
    log_rate,
    bypass_gain,
    norm_gain,
    gated_norm_gain,
    out_proj,
    cotangent,
):
    taps = jnp.concatenate([value_conv, value_conv_bias[None], jnp.zeros((3, 768), jnp.float32)], 0)
    state_taps = jnp.concatenate([state_conv, state_conv_bias[None], jnp.zeros((3, 256), jnp.float32)], 0)
    heads = jnp.pad(per_head_lanes(jnp.stack([step_bias, -jnp.exp(log_rate)])), ((0, 6), (0, 0)))
    segments = segment.reshape(8, 128)
    step_wide = per_head_lanes(step_proj)
    expand = expansion()
    gated_gain = gated_norm_gain[None]
    bypass = jnp.repeat(bypass_gain, 64)[None]
    normed, gate, vpad, spad, step_raw, y, q, states, sums = forward(
        tokens, cotangent, segments, gate_proj, value_proj, state_proj, step_wide, out_proj,
        taps, state_taps, heads, expand, norm_gain[None], gated_gain, bypass,
    )
    sums = summed_over_tensor(sums)
    big, small, branch, dx = backward(
        tokens, cotangent, normed, segments, gate_proj, value_proj, state_proj, step_wide, out_proj,
        taps, state_taps, heads, expand, gated_gain, bypass, gate, vpad, spad, step_raw, y, q, states, sums,
    )
    quarters = (2, 2, 256, 1536)
    big, small, branch, dx = summed(big, small, branch.reshape(quarters), dx.reshape(quarters))
    mixed_out, grad_tokens, grad_gate, grad_value, grad_out, grad_state = finished(
        tokens, cotangent, norm_gain[None], big, branch.reshape(1024, 1536), dx.reshape(1024, 1536)
    )
    small = small.reshape(32, 32, 128).astype(jnp.float32)
    grad_step = jnp.concatenate([small[j, 0:12] for j in range(12)], 1).T
    channels = jnp.concatenate([small[12 + j, 0:8] for j in range(6)], 1)
    states_small = jnp.concatenate([small[j, 16:24] for j in range(2)], 1)
    return (
        mixed_out,
        grad_tokens,
        grad_gate,
        grad_value,
        grad_state.reshape(1536, 256),
        grad_step,
        channels[0:4],
        channels[4],
        states_small[0:4],
        states_small[4],
        small[18, 0, 0:12],
        small[18, 1, 0:12],
        channels[6].reshape(12, 64).sum(1),
        small[2, 16:28].reshape(1536),
        channels[5],
        grad_out,
    )


def solution(mesh):
    placed = (
        P("dp", None),
        P("dp", None),
        P(None, "tensor"),
        P(None, "tensor"),
        P(),
        P(None, "tensor"),
        P(None, "tensor"),
        P("tensor"),
        P(),
        P(),
        P("tensor"),
        P("tensor"),
        P("tensor"),
        P(),
        P("tensor"),
        P("tensor", None),
        P("dp", None),
    )
    return jax.shard_map(
        local,
        mesh=mesh,
        in_specs=placed,
        out_specs=(
            P("dp", None),
            P("dp", None),
            P(None, "tensor"),
            P(None, "tensor"),
            P(),
            P(None, "tensor"),
            P(None, "tensor"),
            P("tensor"),
            P(),
            P(),
            P("tensor"),
            P("tensor"),
            P("tensor"),
            P(),
            P("tensor"),
            P("tensor", None),
        ),
        check_vma=False,
    )
```

```python
import functools

import jax
import jax.numpy as jnp
from jax import lax
from jax.experimental import pallas as pl
from jax.experimental.pallas import tpu as pltpu
from jax.sharding import PartitionSpec as P

EPS = 1e-05
MESH_ID = pl.DeviceIdType.MESH


def place():
    dp = lax.axis_index("dp")
    tensor = lax.axis_index("tensor")
    return {"x": dp // 8, "y": (dp // 4) % 2, "z": dp % 4, "t": tensor}


def device_at(at, **moved):
    spot = dict(at, **moved)
    return (spot["x"] * 8 + spot["y"] * 4 + spot["z"], spot["t"])


def dp_peers(at):
    return [
        device_at(at, x=(at["x"] + 1) % 4),
        device_at(at, x=(at["x"] + 3) % 4),
        device_at(at, z=(at["z"] + 1) % 4),
        device_at(at, z=(at["z"] + 3) % 4),
        device_at(at, y=1 - at["y"]),
    ]


def tensor_peers(at):
    return [device_at(at, t=(at["t"] + step) % 4) for step in (1, 2, 3)]


def greet(peers):
    barrier = pltpu.get_barrier_semaphore()
    for peer in peers:
        pl.semaphore_signal(barrier, inc=1, device_id=peer, device_id_type=MESH_ID)
    pl.semaphore_wait(barrier, len(peers))


def added(*refs):
    total = refs[0][...].astype(jnp.float32)
    for ref in refs[1:]:
        total = total + ref[...].astype(jnp.float32)
    return total.astype(jnp.bfloat16)


class Staged:
    def __init__(self, send, recv, first):
        self.send, self.recv, self.first = send, recv, first

    def made(self, stage):
        at = self.first + sum(self.counts[:stage])
        for n, (src, dst, peer) in enumerate(self.copies(stage)):
            if peer is None:
                yield pltpu.make_async_copy(src, dst, self.recv.at[at + n])
            else:
                yield pltpu.make_async_remote_copy(
                    src_ref=src,
                    dst_ref=dst,
                    send_sem=self.send.at[at + n],
                    recv_sem=self.recv.at[at + n],
                    device_id=peer,
                    device_id_type=MESH_ID,
                )

    def start(self, stage):
        for cp in self.made(stage):
            cp.start()

    def finish(self, stage):
        for cp in self.made(stage):
            cp.wait()
        self.settle(stage)


class SumOverDp(Staged):
    counts = (2, 2, 3, 1, 3, 4, 2, 2)

    def __init__(self, at, order, buf, res, scratch, sems, across=None):
        super().__init__(*sems)
        self.at, self.buf, self.res, self.across = at, buf, res, across
        self.ta1, self.ta2, self.tb, self.ty, self.own, self.tt = scratch
        a_axis, b_axis = order
        self.a, self.b = at[a_axis], at[b_axis]
        self.a_up, self.a_down, self.a_far = [(self.a + n) % 4 for n in (1, 3, 2)]
        self.a_right, self.a_left = [device_at(at, **{a_axis: n}) for n in (self.a_up, self.a_down)]
        self.b_others = [(self.b + n) % 4 for n in (1, 2, 3)]
        self.b_peers = [device_at(at, **{b_axis: n}) for n in self.b_others]
        self.other = device_at(at, y=1 - at["y"])

    def copies(self, stage):
        buf, res, a, b, own = self.buf, self.res, self.a, self.b, self.own
        near, far = pl.ds(0, 2), pl.ds(2, 2)
        if stage == 0:
            return [(buf.at[self.a_far, near], self.ta1.at[0], self.a_right), (buf.at[self.a_far, far], self.ta1.at[1], self.a_left)]
        if stage == 1:
            return [(buf.at[self.a_up], self.ta2.at[0], self.a_right), (buf.at[self.a_down], self.ta2.at[1], self.a_left)]
        if stage == 2:
            return [(buf.at[a, j], self.tb.at[n], peer) for n, (j, peer) in enumerate(zip(self.b_others, self.b_peers))]
        if stage == 3:
            return [(buf.at[a, b], self.ty, self.other)]
        if stage == 4:
            return [(own.at[self.across], self.tt.at[self.at["t"]], peer) for peer in tensor_peers(self.at)]
        if stage == 5:
            return [(own, res.at[a, b], peer) for peer in self.b_peers] + [(own, res.at[a, b], None)]
        if stage == 6:
            return [(res.at[a], res.at[a], self.a_right), (res.at[a], res.at[a], self.a_left)]
        return [
            (res.at[self.a_down, near], res.at[self.a_down, near], self.a_right),
            (res.at[self.a_up, far], res.at[self.a_up, far], self.a_left),
        ]

    def settle(self, stage):
        buf, a, b, own = self.buf, self.a, self.b, self.own
        if stage == 0:
            for j in range(2):
                buf[self.a_up, j] = added(buf.at[self.a_up, j], self.ta1.at[0, j])
                buf[self.a_down, 2 + j] = added(buf.at[self.a_down, 2 + j], self.ta1.at[1, j])
        elif stage == 1:
            for j in range(4):
                buf[a, j] = added(buf.at[a, j], self.ta2.at[0, j], self.ta2.at[1, j])
        elif stage == 2:
            buf[a, b] = added(buf.at[a, b], *(self.tb.at[n] for n in range(3)))
        elif stage == 3:
            own[...] = added(buf.at[a, b], self.ty)
        elif stage == 4:
            self.tt[self.at["t"]] = own[self.across]
            own[self.across] = added(*(self.tt.at[n] for n in range(4)))


DP_SEMS = sum(SumOverDp.counts)


def dp_scratch(rows, width, across=16):
    shapes = [(2, 2, rows, width), (2, 4, rows, width), (3, rows, width), (rows, width), (rows, width), (4, across, width)]
    return [pltpu.VMEM(shape, jnp.bfloat16) for shape in shapes]


class SumOverTensor(Staged):
    counts = (1, 1, 2, 1)

    def __init__(self, at, columns, buf, res, scratch, sems):
        super().__init__(*sems)
        self.buf, self.res, self.columns = buf, res, columns
        self.t0, self.t1 = scratch
        self.c, self.h = at["t"] % 2, at["t"] // 2
        self.sibling = device_at(at, t=self.h * 2 + 1 - self.c)
        self.partner = device_at(at, t=(1 - self.h) * 2 + self.c)

    def copies(self, stage):
        buf, res, c, h, columns = self.buf, self.res, self.c, self.h, self.columns
        if stage == 0:
            return [(buf.at[1 - c, :, :, columns], self.t0.at[:, :, columns], self.sibling)]
        if stage == 1:
            return [(buf.at[c, 1 - h, :, columns], self.t1.at[:, columns], self.partner)]
        if stage == 2:
            mine, theirs = buf.at[c, h, :, columns], res.at[c, h, :, columns]
            return [(mine, theirs, self.partner), (mine, theirs, None)]
        return [(res.at[c, :, :, columns], res.at[c, :, :, columns], self.sibling)]

    def settle(self, stage):
        buf, c, h, columns = self.buf, self.c, self.h, self.columns
        if stage == 0:
            for n in range(2):
                buf[c, n, :, columns] = added(buf.at[c, n, :, columns], self.t0.at[n, :, columns])
        elif stage == 1:
            buf[c, h, :, columns] = added(buf.at[c, h, :, columns], self.t1.at[:, columns])


TENSOR_SEMS = sum(SumOverTensor.counts)


def wide(tile, count=6):
    return jnp.concatenate([tile] * count, axis=1)


def mul(left, right):
    return jnp.dot(left, right, preferred_element_type=jnp.float32)


def mul_nt(left, right):
    return lax.dot_general(left, right, (((1,), (1,)), ((), ())), preferred_element_type=jnp.float32)


def mul_tn(left, right):
    return lax.dot_general(left, right, (((0,), (0,)), ((), ())), preferred_element_type=jnp.float32)


def low(value):
    return value.astype(jnp.bfloat16)


def iota(shape, dim):
    return lax.broadcasted_iota(jnp.int32, shape, dim)


def in_three(value):
    high = low(value).astype(jnp.float32)
    rest = value - high
    middle = low(rest).astype(jnp.float32)
    lane = iota(value.shape, 1)
    return low(jnp.where(lane < 16, high, jnp.where(lane < 32, middle, rest - middle)))


def exact_sum(ones, value):
    high = low(value)
    rest = value - high.astype(jnp.float32)
    middle = low(rest)
    return mul(ones, high) + mul(ones, middle) + mul(ones, low(rest - middle.astype(jnp.float32)))


def softplus(value):
    return jnp.maximum(value, 0.0) + jnp.log1p(jnp.exp(-jnp.abs(value)))


def sigmoid(value):
    return 1.0 / (1.0 + jnp.exp(-value))


def columns_of_segments(seg_ref, segc):
    segc[0:8, :] = jnp.full((8, 128), -1.0, jnp.float32)
    segc[1032:1040, :] = jnp.full((8, 128), -1.0, jnp.float32)

    def fill(k, carry):
        row = jnp.broadcast_to(seg_ref[:, pl.ds(pl.multiple_of(k * 128, 128), 128)].astype(jnp.float32), (128, 128))
        segc[pl.ds(pl.multiple_of(8 + k * 128, 8), 128), :] = row.T
        return carry

    lax.fori_loop(0, 8, fill, 0)


def kept(segc, start):
    around = segc[pl.ds(start, 144), :]
    here = around[8:, :]
    return [(pltpu.roll(around, lag, 0)[8:, :] == here).astype(jnp.float32) for lag in (1, 2, 3)]


def lagged(padded, start, keeps):
    around = padded[pl.ds(start, 136), :]
    count = around.shape[1] // 128
    return [around[8:, :]] + [pltpu.roll(around, lag, 0)[8:, :] * wide(keep[:128], count) for lag, keep in zip((1, 2, 3), keeps)]


def convolved(shifted, taps):
    total = taps[4:5, :] + taps[0:1, :] * shifted[0]
    for lag in (1, 2, 3):
        total = total + taps[lag : lag + 1, :] * shifted[lag]
    return total


def decay(k, start, segc, seg_ref, step_raw, heads):
    rows = pl.ds(start, 128)
    step = softplus(step_raw[rows, :] + heads[0:1, :])
    tri = (iota((128, 128), 0) >= iota((128, 128), 1)).astype(jnp.bfloat16)
    cum = exact_sum(tri, step * heads[1:2, :])
    seg_column = segc[pl.ds(start + 8, 128), :]
    seg_row = seg_ref[:, rows].astype(jnp.float32)
    before = segc[pl.ds(start, 8), :][7:8, :]
    last = seg_column[127:128, :]
    growth = jnp.exp(cum)
    tail = jnp.exp(cum[127:128, :] - cum) * (seg_column == last).astype(jnp.float32)
    return step, cum, seg_column, seg_row, before, last, growth, tail


def expansion():
    row, column = iota((128, 768), 0), iota((128, 768), 1)
    return ((row < 48) & (row % 16 == column // 64)).astype(jnp.bfloat16)


def head_sums(value, expand):
    high = low(value)
    return mul_nt(high, expand) + mul_nt(low(value - high.astype(jnp.float32)), expand)


def slope(pre, sig):
    return sig * (1.0 + pre * (1.0 - sig))


def middle_block(k, total, gated_gain, gate, y_ref, q_ref, acc_v):
    rows = pl.ds(pl.multiple_of(k * 128, 128), 128)
    columns = jnp.concatenate([total] * 16, 0).T
    scale = lax.rsqrt(columns[:, 0:1] / 3072 + EPS)
    pull = columns[:, 1:2] * scale * scale * scale / 3072
    raw, y, q = [ref[rows, :].astype(jnp.float32) for ref in (gate, y_ref, q_ref)]
    sig = sigmoid(raw)
    act = raw * sig
    gated = y * act
    scaled = gated * scale
    y_ref[rows, :] = low(scaled * gated_gain)
    acc_v[5:6, :] += jnp.sum(q * scaled, 0, keepdims=True)
    grad_gated = scale * (q * gated_gain) - gated * pull
    q_ref[rows, :] = low(grad_gated * act)
    gate[rows, :] = low(grad_gated * y * slope(raw, sig))


def put(buf, i, value):
    pieces = low(value.reshape(4, buf.shape[3], 768))
    for stream in range(2):
        buf[stream, i] = pieces[..., stream * 384 : (stream + 1) * 384]


def backward_block(
    k, vpad, spad, step_raw, seg_ref, segc, taps, state_taps, heads, expand, bypass, states, dy,
    dstate, du, dus, head_rows, value_low, state_low, step_low, acc_v, acc_s, acc_h, between,
):
    start = pl.multiple_of(k * 128, 128)
    rows = pl.ds(start, 128)
    keeps = kept(segc, start)
    values = lagged(vpad, start, keeps)
    pre = convolved(values, taps)
    sig = sigmoid(pre)
    x = pre * sig
    state_values = lagged(spad, start, keeps)
    state_pre = convolved(state_values, state_taps)
    state_sig = sigmoid(state_pre)
    state = low(state_pre * state_sig)
    b_in, c_out = state[:, :128], state[:, 128:]
    step, cum, seg_column, seg_row, before, last, growth, tail = decay(k, start, segc, seg_ref, step_raw, heads)
    spread = mul(jnp.concatenate([in_three(step), in_three(growth), in_three(tail)], 0), expand[...])
    step_wide, tail_wide = spread[:128], spread[256:]
    growth_wide = spread[128:256] * wide((seg_column == before).astype(jnp.float32))
    through = spread[255:256] * wide((last == before).astype(jnp.float32))
    xs = x * step_wide
    entering = states[k]
    grad_state = dstate[...]
    grad_state_low = low(grad_state)
    dyk = dy[rows, :].astype(jnp.float32)
    grown = low(dyk * growth_wide)
    outside = mul(c_out, entering) * growth_wide
    dxs_after = mul(b_in, grad_state_low) * tail_wide
    grad_c = mul_nt(grown, entering)
    grad_b = mul_nt(low(xs * tail_wide), grad_state_low)
    end = jnp.sum(entering.astype(jnp.float32) * grad_state, 0, keepdims=True) * through
    dstate[...] = through * grad_state + mul_tn(c_out, grown)
    scores = mul_nt(b_in, c_out)
    row, column = iota((128, 128), 0), iota((128, 128), 1)
    bias = jnp.where((seg_column == seg_row) & (row <= column), 0.0, -1e30)
    tri = (row >= column).astype(jnp.bfloat16)
    strict = row < column
    cum_rows = cum.T
    first = column < 64
    grad_scores = jnp.zeros((128, 128), jnp.float32)
    inside = []
    for pair in range(6):
        if pair == 3:
            between()
        lanes = slice(pair * 128, (pair + 1) * 128)
        own = dyk[:, lanes]
        both = low(jnp.concatenate([jnp.where(first, own, 0.0), jnp.where(first, 0.0, own)], 0))
        grad_weights = mul_nt(low(xs[:, lanes]), both)
        weights, moved = [], []
        for side in range(2):
            h = 2 * pair + side
            faded = jnp.exp(cum_rows[h : h + 1, :] - cum[:, h : h + 1] + bias)
            pulled = grad_weights[:, side * 128 : (side + 1) * 128] * faded
            grad_scores = grad_scores + pulled
            moved.append(low(pulled * scores))
            weights.append(low(scores * faded))
        inside.append(mul(jnp.concatenate(weights, 1), both))
        later = mul(jnp.concatenate(moved, 0), tri)
        for side in range(2):
            h = 2 * pair + side
            part = jnp.where(strict, later[side * 128 : (side + 1) * 128], 0.0)
            head_rows[h : h + 1, :] = jnp.sum(part, 0, keepdims=True)
    grad_scores = low(grad_scores)
    grad_b = grad_b + mul(grad_scores, c_out)
    grad_c = grad_c + mul_tn(grad_scores, b_in)
    dxs = jnp.concatenate(inside, 1) + dxs_after
    dx = dxs * step_wide + bypass * dyk
    summed = head_sums(jnp.concatenate([dxs * x, dyk * outside, xs * dxs_after], 0), expand[...])
    end = head_sums(jnp.broadcast_to(end, (16, 768)), expand[...])
    upper = (row <= column).astype(jnp.bfloat16)
    below = (row > column).astype(jnp.bfloat16)
    grad_decay = exact_sum(upper, summed[128:256]) + exact_sum(below, summed[256:]) + end[0:1, :] + head_rows[...].T
    grad_step = summed[:128] + heads[1:2, :] * grad_decay
    grad_raw = grad_step * sigmoid(step_raw[rows, :] + heads[0:1, :])
    step_low[rows, :] = low(jnp.where(column < 16, grad_raw, 0.0))
    acc_h[0:1, :] += jnp.sum(grad_raw, 0, keepdims=True)
    acc_h[1:2, :] += jnp.sum(step * grad_decay, 0, keepdims=True) * heads[1:2, :]
    for grad, grads, shifted, taps_ref, acc, result in (
        (dx * slope(pre, sig), du, values, taps, acc_v, value_low),
        (jnp.concatenate([grad_b, grad_c], 1) * slope(state_pre, state_sig), dus, state_values, state_taps, acc_s, state_low),
    ):
        grads[128:136, :] = grads[0:8, :]
        grads[0:128, :] = grad
        for lag in range(4):
            acc[lag : lag + 1, :] += jnp.sum(grad * shifted[lag], 0, keepdims=True)
        acc[4:5, :] += jnp.sum(grad, 0, keepdims=True)
        around = grads[...]
        count = around.shape[1] // 128
        total = grad * taps_ref[0:1, :]
        for lag, keep in zip((1, 2, 3), keeps):
            total = total + taps_ref[lag : lag + 1, :] * pltpu.roll(around * wide(keep, count), 136 - lag, 0)[:128, :]
        result[rows, :] = low(total)
    acc_v[6:7, :] += jnp.sum(dyk * x, 0, keepdims=True)


def small_block(j, across):
    first = 32 * across + 16 * (j % 2)
    return (j // 8, (j // 2) % 4, slice(first, first + 16))


def put_small(small, acc_v, acc_s, acc_h, acc_n, step_grad):
    small[...] = jnp.zeros_like(small)
    pad = jnp.zeros((8, 128), jnp.float32)
    for j in range(12):
        small[small_block(j, 0)] = low(step_grad[:, j * 128 : (j + 1) * 128])
    for j in range(6):
        small[small_block(12 + j, 0)] = low(jnp.concatenate([acc_v[:, j * 128 : (j + 1) * 128], pad], 0))
    small[small_block(18, 0)] = low(jnp.concatenate([acc_h[...], pad], 0))
    for j in range(2):
        small[small_block(j, 1)] = low(jnp.concatenate([acc_s[:, j * 128 : (j + 1) * 128], pad], 0))
    gains = [acc_n[:, j * 128 : (j + 1) * 128] for j in range(12)] + [jnp.zeros((4, 128), jnp.float32)]
    small[small_block(2, 1)] = low(jnp.concatenate(gains, 0))


SCAN_PLANS = (
    {0: ("g0>",), 1: ("o0>",), 2: ("b0>",)},
    {3: ("g1>",), 4: ("o1>",), 5: ("g2>",), 6: ("o2>",), 7: ("g3>",)},
)
AFTER_SCAN = ()
VALUE_PLANS = {0: ("o3>",), 1: ("b1>",)}
AFTER_STATE = ("g4>",)
DX_PLANS = ({2: ("o4>",)}, {2: ("v0>",), 3: ("d0>",)})
TAIL = (
    "e0>", "g5>", "s0>", "b2>", "o5>", "b3.", "d1>", "e1>", "v1>", "g6.", "s1>", "o6.",
    "s2>", "v2>", "s3>", "v3>", "s4>", "d2>", "e2>", "d3.", "s5>", "v4>", "e3.", "s6>",
    "v5>", "s7.", "v6.",
)
STEPS = dict.fromkeys("gov", (0, 1, 2, 3, 5, 6, 7)) | {"s": range(8)} | dict.fromkeys("bde", range(4))


def head_row(values, lane, group):
    row = jnp.zeros(lane.shape, jnp.float32)
    for h in range(12):
        row = jnp.where(group(lane, h), values[h], row)
    return row


def layer_kernel(
    remote,
    tokens, cot_in, w_gate_in, w_value_in, w_state_in, w_out_in,
    seg, w_step_in, value_conv, value_bias, state_conv, state_bias, norm_gain, gated_gain, step_bias, log_rate, bypass_gain,
    res_gate, res_out, res_value, res_state, res_small, res_branch, res_dx,
    normed, gate, y_ref, q_ref, vpad, spad, state_low, step_low, step_raw, segc, states, carried, du, dus, head_rows,
    acc_v, acc_s, acc_h, acc_n, taps, state_taps, heads, expand, gains,
    w_gate, w_value, w_state, w_step, w_out, cot, sums, landed,
    sum_gate, sum_out, sum_value, sum_state, small, branch,
    *rest,
):
    scratch = [rest[n * 6 : (n + 1) * 6] for n in range(7)]
    value_scratch = [
        (shared[0], own_ta2, shared[2], own_ty, *shared[4:])
        for shared, own_ta2, own_ty in zip(scratch[0:2], rest[42:44], rest[44:46])
    ]
    branch_scratch = rest[46:48]
    send, recv, local = rest[48:]
    at = place()
    dx = cot
    slots = branch.at[0]

    def fetch(k):
        return pltpu.make_async_copy(tokens.at[pl.ds(pl.multiple_of(k * 256, 256), 256)], slots.at[k % 2], local.at[k % 2])

    loads = [
        pltpu.make_async_copy(src, dst, local.at[2 + n])
        for n, (src, dst) in enumerate(
            ((w_gate_in, w_gate), (w_value_in, w_value), (w_state_in, w_state), (cot_in, cot), (w_out_in, w_out))
        )
    ]
    fetch(0).start()
    for cp in loads:
        cp.start()
    if remote:
        greet(dp_peers(at) + tensor_peers(at))

    orders = (("x", "z"), ("z", "x"))

    def pair(first, buf, res, scratch, across=None):
        return [
            SumOverDp(at, order, buf.at[n], res.at[n], scratch[n], (send, recv, (first + n) * DP_SEMS), across)
            for n, order in enumerate(orders)
        ]

    last = 9 * DP_SEMS
    dx_scratch = (w_out.at[pl.ds(0, 2)], w_out.at[2])
    left, right, both_sides = pl.ds(0, 768), pl.ds(768, 768), pl.ds(0, 1536)
    engines = {
        "g": pair(0, sum_gate, res_gate, scratch[0:2]),
        "o": pair(2, sum_out, res_out, scratch[2:4]),
        "v": pair(4, sum_value, res_value, value_scratch),
        "s": pair(6, sum_state, res_state, scratch[4:6], pl.ds(0, 32))
        + [SumOverDp(at, orders[0], small, res_small, scratch[6], (send, recv, 8 * DP_SEMS), pl.ds(32, 32))],
        "b": [SumOverTensor(at, both_sides, branch, res_branch, branch_scratch, (send, recv, last))],
        "d": [SumOverTensor(at, left, dx, res_dx, dx_scratch, (send, recv, last + TENSOR_SEMS))],
        "e": [SumOverTensor(at, right, dx, res_dx, dx_scratch, (send, recv, last + 2 * TENSOR_SEMS))],
    }

    def act(*plan):
        if not remote:
            return
        for word in plan:
            steps, step = STEPS[word[0]], int(word[1])
            if word[2:]:
                for engine in engines[word[0]]:
                    engine.finish(steps[step])
                step += 1
            if word[2:] != ".":
                for engine in engines[word[0]]:
                    engine.start(steps[step])

    def act_at(i, plans):
        for n, plan in plans.items():

            @pl.when(i == n)
            def _():
                act(*plan)

    for ref in (du, dus, head_rows, carried, acc_v, acc_s, acc_h, acc_n, taps, state_taps, gains):
        ref[...] = jnp.zeros_like(ref)
    vpad[0:8, :] = jnp.zeros((8, 768), jnp.float32)
    spad[0:8, :] = jnp.zeros((8, 256), jnp.float32)
    columns_of_segments(seg, segc)
    taps[0:4, :] = value_conv[...]
    taps[4:5, :] = value_bias[...].reshape(1, 768)
    state_taps[0:4, :] = state_conv[...]
    state_taps[4:5, :] = state_bias[...].reshape(1, 256)
    lane = iota((8, 128), 1)
    heads[...] = head_row(step_bias, lane, lambda l, h: (l % 16 == h) & (l < 48))
    rate = head_row(log_rate, lane, lambda l, h: (l % 16 == h) & (l < 48))
    heads[1:2, :] = jnp.where((lane % 16 < 12) & (lane < 48), -jnp.exp(rate), 0.0)[0:1]
    gains[0:1, :] = norm_gain[...].reshape(1, 1536)
    gains[1:2, 0:768] = gated_gain[...].reshape(1, 768)
    gains[2:3, 0:768] = head_row(bypass_gain, iota((1, 768), 1), lambda l, h: l // 64 == h)
    expand[...] = expansion()
    chosen = ((iota((12, 128), 1) % 16 == iota((12, 128), 0)) & (iota((12, 128), 1) < 48)).astype(jnp.bfloat16)
    w_step[...] = low(mul_tn(chosen, w_step_in[...]))
    for cp in loads[:3]:
        cp.wait()

    def project(k, carry):
        rows = pl.ds(pl.multiple_of(k * 256, 256), 256)
        padded = pl.ds(pl.multiple_of(8 + k * 256, 8), 256)

        @pl.when(k < 3)
        def _():
            fetch(k + 1).start()

        fetch(k).wait()
        hidden = slots[k % 2].astype(jnp.float32)
        inverse = lax.rsqrt(jnp.sum(hidden * hidden, 1, keepdims=True) / 1536 + EPS)
        normal = low(hidden * inverse * gains[0:1, :])
        normed[rows, :] = normal
        gate[rows, :] = low(mul(normal, w_gate[...]))
        vpad[padded, :] = mul(normal, w_value[...])
        spad[padded, :] = mul(normal, w_state[...])
        step_raw[rows, :] = mul_nt(normal, w_step[...])
        return carry

    lax.fori_loop(0, 4, project, 0)
    for cp in loads[3:]:
        cp.wait()

    def project_back(k, carry):
        rows = pl.ds(pl.multiple_of(k * 256, 256), 256)
        q_ref[rows, :] = low(mul_nt(cot[k // 2, k % 2], w_out[...].reshape(768, 1536)))
        return carry

    lax.fori_loop(0, 4, project_back, 0)

    def forward_block(k, carry):
        start = pl.multiple_of(k * 128, 128)
        rows = pl.ds(start, 128)
        keeps = kept(segc, start)
        pre = convolved(lagged(vpad, start, keeps), taps)
        x = pre * sigmoid(pre)
        pre = convolved(lagged(spad, start, keeps), state_taps)
        state = low(pre * sigmoid(pre))
        b_in, c_out = state[:, :128], state[:, 128:]
        step, cum, seg_column, seg_row, before, last, growth, tail = decay(k, start, segc, seg, step_raw, heads)
        spread = mul(jnp.concatenate([in_three(step), in_three(growth), in_three(tail)], 0), expand[...])
        xs = x * spread[:128]
        start_keep = (seg_column == before).astype(jnp.float32)
        entering = carried[...]
        states[k] = low(entering)
        outside = mul(c_out, low(entering)) * (spread[128:256] * wide(start_keep))
        through = spread[255:256] * wide((last == before).astype(jnp.float32))
        carried[...] = through * entering + mul_tn(b_in, low(xs * spread[256:]))
        scores = mul_nt(c_out, b_in)
        bias = jnp.where((seg_column == seg_row) & (iota((128, 128), 0) >= iota((128, 128), 1)), 0.0, -1e30)
        cum_rows = cum.T
        first = iota((128, 128), 1) < 64
        inside = []
        for pair in range(6):
            own = xs[:, pair * 128 : (pair + 1) * 128]
            right = low(jnp.concatenate([jnp.where(first, own, 0.0), jnp.where(first, 0.0, own)], 0))
            left = [
                low(scores * jnp.exp(cum[:, h : h + 1] - cum_rows[h : h + 1, :] + bias)) for h in (2 * pair, 2 * pair + 1)
            ]
            inside.append(mul(jnp.concatenate(left, 1), right))
        y = jnp.concatenate(inside, 1) + outside + gains[2:3, 0:768] * x
        y_ref[rows, :] = low(y)
        raw = gate[rows, :].astype(jnp.float32)
        gated = y * (raw * sigmoid(raw))
        squares = jnp.sum(gated * gated, 1, keepdims=True)
        cross = jnp.sum(q_ref[rows, :].astype(jnp.float32) * gains[1:2, 0:768] * gated, 1, keepdims=True)
        lanes = iota((128, 128), 1)
        sums[k] = jnp.where(lanes == 0, squares, jnp.where(lanes == 1, cross, 0.0)).T[0:8, :]
        return carry

    lax.fori_loop(0, 8, forward_block, 0)

    if remote:
        peers = tensor_peers(at)
        exchange = [
            pltpu.make_async_remote_copy(
                src_ref=sums,
                dst_ref=landed.at[at["t"]],
                send_sem=send.at[last + 3 * TENSOR_SEMS + n],
                recv_sem=recv.at[last + 3 * TENSOR_SEMS + n],
                device_id=peer,
                device_id_type=MESH_ID,
            )
            for n, peer in enumerate(peers)
        ]
        for cp in exchange:
            cp.start()
        landed[at["t"]] = sums[...]
        for cp in exchange:
            cp.wait()
    else:
        for n in range(4):
            landed[n] = sums[...] * 0.75

    def middle(k, carry):
        total = (landed[0, k] + landed[1, k]) + (landed[2, k] + landed[3, k])
        middle_block(k, total, gains[1:2, 0:768], gate, y_ref, q_ref, acc_v)
        return carry

    lax.fori_loop(0, 8, middle, 0)
    gate_low, gate_normed, dy = gate, y_ref, q_ref
    value_low = y_ref

    def gate_weights(i, carry):
        put(sum_gate, i, mul_tn(normed[:, pl.ds(pl.multiple_of(i * 384, 128), 384)], gate_low[...]))
        return carry

    def out_weights(i, carry):
        out_rows = pl.ds(pl.multiple_of((i % 2) * 384, 128), 384)
        out_columns = pl.ds(pl.multiple_of((i // 2) * 768, 128), 768)
        put(sum_out, i, mul_tn(gate_normed[:, out_rows], cot[:, :, :, out_columns].reshape(1024, 768)))
        return carry

    def branch_rows(i, carry):
        rows = pl.ds(pl.multiple_of(i * 256, 256), 256)
        branch[i // 2, i % 2] = low(mul(gate_normed[rows, :], w_out[...].reshape(768, 1536)))
        return carry

    lax.fori_loop(0, 4, gate_weights, 0)
    act("g0")
    lax.fori_loop(0, 4, out_weights, 0)
    act("o0")
    lax.fori_loop(0, 4, branch_rows, 0)
    act("b0")
    carried[...] = jnp.zeros((128, 768), jnp.float32)

    def scan(i, carry):
        act_at(i, SCAN_PLANS[0])
        backward_block(
            7 - i, vpad, spad, step_raw, seg, segc, taps, state_taps, heads, expand, gains[2:3, 0:768], states, dy,
            carried, du, dus, head_rows, value_low, state_low, step_low, acc_v, acc_s, acc_h,
            lambda: act_at(i, SCAN_PLANS[1]),
        )
        return carry

    lax.fori_loop(0, 8, scan, 0)
    act(*AFTER_SCAN)

    def value_weights(i, carry):
        put(sum_value, i, mul_tn(normed[:, pl.ds(pl.multiple_of(i * 384, 128), 384)], value_low[...]))
        act_at(i, VALUE_PLANS)
        return carry

    def state_weights(i, carry):
        thirds = [
            mul_tn(normed[:, pl.ds(pl.multiple_of(q * 512 + i * 128, 128), 128)], state_low[...]) for q in range(3)
        ]
        put(sum_state, i, jnp.concatenate(thirds, 1))
        return carry

    lax.fori_loop(0, 4, value_weights, 0)
    act("v0")
    lax.fori_loop(0, 4, state_weights, 0)
    act(*AFTER_STATE)

    def dx_rows(half, i):
        rows = pl.ds(pl.multiple_of(i * 256, 256), 256)
        columns = slice(half * 768, half * 768 + 768)
        part = mul_nt(gate_low[rows, :], w_gate[columns, :]) + mul_nt(value_low[rows, :], w_value[columns, :])
        part = part + mul_nt(state_low[rows, :], w_state[columns, :]) + mul(step_low[rows, :], w_step[:, columns])
        dx[i // 2, i % 2, :, columns] = low(part)
        acc_n[0:1, columns] += jnp.sum(part * normed[rows, columns].astype(jnp.float32), 0, keepdims=True)
        act_at(i, DX_PLANS[half])

    for half in range(2):

        def dx_half(i, carry):
            dx_rows(half, i)
            return carry

        lax.fori_loop(0, 4, dx_half, 0)
        act("de"[half] + "0")
    step_grad = mul_tn(step_low[...], normed[...])[0:16, :]
    put_small(small, acc_v, acc_s, acc_h, acc_n[0:1, :] / gains[0:1, :], step_grad)
    act("s0", *TAIL)
    if not remote:
        results = (res_gate, res_out, res_value, res_state, res_small, res_branch, res_dx)
        copies = [
            pltpu.make_async_copy(src, dst, local.at[n])
            for n, (src, dst) in enumerate(zip((sum_gate, sum_out, sum_value, sum_state, small, branch, dx), results))
        ]
        for cp in copies:
            cp.start()
        for cp in copies:
            cp.wait()


def layer(*operands, remote=True):
    f32, bf16 = jnp.float32, jnp.bfloat16
    weight, rows = (2, 4, 4, 96, 384), (2, 2, 256, 1536)
    outs = [weight, weight, weight, (2, 4, 4, 32, 384), (4, 4, 64, 128), rows, rows]
    scratch = [
        ((1024, 1536), bf16), ((1024, 768), bf16), ((1024, 768), bf16), ((1024, 768), bf16), ((1032, 768), f32),
        ((1032, 256), f32), ((1024, 256), bf16), ((1024, 128), bf16), ((1024, 128), f32),
        ((1040, 128), f32), ((8, 128, 768), bf16), ((128, 768), f32), ((136, 768), f32), ((136, 256), f32), ((128, 128), f32),
        ((8, 768), f32), ((8, 256), f32), ((8, 128), f32), ((8, 1536), f32), ((8, 768), f32), ((8, 256), f32),
        ((8, 128), f32), ((128, 768), bf16), ((8, 1536), f32),
        ((1536, 768), bf16), ((1536, 768), bf16), ((1536, 256), bf16), ((128, 1536), bf16), ((3, 256, 1536), bf16),
        (rows, bf16), ((8, 8, 128), f32), ((4, 8, 8, 128), f32),
    ] + [(shape, bf16) for shape in outs[:6]]
    vmem, hbm, smem = [pl.BlockSpec(memory_space=space) for space in (pltpu.VMEM, pl.ANY, pltpu.SMEM)]
    count = 9 * DP_SEMS + 3 * TENSOR_SEMS + 3
    return pl.pallas_call(
        functools.partial(layer_kernel, remote),
        out_shape=[jax.ShapeDtypeStruct(shape, bf16) for shape in outs],
        in_specs=[hbm] * 6 + [vmem] * 8 + [smem] * 3,
        out_specs=[hbm] * 7,
        scratch_shapes=[pltpu.VMEM(shape, kind) for shape, kind in scratch]
        + dp_scratch(96, 384) * 4
        + dp_scratch(32, 384, 32) * 2
        + dp_scratch(64, 128, 32)
        + [pltpu.VMEM((2, 4, 96, 384), bf16)] * 2
        + [pltpu.VMEM((96, 384), bf16)] * 2
        + [pltpu.VMEM((2, 256, 1536), bf16), pltpu.VMEM((256, 1536), bf16)]
        + [pltpu.SemaphoreType.DMA((count,)), pltpu.SemaphoreType.DMA((count,)), pltpu.SemaphoreType.DMA((7,))],
        compiler_params=pltpu.CompilerParams(
            collective_id=0 if remote else None, has_side_effects=True, vmem_limit_bytes=63 * 2**20
        ),
        name="layer",
    )(*operands)


def finish_kernel(
    tokens, cot, norm_gain, sum_gate, sum_out, sum_value, sum_state, small, branch, dx,
    mixed, grad_tokens, gate, value, out, state, step, value_taps, value_bias, state_taps, state_bias, step_bias, log_rate,
    bypass, gain, mixer_gain,
):
    hidden = tokens[...].astype(jnp.float32)
    inverse = lax.rsqrt(jnp.sum(hidden * hidden, 1, keepdims=True) / 1536 + EPS)
    mixed[...] = low(hidden + branch[...].astype(jnp.float32))
    scaled = dx[...].astype(jnp.float32) * norm_gain[...].reshape(1, 1536)
    along = jnp.sum(scaled * hidden, 1, keepdims=True) * (inverse * inverse * inverse / 1536)
    grad_tokens[...] = cot[...].astype(jnp.float32) + inverse * scaled - hidden * along
    for stream in range(2):
        columns = slice(stream * 384, (stream + 1) * 384)
        for j in range(2):
            rows = slice(j * 96, (j + 1) * 96)
            for result, summed in ((gate, sum_gate), (out, sum_out), (value, sum_value)):
                result[rows, columns] = summed[stream, 0, j].astype(jnp.float32)
    for j in range(2):
        rows = slice(j * 32, (j + 1) * 32)
        first, second = [sum_state[stream, 0, j].astype(jnp.float32) for stream in range(2)]
        state[0, rows, :] = first[:, 0:256]
        state[1, rows, 0:128] = first[:, 256:384]
        state[1, rows, 128:256] = second[:, 0:128]
        state[2, rows, :] = second[:, 128:384]

    @pl.when(pl.program_id(0) == 0)
    def _():
        def block(j, across):
            return small[small_block(j, across)].astype(jnp.float32)

        step[...] = jnp.concatenate([block(j, 0) for j in range(12)], 1)[0:12, :]
        channels = jnp.concatenate([block(12 + j, 0) for j in range(6)], 1)
        value_taps[...] = channels[0:4]
        value_bias[...] = channels[4:5].reshape(768)
        mixer_gain[...] = channels[5:6].reshape(768)
        bypass[...] = mul_nt(low(channels), expansion())[6:7, 0:12].reshape(12)
        per_head = block(18, 0)
        step_bias[...] = per_head[0:1, 0:12].reshape(12)
        log_rate[...] = per_head[1:2, 0:12].reshape(12)
        states_small = jnp.concatenate([block(j, 1) for j in range(2)], 1)
        state_taps[...] = states_small[0:4]
        state_bias[...] = states_small[4:5].reshape(256)
        gains = block(2, 1)
        gain[...] = jnp.concatenate([gains[j : j + 1, :] for j in range(12)], 1).reshape(1536)


def finished(tokens, cot, norm_gain, *sums):
    f32 = jnp.float32
    by_rows = pl.BlockSpec((128, 1536), lambda g: (g, 0))
    weight = pl.BlockSpec((192, 768), lambda g: (g, 0))

    def whole(*shape):
        return pl.BlockSpec(shape, lambda g: (0,) * len(shape))

    rest = [(12, 1536), (4, 768), (768,), (4, 256), (256,), (12,), (12,), (12,), (1536,), (768,)]
    return pl.pallas_call(
        finish_kernel,
        grid=(8,),
        out_shape=[
            jax.ShapeDtypeStruct((1024, 1536), jnp.bfloat16),
            jax.ShapeDtypeStruct((1024, 1536), f32),
            jax.ShapeDtypeStruct((1536, 768), f32),
            jax.ShapeDtypeStruct((1536, 768), f32),
            jax.ShapeDtypeStruct((768, 1536), f32),
            jax.ShapeDtypeStruct((3, 512, 256), f32),
        ]
        + [jax.ShapeDtypeStruct(shape, f32) for shape in rest],
        in_specs=[
            by_rows,
            by_rows,
            whole(1536),
            *[pl.BlockSpec((2, 1, 2, 96, 384), lambda g: (0, g // 2, g % 2, 0, 0))] * 3,
            pl.BlockSpec((2, 1, 2, 32, 384), lambda g: (0, g // 2, g % 2, 0, 0)),
            whole(4, 4, 64, 128),
            by_rows,
            by_rows,
        ],
        out_specs=[
            by_rows,
            by_rows,
            weight,
            weight,
            pl.BlockSpec((192, 768), lambda g: ((g // 2) % 2 * 2 + g % 2, g // 4)),
            pl.BlockSpec((3, 64, 256), lambda g: (0, g, 0)),
        ]
        + [whole(*shape) for shape in rest],
        compiler_params=pltpu.CompilerParams(vmem_limit_bytes=60 * 2**20),
        name="finish",
    )(tokens, cot, norm_gain, *sums)


def local(
    tokens,
    segment,
    gate_proj,
    value_proj,
    state_proj,
    step_proj,
    value_conv,
    value_conv_bias,
    state_conv,
    state_conv_bias,
    step_bias,
    log_rate,
    bypass_gain,
    norm_gain,
    gated_norm_gain,
    out_proj,
    cotangent,
):
    *sums, branch, dx = layer(
        tokens, cotangent.reshape(2, 2, 256, 1536), gate_proj, value_proj, state_proj, out_proj.reshape(3, 256, 1536), segment, step_proj.T,
        value_conv, value_conv_bias, state_conv, state_conv_bias, norm_gain, gated_norm_gain, step_bias, log_rate, bypass_gain,
    )
    rows = tokens.shape
    (
        mixed_out, grad_tokens, grad_gate, grad_value, grad_out, grad_state, grad_step, grad_value_conv, grad_value_bias,
        grad_state_conv, grad_state_bias, grad_step_bias, grad_log_rate, grad_bypass, grad_gain, grad_mixer_gain,
    ) = finished(tokens, cotangent, norm_gain, *sums, branch.reshape(rows), dx.reshape(rows))
    return (
        mixed_out,
        grad_tokens,
        grad_gate,
        grad_value,
        grad_state.reshape(state_proj.shape),
        grad_step.T,
        grad_value_conv,
        grad_value_bias,
        grad_state_conv,
        grad_state_bias,
        grad_step_bias,
        grad_log_rate,
        grad_bypass,
        grad_gain,
        grad_mixer_gain,
        grad_out,
    )


def solution(mesh):
    placed = (
        P("dp", None),
        P("dp", None),
        P(None, "tensor"),
        P(None, "tensor"),
        P(),
        P(None, "tensor"),
        P(None, "tensor"),
        P("tensor"),
        P(),
        P(),
        P("tensor"),
        P("tensor"),
        P("tensor"),
        P(),
        P("tensor"),
        P("tensor", None),
        P("dp", None),
    )
    return jax.shard_map(
        local,
        mesh=mesh,
        in_specs=placed,
        out_specs=(
            P("dp", None),
            P("dp", None),
            P(None, "tensor"),
            P(None, "tensor"),
            P(),
            P(None, "tensor"),
            P(None, "tensor"),
            P("tensor"),
            P(),
            P(),
            P("tensor"),
            P("tensor"),
            P("tensor"),
            P(),
            P("tensor"),
            P("tensor", None),
        ),
        check_vma=False,
    )
```

```python
import functools

import jax
import jax.numpy as jnp
from jax import lax
from jax.experimental import pallas as pl
from jax.experimental.pallas import tpu as pltpu
from jax.sharding import PartitionSpec as P

EPS = 1e-05
MESH_ID = pl.DeviceIdType.MESH


def place():
    dp = lax.axis_index("dp")
    tensor = lax.axis_index("tensor")
    return {"x": dp // 8, "y": (dp // 4) % 2, "z": dp % 4, "t": tensor}


def device_at(at, **moved):
    spot = dict(at, **moved)
    return (spot["x"] * 8 + spot["y"] * 4 + spot["z"], spot["t"])


def dp_peers(at):
    return [
        device_at(at, x=(at["x"] + 1) % 4),
        device_at(at, x=(at["x"] + 3) % 4),
        device_at(at, z=(at["z"] + 1) % 4),
        device_at(at, z=(at["z"] + 3) % 4),
        device_at(at, y=1 - at["y"]),
    ]


def tensor_peers(at):
    return [device_at(at, t=(at["t"] + step) % 4) for step in (1, 2, 3)]


def greet(peers):
    barrier = pltpu.get_barrier_semaphore()
    for peer in peers:
        pl.semaphore_signal(barrier, inc=1, device_id=peer, device_id_type=MESH_ID)


def added(*refs):
    total = refs[0][...].astype(jnp.float32)
    for ref in refs[1:]:
        total = total + ref[...].astype(jnp.float32)
    return total.astype(jnp.bfloat16)


class Staged:
    def __init__(self, send, recv, first):
        self.send, self.recv, self.first = send, recv, first

    def made(self, stage):
        at = self.first + sum(self.counts[:stage])
        for n, (src, dst, peer) in enumerate(self.copies(stage)):
            if peer is None:
                yield pltpu.make_async_copy(src, dst, self.recv.at[at + n])
            else:
                yield pltpu.make_async_remote_copy(
                    src_ref=src,
                    dst_ref=dst,
                    send_sem=self.send.at[at + n],
                    recv_sem=self.recv.at[at + n],
                    device_id=peer,
                    device_id_type=MESH_ID,
                )

    def start(self, stage):
        for cp in self.made(stage):
            cp.start()

    def finish(self, stage):
        for cp in self.made(stage):
            cp.wait()
        self.settle(stage)


class SumOverDp(Staged):
    counts = (3, 2, 3, 1, 3, 4, 3, 2)

    def __init__(self, at, order, buf, res, scratch, sems, across=None, direct=False):
        super().__init__(*sems)
        self.at, self.buf, self.res, self.across, self.direct = at, buf, res, across, direct
        self.ta1, self.ta2, self.tb, self.ty, self.own, self.tt = scratch
        a_axis, b_axis = order
        self.a, self.b = at[a_axis], at[b_axis]
        self.a_up, self.a_down, self.a_far = [(self.a + n) % 4 for n in (1, 3, 2)]
        self.a_right, self.a_left = [device_at(at, **{a_axis: n}) for n in (self.a_up, self.a_down)]
        self.a_others = [(self.a + n) % 4 for n in (1, 2, 3)]
        self.a_peers = [device_at(at, **{a_axis: n}) for n in self.a_others]
        self.b_others = [(self.b + n) % 4 for n in (1, 2, 3)]
        self.b_peers = [device_at(at, **{b_axis: n}) for n in self.b_others]
        self.other = device_at(at, y=1 - at["y"])

    def copies(self, stage):
        buf, res, a, b, own = self.buf, self.res, self.a, self.b, self.own
        near, far = pl.ds(0, 2), pl.ds(2, 2)
        if stage == 0 and self.direct:
            return [(buf.at[i], self.ta1.at[n], peer) for n, (i, peer) in enumerate(zip(self.a_others, self.a_peers))]
        if stage == 6 and self.direct:
            return [(res.at[a], res.at[a], peer) for peer in self.a_peers]
        if stage == 0:
            return [(buf.at[self.a_far, near], self.ta1.at[0], self.a_right), (buf.at[self.a_far, far], self.ta1.at[1], self.a_left)]
        if stage == 1:
            return [(buf.at[self.a_up], self.ta2.at[0], self.a_right), (buf.at[self.a_down], self.ta2.at[1], self.a_left)]
        if stage == 2:
            return [(buf.at[a, j], self.tb.at[n], peer) for n, (j, peer) in enumerate(zip(self.b_others, self.b_peers))]
        if stage == 3:
            return [(buf.at[a, b], self.ty, self.other)]
        if stage == 4:
            return [(own.at[self.across], self.tt.at[self.at["t"]], peer) for peer in tensor_peers(self.at)]
        if stage == 5:
            home = res.at[a, b]
            return [(own, home, peer) for peer in self.b_peers] + [(own, home, None)]
        if stage == 6:
            return [(res.at[a], res.at[a], self.a_right), (res.at[a], res.at[a], self.a_left)]
        return [
            (res.at[self.a_down, near], res.at[self.a_down, near], self.a_right),
            (res.at[self.a_up, far], res.at[self.a_up, far], self.a_left),
        ]

    def settle(self, stage):
        buf, a, b, own = self.buf, self.a, self.b, self.own
        if stage == 0 and self.direct:
            for j in range(4):
                buf[a, j] = added(buf.at[a, j], *(self.ta1.at[n, j] for n in range(3)))
        elif stage == 0:
            for j in range(2):
                buf[self.a_up, j] = added(buf.at[self.a_up, j], self.ta1.at[0, j])
                buf[self.a_down, 2 + j] = added(buf.at[self.a_down, 2 + j], self.ta1.at[1, j])
        elif stage == 1:
            for j in range(4):
                buf[a, j] = added(buf.at[a, j], self.ta2.at[0, j], self.ta2.at[1, j])
        elif stage == 2:
            buf[a, b] = added(buf.at[a, b], *(self.tb.at[n] for n in range(3)))
        elif stage == 3:
            own[...] = added(buf.at[a, b], self.ty)
        elif stage == 4:
            self.tt[self.at["t"]] = own[self.across]
            own[self.across] = added(*(self.tt.at[n] for n in range(4)))


DP_SEMS = sum(SumOverDp.counts)


def dp_scratch(rows, width, across=16, direct=False):
    first = [(3, 4, rows, width), (1, 16, width)] if direct else [(2, 2, rows, width), (2, 4, rows, width)]
    shapes = first + [(3, rows, width), (rows, width), (rows, width), (4, across, width)]
    return [pltpu.VMEM(shape, jnp.bfloat16) for shape in shapes]


class SumOverTensor(Staged):
    counts = (1, 1, 2, 1)

    def __init__(self, at, columns, buf, res, scratch, sems):
        super().__init__(*sems)
        self.buf, self.res, self.columns = buf, res, columns
        self.t0, self.t1 = scratch
        self.c, self.h = at["t"] % 2, at["t"] // 2
        self.sibling = device_at(at, t=self.h * 2 + 1 - self.c)
        self.partner = device_at(at, t=(1 - self.h) * 2 + self.c)

    def copies(self, stage):
        buf, res, c, h, columns = self.buf, self.res, self.c, self.h, self.columns
        if stage == 0:
            return [(buf.at[1 - c, :, :, columns], self.t0.at[:, :, columns], self.sibling)]
        if stage == 1:
            return [(buf.at[c, 1 - h, :, columns], self.t1.at[:, columns], self.partner)]
        if stage == 2:
            mine, theirs = buf.at[c, h, :, columns], res.at[c, h, :, columns]
            return [(mine, theirs, self.partner), (mine, theirs, None)]
        return [(res.at[c, :, :, columns], res.at[c, :, :, columns], self.sibling)]

    def settle(self, stage):
        buf, c, h, columns = self.buf, self.c, self.h, self.columns
        if stage == 0:
            for n in range(2):
                buf[c, n, :, columns] = added(buf.at[c, n, :, columns], self.t0.at[n, :, columns])
        elif stage == 1:
            buf[c, h, :, columns] = added(buf.at[c, h, :, columns], self.t1.at[:, columns])


TENSOR_SEMS = sum(SumOverTensor.counts)


class SumState(Staged):
    counts = (1, 3, 3, 1, 1, 4, 3, 1)

    def __init__(self, at, buf, res, scratch, sems):
        super().__init__(*sems)
        self.buf, self.res = buf, res
        self.t0, self.ta, self.tb, self.ty, self.tt, self.own = scratch
        x, y, z, t = at["x"], at["y"], at["z"], at["t"]
        c = t % 2
        self.c, self.a, self.b = c, x * (1 - c) + z * c, z * (1 - c) + x * c
        self.sibling = device_at(at, t=t // 2 * 2 + 1 - c)
        self.partner = device_at(at, t=(1 - t // 2) * 2 + c)
        self.other = device_at(at, y=1 - y)
        self.a_peers = [device_at(at, x=(x + n * (1 - c)) % 4, z=(z + n * c) % 4) for n in (1, 2, 3)]
        self.b_peers = [device_at(at, x=(x + n * c) % 4, z=(z + n * (1 - c)) % 4) for n in (1, 2, 3)]

    def copies(self, stage):
        buf, res, a, b, c, own = self.buf, self.res, self.a, self.b, self.c, self.own
        if stage == 0:
            return [(buf.at[1 - c], self.t0, self.sibling)]
        if stage == 1:
            return [(buf.at[c, (a + n + 1) % 4], self.ta.at[n], peer) for n, peer in enumerate(self.a_peers)]
        if stage == 2:
            return [(buf.at[c, a, (b + n + 1) % 4], self.tb.at[n], peer) for n, peer in enumerate(self.b_peers)]
        if stage == 3:
            return [(buf.at[c, a, b], self.ty, self.other)]
        if stage == 4:
            return [(own, self.tt, self.partner)]
        if stage == 5:
            return [(own, res.at[c, a, b], peer) for peer in self.b_peers] + [(own, res.at[c, a, b], None)]
        if stage == 6:
            return [(res.at[c, a], res.at[c, a], peer) for peer in self.a_peers]
        return [(res.at[c], res.at[c], self.sibling)]

    def settle(self, stage):
        buf, a, b, c = self.buf, self.a, self.b, self.c
        if stage == 0:
            for i in range(4):
                for j in range(4):
                    buf[c, i, j] = added(buf.at[c, i, j], self.t0.at[i, j])
        elif stage == 1:
            for j in range(4):
                buf[c, a, j] = added(buf.at[c, a, j], *(self.ta.at[n, j] for n in range(3)))
        elif stage == 2:
            buf[c, a, b] = added(buf.at[c, a, b], *(self.tb.at[n] for n in range(3)))
        elif stage == 3:
            self.own[...] = added(buf.at[c, a, b], self.ty)
        elif stage == 4:
            self.own[...] = added(self.own, self.tt)


STATE_SEMS = sum(SumState.counts)


def state_scratch(rows, width):
    block = (rows, width)
    shapes = [(4, 4) + block, (3, 4) + block, (3,) + block, block, block, block]
    return [pltpu.VMEM(shape, jnp.bfloat16) for shape in shapes]


def wide(tile, count=6):
    return jnp.concatenate([tile] * count, axis=1)


def mul(left, right):
    return jnp.dot(left, right, preferred_element_type=jnp.float32)


def mul_nt(left, right):
    return lax.dot_general(left, right, (((1,), (1,)), ((), ())), preferred_element_type=jnp.float32)


def mul_tn(left, right):
    return lax.dot_general(left, right, (((0,), (0,)), ((), ())), preferred_element_type=jnp.float32)


def low(value):
    return value.astype(jnp.bfloat16)


def iota(shape, dim):
    return lax.broadcasted_iota(jnp.int32, shape, dim)


def in_three(value):
    high = low(value).astype(jnp.float32)
    rest = value - high
    middle = low(rest).astype(jnp.float32)
    lane = iota(value.shape, 1)
    return low(jnp.where(lane < 16, high, jnp.where(lane < 32, middle, rest - middle)))


def exact_sum(ones, value):
    high = low(value)
    rest = value - high.astype(jnp.float32)
    middle = low(rest)
    return mul(ones, high) + mul(ones, middle) + mul(ones, low(rest - middle.astype(jnp.float32)))


def softplus(value):
    return jnp.maximum(value, 0.0) + jnp.log1p(jnp.exp(-jnp.abs(value)))


def sigmoid(value):
    return 1.0 / (1.0 + jnp.exp(-value))


def columns_of_segments(seg_ref, segc):
    segc[0:8, :] = jnp.full((8, 128), -1.0, jnp.float32)
    segc[1032:1040, :] = jnp.full((8, 128), -1.0, jnp.float32)

    def fill(k, carry):
        row = jnp.broadcast_to(seg_ref[:, pl.ds(pl.multiple_of(k * 128, 128), 128)].astype(jnp.float32), (128, 128))
        segc[pl.ds(pl.multiple_of(8 + k * 128, 8), 128), :] = row.T
        return carry

    lax.fori_loop(0, 8, fill, 0)


def kept(segc, start):
    around = segc[pl.ds(start, 144), :]
    here = around[8:, :]
    return [(pltpu.roll(around, lag, 0)[8:, :] == here).astype(jnp.float32) for lag in (1, 2, 3)]


def lagged(padded, start, keeps):
    around = padded[pl.ds(start, 136), :]
    count = around.shape[1] // 128
    return [around[8:, :]] + [pltpu.roll(around, lag, 0)[8:, :] * wide(keep[:128], count) for lag, keep in zip((1, 2, 3), keeps)]


def convolved(shifted, taps):
    total = taps[4:5, :] + taps[0:1, :] * shifted[0]
    for lag in (1, 2, 3):
        total = total + taps[lag : lag + 1, :] * shifted[lag]
    return total


def decay(k, start, segc, seg_ref, step_raw, heads):
    rows = pl.ds(start, 128)
    step = softplus(step_raw[rows, :] + heads[0:1, :])
    tri = (iota((128, 128), 0) >= iota((128, 128), 1)).astype(jnp.bfloat16)
    cum = exact_sum(tri, step * heads[1:2, :])
    seg_column = segc[pl.ds(start + 8, 128), :]
    seg_row = seg_ref[:, rows].astype(jnp.float32)
    before = segc[pl.ds(start, 8), :][7:8, :]
    last = seg_column[127:128, :]
    growth = jnp.exp(cum)
    tail = jnp.exp(cum[127:128, :] - cum) * (seg_column == last).astype(jnp.float32)
    return step, cum, seg_column, seg_row, before, last, growth, tail


def expansion():
    row, column = iota((128, 768), 0), iota((128, 768), 1)
    return ((row < 48) & (row % 16 == column // 64)).astype(jnp.bfloat16)


def head_sums(value, expand):
    high = low(value)
    return mul_nt(high, expand) + mul_nt(low(value - high.astype(jnp.float32)), expand)


def slope(pre, sig):
    return sig * (1.0 + pre * (1.0 - sig))


def middle_block(k, total, gated_gain, gate, y_ref, q_ref, acc_v):
    rows = pl.ds(pl.multiple_of(k * 128, 128), 128)
    columns = jnp.concatenate([total] * 16, 0).T
    scale = lax.rsqrt(columns[:, 0:1] / 3072 + EPS)
    pull = columns[:, 1:2] * scale * scale * scale / 3072
    raw, y, q = [ref[rows, :].astype(jnp.float32) for ref in (gate, y_ref, q_ref)]
    sig = sigmoid(raw)
    act = raw * sig
    gated = y * act
    scaled = gated * scale
    y_ref[rows, :] = low(scaled * gated_gain)
    acc_v[5:6, :] += jnp.sum(q * scaled, 0, keepdims=True)
    grad_gated = scale * (q * gated_gain) - gated * pull
    q_ref[rows, :] = low(grad_gated * act)
    gate[rows, :] = low(grad_gated * y * slope(raw, sig))


def put(buf, i, value):
    pieces = low(value.reshape(4, value.shape[0] // 4, 768))
    for stream in range(2):
        buf[stream, i] = pieces[..., stream * 384 : (stream + 1) * 384]


def backward_block(
    k, vpad, spad, step_raw, seg_ref, segc, taps, state_taps, heads, expand, bypass, states, dy,
    dstate, du, dus, head_rows, value_low, state_low, step_low, acc_v, acc_s, acc_h, between,
):
    start = pl.multiple_of(k * 128, 128)
    rows = pl.ds(start, 128)
    keeps = kept(segc, start)
    values = lagged(vpad, start, keeps)
    pre = convolved(values, taps)
    sig = sigmoid(pre)
    x = pre * sig
    state_values = lagged(spad, start, keeps)
    state_pre = convolved(state_values, state_taps)
    state_sig = sigmoid(state_pre)
    state = low(state_pre * state_sig)
    b_in, c_out = state[:, :128], state[:, 128:]
    step, cum, seg_column, seg_row, before, last, growth, tail = decay(k, start, segc, seg_ref, step_raw, heads)
    spread = mul(jnp.concatenate([in_three(step), in_three(growth), in_three(tail)], 0), expand[...])
    step_wide, tail_wide = spread[:128], spread[256:]
    growth_wide = spread[128:256] * wide((seg_column == before).astype(jnp.float32))
    through = spread[255:256] * wide((last == before).astype(jnp.float32))
    xs = x * step_wide
    entering = states[k]
    grad_state = dstate[...]
    grad_state_low = low(grad_state)
    dyk = dy[rows, :].astype(jnp.float32)
    grown = low(dyk * growth_wide)
    outside = mul(c_out, entering) * growth_wide
    dxs_after = mul(b_in, grad_state_low) * tail_wide
    grad_c = mul_nt(grown, entering)
    grad_b = mul_nt(low(xs * tail_wide), grad_state_low)
    end = jnp.sum(entering.astype(jnp.float32) * grad_state, 0, keepdims=True) * through
    dstate[...] = through * grad_state + mul_tn(c_out, grown)
    scores = mul_nt(b_in, c_out)
    row, column = iota((128, 128), 0), iota((128, 128), 1)
    bias = jnp.where((seg_column == seg_row) & (row <= column), 0.0, -1e30)
    tri = (row >= column).astype(jnp.bfloat16)
    strict = row < column
    cum_rows = cum.T
    first = column < 64
    grad_scores = jnp.zeros((128, 128), jnp.float32)
    inside = []
    for pair in range(6):
        if pair == 3:
            between()
        lanes = slice(pair * 128, (pair + 1) * 128)
        own = dyk[:, lanes]
        both = low(jnp.concatenate([jnp.where(first, own, 0.0), jnp.where(first, 0.0, own)], 0))
        grad_weights = mul_nt(low(xs[:, lanes]), both)
        weights, moved = [], []
        for side in range(2):
            h = 2 * pair + side
            faded = jnp.exp(cum_rows[h : h + 1, :] - cum[:, h : h + 1] + bias)
            pulled = grad_weights[:, side * 128 : (side + 1) * 128] * faded
            grad_scores = grad_scores + pulled
            moved.append(low(pulled * scores))
            weights.append(low(scores * faded))
        inside.append(mul(jnp.concatenate(weights, 1), both))
        later = mul(jnp.concatenate(moved, 0), tri)
        for side in range(2):
            h = 2 * pair + side
            part = jnp.where(strict, later[side * 128 : (side + 1) * 128], 0.0)
            head_rows[h : h + 1, :] = jnp.sum(part, 0, keepdims=True)
    grad_scores = low(grad_scores)
    grad_b = grad_b + mul(grad_scores, c_out)
    grad_c = grad_c + mul_tn(grad_scores, b_in)
    dxs = jnp.concatenate(inside, 1) + dxs_after
    dx = dxs * step_wide + bypass * dyk
    summed = head_sums(jnp.concatenate([dxs * x, dyk * outside, xs * dxs_after], 0), expand[...])
    end = head_sums(jnp.broadcast_to(end, (16, 768)), expand[...])
    upper = (row <= column).astype(jnp.bfloat16)
    below = (row > column).astype(jnp.bfloat16)
    grad_decay = exact_sum(upper, summed[128:256]) + exact_sum(below, summed[256:]) + end[0:1, :] + head_rows[...].T
    grad_step = summed[:128] + heads[1:2, :] * grad_decay
    grad_raw = grad_step * sigmoid(step_raw[rows, :] + heads[0:1, :])
    step_low[rows, :] = low(jnp.where(column < 16, grad_raw, 0.0))
    acc_h[0:1, :] += jnp.sum(grad_raw, 0, keepdims=True)
    acc_h[1:2, :] += jnp.sum(step * grad_decay, 0, keepdims=True) * heads[1:2, :]
    for grad, grads, shifted, taps_ref, acc, result in (
        (dx * slope(pre, sig), du, values, taps, acc_v, value_low),
        (jnp.concatenate([grad_b, grad_c], 1) * slope(state_pre, state_sig), dus, state_values, state_taps, acc_s, state_low),
    ):
        grads[128:136, :] = grads[0:8, :]
        grads[0:128, :] = grad
        for lag in range(4):
            acc[lag : lag + 1, :] += jnp.sum(grad * shifted[lag], 0, keepdims=True)
        acc[4:5, :] += jnp.sum(grad, 0, keepdims=True)
        around = grads[...]
        count = around.shape[1] // 128
        total = grad * taps_ref[0:1, :]
        for lag, keep in zip((1, 2, 3), keeps):
            total = total + taps_ref[lag : lag + 1, :] * pltpu.roll(around * wide(keep, count), 136 - lag, 0)[:128, :]
        result[rows, :] = low(total)
    acc_v[6:7, :] += jnp.sum(dyk * x, 0, keepdims=True)


def put_small(small, acc_v, acc_h, step_grad):
    small[...] = jnp.zeros_like(small)
    rows = [acc_v[n : n + 1, j * 128 : (j + 1) * 128] for n in range(7) for j in range(6)] + [acc_h[0:1, :], acc_h[1:2, :]]
    place_in = iota((16, 128), 0)
    for j in range(12):
        block = jnp.where(place_in < 12, step_grad[:, j * 128 : (j + 1) * 128], 0.0)
        for n, row in enumerate(rows[4 * j : 4 * j + 4]):
            block = jnp.where(place_in == 12 + n, row, block)
        small[j // 4, j % 4] = low(block)


def put_shared(shared, acc_s, acc_n):
    shared[...] = jnp.zeros_like(shared)
    place_in = iota((16, 128), 0)
    for j, rows in enumerate(
        (
            [acc_n[:, n * 128 : (n + 1) * 128] for n in range(12)],
            [acc_s[n : n + 1, j * 128 : (j + 1) * 128] for n in range(5) for j in range(2)],
        )
    ):
        block = jnp.zeros((16, 128), jnp.float32)
        for n, row in enumerate(rows):
            block = jnp.where(place_in == n, row, block)
        shared[0, j] = low(block)


SCAN_PLANS = (
    {4: ("g2>",), 6: ("o0>", "b1>"), 7: ("g4>",)},
    {0: ("b0>",), 2: ("g1>",), 4: ("o0",), 5: ("g3>",)},
)
AFTER_SCAN = ()
VALUE_PLANS = {}
AFTER_STATE = ("o1>",)
DX_PLANS = ({3: ("g5>", "b2>")}, {0: ("v0>",), 1: ("o2>",), 3: ("d0>", "g6.", "o3>", "b3.")})
TAIL = (
    "v1>", "e0>", "s0>", "o4>", "d1>", "v2>", "s1>", "s2>", "o5>", "v3>", "s3>", "e1>",
    "s4>", "o6.", "v4>", "d2>", "s5>", "d3.", "e2>", "s6>", "e3.", "v5>", "s7.", "v6.",
)
RING = (0, 1, 2, 3, 5, 6, 7)


def head_row(values, lane, group):
    row = jnp.zeros(lane.shape, jnp.float32)
    for h in range(12):
        row = jnp.where(group(lane, h), values[h], row)
    return row


def layer_kernel(
    remote,
    tokens, cot_in, w_gate_in, w_value_in, w_state_in, w_out_in,
    seg, w_step_in, value_conv, value_bias, state_conv, state_bias, norm_gain, gated_gain, step_bias, log_rate, bypass_gain,
    res_gate, res_out, res_value, res_state, res_small, res_shared, res_branch, res_dx,
    normed, gate, y_ref, q_ref, vpad, spad, state_low, step_low, step_raw, segc, states, carried, du, dus, head_rows,
    acc_v, acc_s, acc_h, acc_n, taps, state_taps, heads, expand, gains,
    w_gate, w_value, w_state, w_step, w_out, cot, sums, landed,
    sum_gate, sum_out, sum_value, sum_state, small, shared, branch,
    *rest,
):
    scratch = [rest[n * 6 : (n + 1) * 6] for n in range(7)]
    value_scratch = [
        (early[0], own_ta2, early[2], own_ty, *early[4:])
        for early, own_ta2, own_ty in zip(scratch[0:2], rest[42:44], rest[44:46])
    ]
    branch_scratch = rest[46:48]
    send, recv, local = rest[48:]
    at = place()
    dx = cot
    slots = branch.at[0]

    def fetch(k):
        return pltpu.make_async_copy(tokens.at[pl.ds(pl.multiple_of(k * 256, 256), 256)], slots.at[k % 2], local.at[k % 2])

    loads = [
        pltpu.make_async_copy(src, dst, local.at[2 + n])
        for n, (src, dst) in enumerate(
            ((w_gate_in, w_gate), (w_value_in, w_value), (w_state_in, w_state), (cot_in, cot), (w_out_in, w_out))
        )
    ]
    fetch(0).start()
    for cp in loads[:3]:
        cp.start()
    friends = dp_peers(at) + tensor_peers(at)
    if remote:
        greet(friends)

    orders = (("x", "z"), ("z", "x"))

    def pair(first, buf, res, scratch):
        return [
            (SumOverDp(at, order, buf.at[n], res.at[n], scratch[n], (send, recv, (first + n) * DP_SEMS)), RING)
            for n, order in enumerate(orders)
        ]

    last = 8 * DP_SEMS + STATE_SEMS
    dx_scratch = (w_out.at[pl.ds(0, 2)], w_out.at[2])
    left, right, both_sides = pl.ds(0, 768), pl.ds(768, 768), pl.ds(0, 1536)
    engines = {
        "g": pair(0, sum_gate, res_gate, scratch[0:2]),
        "o": pair(2, sum_out, res_out, scratch[2:4]),
        "v": pair(4, sum_value, res_value, value_scratch)
        + [(SumOverDp(at, orders[0], small, res_small, scratch[4], (send, recv, 6 * DP_SEMS)), RING)],
        "s": [
            (SumState(at, sum_state, res_state, scratch[6], (send, recv, 8 * DP_SEMS)), range(8)),
            (
                SumOverDp(at, orders[0], shared, res_shared, scratch[5], (send, recv, 7 * DP_SEMS), pl.ds(0, 16), True),
                (None, 0, 2, 3, 4, 5, 6, None),
            ),
        ],
        "b": [(SumOverTensor(at, both_sides, branch, res_branch, branch_scratch, (send, recv, last)), range(4))],
        "d": [(SumOverTensor(at, left, dx, res_dx, dx_scratch, (send, recv, last + TENSOR_SEMS)), range(4))],
        "e": [(SumOverTensor(at, right, dx, res_dx, dx_scratch, (send, recv, last + 2 * TENSOR_SEMS)), range(4))],
    }

    def act(*plan):
        if not remote:
            return
        for word in plan:
            step = int(word[1])
            if word[2:]:
                for engine, stages in engines[word[0]]:
                    if stages[step] is not None:
                        engine.finish(stages[step])
                step += 1
            if word[2:] != ".":
                for engine, stages in engines[word[0]]:
                    if stages[step] is not None:
                        engine.start(stages[step])

    def act_at(i, plans):
        for n, plan in plans.items():

            @pl.when(i == n)
            def _():
                act(*plan)

    for ref in (du, dus, head_rows, carried, acc_v, acc_s, acc_h, acc_n, taps, state_taps, gains):
        ref[...] = jnp.zeros_like(ref)
    vpad[0:8, :] = jnp.zeros((8, 768), jnp.float32)
    spad[0:8, :] = jnp.zeros((8, 256), jnp.float32)
    columns_of_segments(seg, segc)
    taps[0:4, :] = value_conv[...]
    taps[4:5, :] = value_bias[...].reshape(1, 768)
    state_taps[0:4, :] = state_conv[...]
    state_taps[4:5, :] = state_bias[...].reshape(1, 256)
    lane = iota((8, 128), 1)
    heads[...] = head_row(step_bias, lane, lambda l, h: (l % 16 == h) & (l < 48))
    rate = head_row(log_rate, lane, lambda l, h: (l % 16 == h) & (l < 48))
    heads[1:2, :] = jnp.where((lane % 16 < 12) & (lane < 48), -jnp.exp(rate), 0.0)[0:1]
    gains[0:1, :] = norm_gain[...].reshape(1, 1536)
    gains[1:2, 0:768] = gated_gain[...].reshape(1, 768)
    gains[2:3, 0:768] = head_row(bypass_gain, iota((1, 768), 1), lambda l, h: l // 64 == h)
    expand[...] = expansion()
    chosen = ((iota((12, 128), 1) % 16 == iota((12, 128), 0)) & (iota((12, 128), 1) < 48)).astype(jnp.bfloat16)
    w_step[...] = low(mul_tn(chosen, w_step_in[...]))
    for cp in loads[:3]:
        cp.wait()
    for cp in loads[3:]:
        cp.start()

    def project(k, carry):
        rows = pl.ds(pl.multiple_of(k * 256, 256), 256)
        padded = pl.ds(pl.multiple_of(8 + k * 256, 8), 256)

        @pl.when(k < 3)
        def _():
            fetch(k + 1).start()

        fetch(k).wait()
        hidden = slots[k % 2].astype(jnp.float32)
        inverse = lax.rsqrt(jnp.sum(hidden * hidden, 1, keepdims=True) / 1536 + EPS)
        normal = low(hidden * inverse * gains[0:1, :])
        normed[rows, :] = normal
        gate[rows, :] = low(mul(normal, w_gate[...]))
        vpad[padded, :] = mul(normal, w_value[...])
        spad[padded, :] = mul(normal, w_state[...])
        step_raw[rows, :] = mul_nt(normal, w_step[...])
        return carry

    lax.fori_loop(0, 4, project, 0)
    for cp in loads[3:]:
        cp.wait()

    def project_back(k, carry):
        rows = pl.ds(pl.multiple_of(k * 256, 256), 256)
        q_ref[rows, :] = low(mul_nt(cot[k // 2, k % 2], w_out[...].reshape(768, 1536)))
        return carry

    lax.fori_loop(0, 4, project_back, 0)

    def forward_block(k, carry):
        start = pl.multiple_of(k * 128, 128)
        rows = pl.ds(start, 128)
        keeps = kept(segc, start)
        pre = convolved(lagged(vpad, start, keeps), taps)
        x = pre * sigmoid(pre)
        pre = convolved(lagged(spad, start, keeps), state_taps)
        state = low(pre * sigmoid(pre))
        b_in, c_out = state[:, :128], state[:, 128:]
        step, cum, seg_column, seg_row, before, last, growth, tail = decay(k, start, segc, seg, step_raw, heads)
        spread = mul(jnp.concatenate([in_three(step), in_three(growth), in_three(tail)], 0), expand[...])
        xs = x * spread[:128]
        start_keep = (seg_column == before).astype(jnp.float32)
        entering = carried[...]
        states[k] = low(entering)
        outside = mul(c_out, low(entering)) * (spread[128:256] * wide(start_keep))
        through = spread[255:256] * wide((last == before).astype(jnp.float32))
        carried[...] = through * entering + mul_tn(b_in, low(xs * spread[256:]))
        scores = mul_nt(c_out, b_in)
        bias = jnp.where((seg_column == seg_row) & (iota((128, 128), 0) >= iota((128, 128), 1)), 0.0, -1e30)
        cum_rows = cum.T
        first = iota((128, 128), 1) < 64
        inside = []
        for pair in range(6):
            own = xs[:, pair * 128 : (pair + 1) * 128]
            right = low(jnp.concatenate([jnp.where(first, own, 0.0), jnp.where(first, 0.0, own)], 0))
            left = [
                low(scores * jnp.exp(cum[:, h : h + 1] - cum_rows[h : h + 1, :] + bias)) for h in (2 * pair, 2 * pair + 1)
            ]
            inside.append(mul(jnp.concatenate(left, 1), right))
        y = jnp.concatenate(inside, 1) + outside + gains[2:3, 0:768] * x
        y_ref[rows, :] = low(y)
        raw = gate[rows, :].astype(jnp.float32)
        gated = y * (raw * sigmoid(raw))
        squares = jnp.sum(gated * gated, 1, keepdims=True)
        cross = jnp.sum(q_ref[rows, :].astype(jnp.float32) * gains[1:2, 0:768] * gated, 1, keepdims=True)
        lanes = iota((128, 128), 1)
        sums[k] = jnp.where(lanes == 0, squares, jnp.where(lanes == 1, cross, 0.0)).T[0:8, :]
        return carry

    lax.fori_loop(0, 8, forward_block, 0)

    if remote:
        pl.semaphore_wait(pltpu.get_barrier_semaphore(), len(friends))
        peers = tensor_peers(at)
        exchange = [
            pltpu.make_async_remote_copy(
                src_ref=sums,
                dst_ref=landed.at[at["t"]],
                send_sem=send.at[last + 3 * TENSOR_SEMS + n],
                recv_sem=recv.at[last + 3 * TENSOR_SEMS + n],
                device_id=peer,
                device_id_type=MESH_ID,
            )
            for n, peer in enumerate(peers)
        ]
        for cp in exchange:
            cp.start()
        landed[at["t"]] = sums[...]
        for cp in exchange:
            cp.wait()
    else:
        for n in range(4):
            landed[n] = sums[...] * 0.75

    def middle(k, carry):
        total = (landed[0, k] + landed[1, k]) + (landed[2, k] + landed[3, k])
        middle_block(k, total, gains[1:2, 0:768], gate, y_ref, q_ref, acc_v)
        return carry

    lax.fori_loop(0, 8, middle, 0)
    gate_low, gate_normed, dy = gate, y_ref, q_ref
    value_low = y_ref

    def gate_weights(i, carry):
        put(sum_gate, i, mul_tn(normed[:, pl.ds(pl.multiple_of(i * 384, 128), 384)], gate_low[...]))
        return carry

    def out_weights(i, carry):
        out_rows = pl.ds(pl.multiple_of((i % 2) * 384, 128), 384)
        out_columns = pl.ds(pl.multiple_of((i // 2) * 768, 128), 768)
        put(sum_out, i, mul_tn(gate_normed[:, out_rows], cot[:, :, :, out_columns].reshape(1024, 768)))
        return carry

    def branch_rows(i, carry):
        rows = pl.ds(pl.multiple_of(i * 256, 256), 256)
        branch[i // 2, i % 2] = low(mul(gate_normed[rows, :], w_out[...].reshape(768, 1536)))
        return carry

    lax.fori_loop(0, 4, gate_weights, 0)
    act("g0")
    lax.fori_loop(0, 4, branch_rows, 0)
    act("b0")
    lax.fori_loop(0, 4, out_weights, 0)
    act("g0>")
    carried[...] = jnp.zeros((128, 768), jnp.float32)

    def scan(i, carry):
        act_at(i, SCAN_PLANS[0])
        backward_block(
            7 - i, vpad, spad, step_raw, seg, segc, taps, state_taps, heads, expand, gains[2:3, 0:768], states, dy,
            carried, du, dus, head_rows, value_low, state_low, step_low, acc_v, acc_s, acc_h,
            lambda: act_at(i, SCAN_PLANS[1]),
        )
        return carry

    lax.fori_loop(0, 8, scan, 0)
    act(*AFTER_SCAN)

    def value_weights(i, carry):
        put(sum_value, i, mul_tn(normed[:, pl.ds(pl.multiple_of(i * 384, 128), 384)], value_low[...]))
        act_at(i, VALUE_PLANS)
        return carry

    def state_weights(i, carry):
        thirds = [
            mul_tn(normed[:, pl.ds(pl.multiple_of(q * 512 + i * 128, 128), 128)], state_low[...]) for q in range(3)
        ]
        put(sum_state, i, jnp.concatenate(thirds, 1))
        return carry

    lax.fori_loop(0, 4, value_weights, 0)
    put_small(small, acc_v, acc_h, mul_tn(step_low[...], normed[...])[0:16, :])
    act("v0")
    lax.fori_loop(0, 4, state_weights, 0)
    act(*AFTER_STATE)

    def dx_rows(half, i):
        rows = pl.ds(pl.multiple_of(i * 256, 256), 256)
        columns = slice(half * 768, half * 768 + 768)
        part = mul_nt(gate_low[rows, :], w_gate[columns, :]) + mul_nt(value_low[rows, :], w_value[columns, :])
        part = part + mul_nt(state_low[rows, :], w_state[columns, :]) + mul(step_low[rows, :], w_step[:, columns])
        dx[i // 2, i % 2, :, columns] = low(part)
        acc_n[0:1, columns] += jnp.sum(part * normed[rows, columns].astype(jnp.float32), 0, keepdims=True)
        act_at(i, DX_PLANS[half])

    for half in range(2):

        def dx_half(i, carry):
            dx_rows(half, i)
            return carry

        lax.fori_loop(0, 4, dx_half, 0)
        act("de"[half] + "0")
    put_shared(shared, acc_s, acc_n[0:1, :] / gains[0:1, :])
    act("s0", *TAIL)
    if not remote:
        results = (res_gate, res_out, res_value, res_state, res_small, res_shared, res_branch, res_dx)
        copies = [
            pltpu.make_async_copy(src, dst, local.at[n])
            for n, (src, dst) in enumerate(zip((sum_gate, sum_out, sum_value, sum_state, small, shared, branch, dx), results))
        ]
        for cp in copies:
            cp.start()
        for cp in copies:
            cp.wait()


def layer(*operands, remote=True):
    f32, bf16 = jnp.float32, jnp.bfloat16
    weight, rows = (2, 4, 4, 96, 384), (2, 2, 256, 1536)
    outs = [weight, weight, weight, (2, 4, 4, 32, 384), (4, 4, 16, 128), (4, 4, 16, 128), rows, rows]
    scratch = [
        ((1024, 1536), bf16), ((1024, 768), bf16), ((1024, 768), bf16), ((1024, 768), bf16), ((1032, 768), f32),
        ((1032, 256), f32), ((1024, 256), bf16), ((1024, 128), bf16), ((1024, 128), f32),
        ((1040, 128), f32), ((8, 128, 768), bf16), ((128, 768), f32), ((136, 768), f32), ((136, 256), f32), ((128, 128), f32),
        ((8, 768), f32), ((8, 256), f32), ((8, 128), f32), ((8, 1536), f32), ((8, 768), f32), ((8, 256), f32),
        ((8, 128), f32), ((128, 768), bf16), ((8, 1536), f32),
        ((1536, 768), bf16), ((1536, 768), bf16), ((1536, 256), bf16), ((128, 1536), bf16), ((3, 256, 1536), bf16),
        (rows, bf16), ((8, 8, 128), f32), ((4, 8, 8, 128), f32),
    ] + [(shape, bf16) for shape in outs[:7]]
    vmem, hbm, smem = [pl.BlockSpec(memory_space=space) for space in (pltpu.VMEM, pl.ANY, pltpu.SMEM)]
    count = 8 * DP_SEMS + STATE_SEMS + 3 * TENSOR_SEMS + 3
    return pl.pallas_call(
        functools.partial(layer_kernel, remote),
        out_shape=[jax.ShapeDtypeStruct(shape, bf16) for shape in outs],
        in_specs=[hbm] * 6 + [vmem] * 8 + [smem] * 3,
        out_specs=[hbm] * 8,
        scratch_shapes=[pltpu.VMEM(shape, kind) for shape, kind in scratch]
        + dp_scratch(96, 384) * 4
        + dp_scratch(16, 128)
        + dp_scratch(16, 128, 16, True)
        + state_scratch(32, 384)
        + [pltpu.VMEM((2, 4, 96, 384), bf16)] * 2
        + [pltpu.VMEM((96, 384), bf16)] * 2
        + [pltpu.VMEM((2, 256, 1536), bf16), pltpu.VMEM((256, 1536), bf16)]
        + [pltpu.SemaphoreType.DMA((count,)), pltpu.SemaphoreType.DMA((count,)), pltpu.SemaphoreType.DMA((8,))],
        compiler_params=pltpu.CompilerParams(
            collective_id=0 if remote else None, has_side_effects=True, vmem_limit_bytes=63 * 2**20
        ),
        name="layer",
    )(*operands)


def finish_kernel(
    tokens_in, cot_in, norm_gain, gate_in, out_in, value_in, state_in, small, shared, branch_in, dx_in,
    mixed_out, tokens_out, gate_out, value_out, out_out, state_out, step, value_taps, value_bias, state_taps, state_bias, step_bias,
    log_rate, bypass, gain, mixer_gain,
    tokens, cot, branch, dx, sum_gate, sum_out, sum_value, sum_state, mixed, grad_tokens, gate, value, out, state, arrive, leave,
):
    quarters = [pl.ds(n * 256, 256) for n in range(4)]
    loads = []
    for n, (src, dst) in enumerate(((gate_in, sum_gate), (value_in, sum_value), (out_in, sum_out), (state_in, sum_state))):
        loads.append([pltpu.make_async_copy(src, dst, arrive.at[n])])
    for n, rows in enumerate(quarters):
        loads.append(
            [
                pltpu.make_async_copy(src.at[rows], dst.at[rows], arrive.at[4 + 4 * n + m])
                for m, (src, dst) in enumerate(((tokens_in, tokens), (dx_in, dx), (cot_in, cot), (branch_in, branch)))
            ]
        )
    for group in loads:
        for cp in group:
            cp.start()
    stores = []

    def store(src, dst):
        stores.append(pltpu.make_async_copy(src, dst, leave.at[len(stores)]))
        stores[-1].start()

    for n, (summed, result, home) in enumerate(
        ((sum_gate, gate, gate_out), (sum_value, value, value_out), (sum_out, out, out_out))
    ):
        loads[n][0].wait()
        for i in range(4):
            for stream in range(2):
                if n < 2:
                    rows, columns = pl.ds(i * 384, 384), pl.ds(stream * 384, 384)
                else:
                    rows, columns = pl.ds(i % 2 * 384, 384), pl.ds(i // 2 * 768 + stream * 384, 384)
                result[rows, columns] = summed[stream, i].astype(jnp.float32).reshape(384, 384)
            if n < 2:
                store(result.at[rows], home.at[rows])
            elif i > 1:
                store(result.at[rows], home.at[rows])
    blocks = [small[j // 4, j % 4].astype(jnp.float32) for j in range(12)]
    step[...] = jnp.concatenate([block[0:12] for block in blocks], 1)
    rows = [block[n : n + 1] for block in blocks for n in range(12, 16)]
    channels = [jnp.concatenate(rows[6 * n : 6 * n + 6], 1) for n in range(7)]
    value_taps[...] = jnp.concatenate(channels[0:4], 0)
    value_bias[...] = channels[4].reshape(768)
    mixer_gain[...] = channels[5].reshape(768)
    bypass[...] = mul_nt(low(jnp.broadcast_to(channels[6], (16, 768))), expansion())[0:1, 0:12].reshape(12)
    step_bias[...] = rows[42][:, 0:12].reshape(12)
    log_rate[...] = rows[43][:, 0:12].reshape(12)
    gains, convs = [shared[0, j].astype(jnp.float32) for j in range(2)]
    gain[...] = jnp.concatenate([gains[n : n + 1] for n in range(12)], 1).reshape(1536)
    taps = [jnp.concatenate([convs[2 * n : 2 * n + 1], convs[2 * n + 1 : 2 * n + 2]], 1) for n in range(5)]
    state_taps[...] = jnp.concatenate(taps[0:4], 0)
    state_bias[...] = taps[4].reshape(256)
    loads[3][0].wait()
    for i in range(4):
        rows = pl.ds(i * 128, 128)
        first, second = [sum_state[stream, i].astype(jnp.float32).reshape(128, 384) for stream in range(2)]
        state[0, rows, :] = first[:, 0:256]
        state[1, rows, 0:128] = first[:, 256:384]
        state[1, rows, 128:256] = second[:, 0:128]
        state[2, rows, :] = second[:, 128:384]
    store(state, state_out)
    for n, rows in enumerate(quarters):
        for cp in loads[4 + n]:
            cp.wait()
        hidden = tokens[rows, :].astype(jnp.float32)
        inverse = lax.rsqrt(jnp.sum(hidden * hidden, 1, keepdims=True) / 1536 + EPS)
        mixed[rows, :] = low(hidden + branch[rows, :].astype(jnp.float32))
        store(mixed.at[rows], mixed_out.at[rows])
        scaled = dx[rows, :].astype(jnp.float32) * norm_gain[...].reshape(1, 1536)
        along = jnp.sum(scaled * hidden, 1, keepdims=True) * (inverse * inverse * inverse / 1536)
        grad_tokens[rows, :] = cot[rows, :].astype(jnp.float32) + inverse * scaled - hidden * along
        store(grad_tokens.at[rows], tokens_out.at[rows])
    for cp in stores:
        cp.wait()


def finished(tokens, cot, norm_gain, *sums):
    f32, bf16 = jnp.float32, jnp.bfloat16
    large = [((1024, 1536), bf16), ((1024, 1536), f32), ((1536, 768), f32), ((1536, 768), f32), ((768, 1536), f32), ((3, 512, 256), f32)]
    rest = [((12, 1536), f32), ((4, 768), f32), ((768,), f32), ((4, 256), f32), ((256,), f32)] + [((12,), f32)] * 3
    rest += [((1536,), f32), ((768,), f32)]
    scratch = [((1024, 1536), bf16)] * 4 + [((2, 4, 4, 96, 384), bf16)] * 3 + [((2, 4, 4, 32, 384), bf16)] + large
    vmem, hbm = pl.BlockSpec(memory_space=pltpu.VMEM), pl.BlockSpec(memory_space=pl.ANY)
    return pl.pallas_call(
        finish_kernel,
        out_shape=[jax.ShapeDtypeStruct(shape, kind) for shape, kind in large + rest],
        in_specs=[hbm, hbm, vmem, hbm, hbm, hbm, hbm, vmem, vmem, hbm, hbm],
        out_specs=[hbm] * len(large) + [vmem] * len(rest),
        scratch_shapes=[pltpu.VMEM(shape, kind) for shape, kind in scratch]
        + [pltpu.SemaphoreType.DMA((20,)), pltpu.SemaphoreType.DMA((19,))],
        compiler_params=pltpu.CompilerParams(vmem_limit_bytes=60 * 2**20),
        name="finish",
    )(tokens, cot, norm_gain, *sums)


def local(
    tokens,
    segment,
    gate_proj,
    value_proj,
    state_proj,
    step_proj,
    value_conv,
    value_conv_bias,
    state_conv,
    state_conv_bias,
    step_bias,
    log_rate,
    bypass_gain,
    norm_gain,
    gated_norm_gain,
    out_proj,
    cotangent,
):
    *sums, branch, dx = layer(
        tokens, cotangent.reshape(2, 2, 256, 1536), gate_proj, value_proj, state_proj, out_proj.reshape(3, 256, 1536), segment, step_proj.T,
        value_conv, value_conv_bias, state_conv, state_conv_bias, norm_gain, gated_norm_gain, step_bias, log_rate, bypass_gain,
    )
    rows = tokens.shape
    (
        mixed_out, grad_tokens, grad_gate, grad_value, grad_out, grad_state, grad_step, grad_value_conv, grad_value_bias,
        grad_state_conv, grad_state_bias, grad_step_bias, grad_log_rate, grad_bypass, grad_gain, grad_mixer_gain,
    ) = finished(tokens, cotangent, norm_gain, *sums, branch.reshape(rows), dx.reshape(rows))
    return (
        mixed_out,
        grad_tokens,
        grad_gate,
        grad_value,
        grad_state.reshape(state_proj.shape),
        grad_step.T,
        grad_value_conv,
        grad_value_bias,
        grad_state_conv,
        grad_state_bias,
        grad_step_bias,
        grad_log_rate,
        grad_bypass,
        grad_gain,
        grad_mixer_gain,
        grad_out,
    )


def solution(mesh):
    placed = (
        P("dp", None),
        P("dp", None),
        P(None, "tensor"),
        P(None, "tensor"),
        P(),
        P(None, "tensor"),
        P(None, "tensor"),
        P("tensor"),
        P(),
        P(),
        P("tensor"),
        P("tensor"),
        P("tensor"),
        P(),
        P("tensor"),
        P("tensor", None),
        P("dp", None),
    )
    return jax.shard_map(
        local,
        mesh=mesh,
        in_specs=placed,
        out_specs=(
            P("dp", None),
            P("dp", None),
            P(None, "tensor"),
            P(None, "tensor"),
            P(),
            P(None, "tensor"),
            P(None, "tensor"),
            P("tensor"),
            P(),
            P(),
            P("tensor"),
            P("tensor"),
            P("tensor"),
            P(),
            P("tensor"),
            P("tensor", None),
        ),
        check_vma=False,
    )
```

```python
import functools

import jax
import jax.numpy as jnp
from jax import lax
from jax.experimental import pallas as pl
from jax.experimental.pallas import tpu as pltpu
from jax.sharding import PartitionSpec as P

EPS = 1e-05
MESH_ID = pl.DeviceIdType.MESH


def place():
    dp = lax.axis_index("dp")
    tensor = lax.axis_index("tensor")
    return {"x": dp // 8, "y": (dp // 4) % 2, "z": dp % 4, "t": tensor}


def device_at(at, **moved):
    spot = dict(at, **moved)
    return (spot["x"] * 8 + spot["y"] * 4 + spot["z"], spot["t"])


def dp_peers(at):
    return [
        device_at(at, x=(at["x"] + 1) % 4),
        device_at(at, x=(at["x"] + 3) % 4),
        device_at(at, z=(at["z"] + 1) % 4),
        device_at(at, z=(at["z"] + 3) % 4),
        device_at(at, y=1 - at["y"]),
    ]


def tensor_peers(at):
    return [device_at(at, t=(at["t"] + step) % 4) for step in (1, 2, 3)]


def greet(peers):
    barrier = pltpu.get_barrier_semaphore()
    for peer in peers:
        pl.semaphore_signal(barrier, inc=1, device_id=peer, device_id_type=MESH_ID)


def added(*refs):
    total = refs[0][...].astype(jnp.float32)
    for ref in refs[1:]:
        total = total + ref[...].astype(jnp.float32)
    return total.astype(jnp.bfloat16)


class Staged:
    def __init__(self, send, recv, first):
        self.send, self.recv, self.first = send, recv, first

    def made(self, stage):
        at = self.first + sum(self.counts[:stage])
        for n, (src, dst, peer) in enumerate(self.copies(stage)):
            if peer is None:
                yield pltpu.make_async_copy(src, dst, self.recv.at[at + n])
            else:
                yield pltpu.make_async_remote_copy(
                    src_ref=src,
                    dst_ref=dst,
                    send_sem=self.send.at[at + n],
                    recv_sem=self.recv.at[at + n],
                    device_id=peer,
                    device_id_type=MESH_ID,
                )

    def start(self, stage):
        for cp in self.made(stage):
            cp.start()

    def finish(self, stage):
        for cp in self.made(stage):
            cp.wait()
        self.settle(stage)


class SumOverDp(Staged):
    counts = (3, 2, 3, 1, 3, 4, 3, 2)

    def __init__(self, at, order, buf, res, scratch, sems, across=None, direct=False):
        super().__init__(*sems)
        self.at, self.buf, self.res, self.across, self.direct = at, buf, res, across, direct
        self.ta1, self.ta2, self.tb, self.ty, self.own, self.tt = scratch
        a_axis, b_axis = order
        self.a, self.b = at[a_axis], at[b_axis]
        self.a_up, self.a_down, self.a_far = [(self.a + n) % 4 for n in (1, 3, 2)]
        self.a_right, self.a_left = [device_at(at, **{a_axis: n}) for n in (self.a_up, self.a_down)]
        self.a_others = [(self.a + n) % 4 for n in (1, 2, 3)]
        self.a_peers = [device_at(at, **{a_axis: n}) for n in self.a_others]
        self.b_others = [(self.b + n) % 4 for n in (1, 2, 3)]
        self.b_peers = [device_at(at, **{b_axis: n}) for n in self.b_others]
        self.other = device_at(at, y=1 - at["y"])

    def copies(self, stage):
        buf, res, a, b, own = self.buf, self.res, self.a, self.b, self.own
        near, far = pl.ds(0, 2), pl.ds(2, 2)
        if stage == 0 and self.direct:
            return [(buf.at[i], self.ta1.at[n], peer) for n, (i, peer) in enumerate(zip(self.a_others, self.a_peers))]
        if stage == 6 and self.direct:
            return [(res.at[a], res.at[a], peer) for peer in self.a_peers]
        if stage == 0:
            return [(buf.at[self.a_far, near], self.ta1.at[0], self.a_right), (buf.at[self.a_far, far], self.ta1.at[1], self.a_left)]
        if stage == 1:
            return [(buf.at[self.a_up], self.ta2.at[0], self.a_right), (buf.at[self.a_down], self.ta2.at[1], self.a_left)]
        if stage == 2:
            return [(buf.at[a, j], self.tb.at[n], peer) for n, (j, peer) in enumerate(zip(self.b_others, self.b_peers))]
        if stage == 3:
            return [(buf.at[a, b], self.ty, self.other)]
        if stage == 4:
            return [(own.at[self.across], self.tt.at[self.at["t"]], peer) for peer in tensor_peers(self.at)]
        if stage == 5:
            home = res.at[a, b]
            return [(own, home, peer) for peer in self.b_peers] + [(own, home, None)]
        if stage == 6:
            return [(res.at[a], res.at[a], self.a_right), (res.at[a], res.at[a], self.a_left)]
        return [
            (res.at[self.a_down, near], res.at[self.a_down, near], self.a_right),
            (res.at[self.a_up, far], res.at[self.a_up, far], self.a_left),
        ]

    def settle(self, stage):
        buf, a, b, own = self.buf, self.a, self.b, self.own
        if stage == 0 and self.direct:
            for j in range(4):
                buf[a, j] = added(buf.at[a, j], *(self.ta1.at[n, j] for n in range(3)))
        elif stage == 0:
            for j in range(2):
                buf[self.a_up, j] = added(buf.at[self.a_up, j], self.ta1.at[0, j])
                buf[self.a_down, 2 + j] = added(buf.at[self.a_down, 2 + j], self.ta1.at[1, j])
        elif stage == 1:
            for j in range(4):
                buf[a, j] = added(buf.at[a, j], self.ta2.at[0, j], self.ta2.at[1, j])
        elif stage == 2:
            buf[a, b] = added(buf.at[a, b], *(self.tb.at[n] for n in range(3)))
        elif stage == 3:
            own[...] = added(buf.at[a, b], self.ty)
        elif stage == 4:
            self.tt[self.at["t"]] = own[self.across]
            own[self.across] = added(*(self.tt.at[n] for n in range(4)))


DP_SEMS = sum(SumOverDp.counts)


def dp_scratch(rows, width, across=16, direct=False):
    first = [(3, 4, rows, width), (1, 16, width)] if direct else [(2, 2, rows, width), (2, 4, rows, width)]
    shapes = first + [(3, rows, width), (rows, width), (rows, width), (4, across, width)]
    return [pltpu.VMEM(shape, jnp.bfloat16) for shape in shapes]


class SumOverTensor(Staged):
    counts = (1, 1, 2, 1)

    def __init__(self, at, rows, buf, res, scratch, sems, ending):
        super().__init__(*sems)
        self.buf, self.res, self.rows, self.ending = buf, res, rows, ending
        self.t0, self.t1 = scratch
        self.c, self.h = at["t"] % 2, at["t"] // 2
        self.sibling = device_at(at, t=self.h * 2 + 1 - self.c)
        self.partner = device_at(at, t=(1 - self.h) * 2 + self.c)

    def copies(self, stage):
        buf, res, c, h, rows = self.buf, self.res, self.c, self.h, self.rows
        if stage == 0:
            return [(buf.at[1 - c, :, rows], self.t0.at[:, rows], self.sibling)]
        if stage == 1:
            return [(buf.at[c, 1 - h, rows], self.t1.at[rows], self.partner)]
        if stage == 2:
            mine, theirs = buf.at[c, h, rows], res.at[c, h, rows]
            return [(mine, theirs, self.partner), (mine, theirs, None)]
        return [(res.at[c, :, rows], res.at[c, :, rows], self.sibling)]

    def settle(self, stage):
        buf, c, h, rows = self.buf, self.c, self.h, self.rows
        if stage == 0:
            for n in range(2):
                buf[c, n, rows] = added(buf.at[c, n, rows], self.t0.at[n, rows])
        elif stage == 1:
            total = buf[c, h, rows].astype(jnp.float32) + self.t1[rows].astype(jnp.float32)
            buf[c, h, rows] = self.ending(total, rows)


TENSOR_SEMS = sum(SumOverTensor.counts)


class SumState(Staged):
    counts = (1, 3, 3, 1, 1, 4, 3, 1)

    def __init__(self, at, buf, res, scratch, sems):
        super().__init__(*sems)
        self.buf, self.res = buf, res
        self.t0, self.ta, self.tb, self.ty, self.tt, self.own = scratch
        x, y, z, t = at["x"], at["y"], at["z"], at["t"]
        c = t % 2
        self.c, self.a, self.b = c, x * (1 - c) + z * c, z * (1 - c) + x * c
        self.sibling = device_at(at, t=t // 2 * 2 + 1 - c)
        self.partner = device_at(at, t=(1 - t // 2) * 2 + c)
        self.other = device_at(at, y=1 - y)
        self.a_peers = [device_at(at, x=(x + n * (1 - c)) % 4, z=(z + n * c) % 4) for n in (1, 2, 3)]
        self.b_peers = [device_at(at, x=(x + n * c) % 4, z=(z + n * (1 - c)) % 4) for n in (1, 2, 3)]

    def copies(self, stage):
        buf, res, a, b, c, own = self.buf, self.res, self.a, self.b, self.c, self.own
        if stage == 0:
            return [(buf.at[1 - c], self.t0, self.sibling)]
        if stage == 1:
            return [(buf.at[c, (a + n + 1) % 4], self.ta.at[n], peer) for n, peer in enumerate(self.a_peers)]
        if stage == 2:
            return [(buf.at[c, a, (b + n + 1) % 4], self.tb.at[n], peer) for n, peer in enumerate(self.b_peers)]
        if stage == 3:
            return [(buf.at[c, a, b], self.ty, self.other)]
        if stage == 4:
            return [(own, self.tt, self.partner)]
        if stage == 5:
            return [(own, res.at[c, a, b], peer) for peer in self.b_peers] + [(own, res.at[c, a, b], None)]
        if stage == 6:
            return [(res.at[c, a], res.at[c, a], peer) for peer in self.a_peers]
        return [(res.at[c], res.at[c], self.sibling)]

    def settle(self, stage):
        buf, a, b, c = self.buf, self.a, self.b, self.c
        if stage == 0:
            for i in range(4):
                for j in range(4):
                    buf[c, i, j] = added(buf.at[c, i, j], self.t0.at[i, j])
        elif stage == 1:
            for j in range(4):
                buf[c, a, j] = added(buf.at[c, a, j], *(self.ta.at[n, j] for n in range(3)))
        elif stage == 2:
            buf[c, a, b] = added(buf.at[c, a, b], *(self.tb.at[n] for n in range(3)))
        elif stage == 3:
            self.own[...] = added(buf.at[c, a, b], self.ty)
        elif stage == 4:
            self.own[...] = added(self.own, self.tt)


STATE_SEMS = sum(SumState.counts)


def state_scratch(rows, width):
    block = (rows, width)
    shapes = [(4, 4) + block, (3, 4) + block, (3,) + block, block, block, block]
    return [pltpu.VMEM(shape, jnp.bfloat16) for shape in shapes]


def wide(tile, count=6):
    return jnp.concatenate([tile] * count, axis=1)


def mul(left, right):
    return jnp.dot(left, right, preferred_element_type=jnp.float32)


def mul_nt(left, right):
    return lax.dot_general(left, right, (((1,), (1,)), ((), ())), preferred_element_type=jnp.float32)


def mul_tn(left, right):
    return lax.dot_general(left, right, (((0,), (0,)), ((), ())), preferred_element_type=jnp.float32)


def low(value):
    return value.astype(jnp.bfloat16)


def iota(shape, dim):
    return lax.broadcasted_iota(jnp.int32, shape, dim)


def in_three(value):
    high = low(value).astype(jnp.float32)
    rest = value - high
    middle = low(rest).astype(jnp.float32)
    lane = iota(value.shape, 1)
    return low(jnp.where(lane < 16, high, jnp.where(lane < 32, middle, rest - middle)))


def exact_sum(ones, value):
    high = low(value)
    rest = value - high.astype(jnp.float32)
    middle = low(rest)
    return mul(ones, high) + mul(ones, middle) + mul(ones, low(rest - middle.astype(jnp.float32)))


def softplus(value):
    return jnp.maximum(value, 0.0) + jnp.log1p(jnp.exp(-jnp.abs(value)))


def sigmoid(value):
    return 1.0 / (1.0 + jnp.exp(-value))


def columns_of_segments(seg_ref, segc):
    segc[0:8, :] = jnp.full((8, 128), -1.0, jnp.float32)
    segc[1032:1040, :] = jnp.full((8, 128), -1.0, jnp.float32)

    def fill(k, carry):
        row = jnp.broadcast_to(seg_ref[:, pl.ds(pl.multiple_of(k * 128, 128), 128)].astype(jnp.float32), (128, 128))
        segc[pl.ds(pl.multiple_of(8 + k * 128, 8), 128), :] = row.T
        return carry

    lax.fori_loop(0, 8, fill, 0)


def kept(segc, start):
    around = segc[pl.ds(start, 144), :]
    here = around[8:, :]
    return [(pltpu.roll(around, lag, 0)[8:, :] == here).astype(jnp.float32) for lag in (1, 2, 3)]


def lagged(padded, start, keeps):
    around = padded[pl.ds(start, 136), :]
    count = around.shape[1] // 128
    return [around[8:, :]] + [pltpu.roll(around, lag, 0)[8:, :] * wide(keep[:128], count) for lag, keep in zip((1, 2, 3), keeps)]


def convolved(shifted, taps):
    total = taps[4:5, :] + taps[0:1, :] * shifted[0]
    for lag in (1, 2, 3):
        total = total + taps[lag : lag + 1, :] * shifted[lag]
    return total


def decay(k, start, segc, seg_ref, step_raw, heads):
    rows = pl.ds(start, 128)
    step = softplus(step_raw[rows, :] + heads[0:1, :])
    tri = (iota((128, 128), 0) >= iota((128, 128), 1)).astype(jnp.bfloat16)
    cum = exact_sum(tri, step * heads[1:2, :])
    seg_column = segc[pl.ds(start + 8, 128), :]
    seg_row = seg_ref[:, rows].astype(jnp.float32)
    before = segc[pl.ds(start, 8), :][7:8, :]
    last = seg_column[127:128, :]
    growth = jnp.exp(cum)
    tail = jnp.exp(cum[127:128, :] - cum) * (seg_column == last).astype(jnp.float32)
    return step, cum, seg_column, seg_row, before, last, growth, tail


def expansion():
    row, column = iota((128, 768), 0), iota((128, 768), 1)
    return ((row < 48) & (row % 16 == column // 64)).astype(jnp.bfloat16)


def head_sums(value, expand):
    return mul_nt(low(value), expand)


def slope(pre, sig):
    return sig * (1.0 + pre * (1.0 - sig))


def middle_block(k, total, kept_act, bent, gated_ref, pulled, acc_v):
    rows = pl.ds(pl.multiple_of(k * 128, 128), 128)
    columns = jnp.concatenate([total] * 16, 0).T
    scale = lax.rsqrt(columns[:, 0:1] / 3072 + EPS)
    pull = columns[:, 1:2] * scale * scale * scale / 3072
    gated, q, act, bend = [
        value.astype(jnp.float32) for value in (gated_ref[rows, :], pulled[rows, :], kept_act[...], bent[rows, :])
    ]
    scaled = gated * scale
    acc_v[5:6, :] += jnp.sum(q * scaled, 0, keepdims=True)
    grad_gated = scale * q - gated * pull
    pulled[rows, :] = low(grad_gated * act)
    bent[rows, :] = low(grad_gated * bend)
    return rows, scaled


def put(buf, i, value):
    pieces = low(value.reshape(4, value.shape[0] // 4, 768))
    for stream in range(2):
        buf[stream, i] = pieces[..., stream * 384 : (stream + 1) * 384]


def backward_block(
    k, vpad, spad, step_raw, seg_ref, segc, taps, state_taps, heads, expand, bypass, states, dy,
    dstate, du, dus, head_rows, value_low, state_low, step_low, acc_v, acc_s, acc_h, between,
):
    start = pl.multiple_of(k * 128, 128)
    rows = pl.ds(start, 128)
    keeps = kept(segc, start)
    values = lagged(vpad, start, keeps)
    pre = convolved(values, taps)
    sig = sigmoid(pre)
    x = pre * sig
    state_values = lagged(spad, start, keeps)
    state_pre = convolved(state_values, state_taps)
    state_sig = sigmoid(state_pre)
    state = low(state_pre * state_sig)
    b_in, c_out = state[:, :128], state[:, 128:]
    step, cum, seg_column, seg_row, before, last, growth, tail = decay(k, start, segc, seg_ref, step_raw, heads)
    spread = mul(jnp.concatenate([in_three(step), in_three(growth), in_three(tail)], 0), expand[...])
    step_wide, tail_wide = spread[:128], spread[256:]
    growth_wide = spread[128:256] * wide((seg_column == before).astype(jnp.float32))
    through = spread[255:256] * wide((last == before).astype(jnp.float32))
    xs = x * step_wide
    entering = states[k]
    grad_state = dstate[...]
    grad_state_low = low(grad_state)
    dyk = dy[rows, :].astype(jnp.float32)
    grown = low(dyk * growth_wide)
    outside = mul(c_out, entering) * growth_wide
    dxs_after = mul(b_in, grad_state_low) * tail_wide
    grad_c = mul_nt(grown, entering)
    grad_b = mul_nt(low(xs * tail_wide), grad_state_low)
    end = jnp.sum(entering.astype(jnp.float32) * grad_state, 0, keepdims=True) * through
    dstate[...] = through * grad_state + mul_tn(c_out, grown)
    scores = mul_nt(b_in, c_out)
    row, column = iota((128, 128), 0), iota((128, 128), 1)
    bias = jnp.where((seg_column == seg_row) & (row <= column), 0.0, -1e30)
    tri = (row >= column).astype(jnp.bfloat16)
    strict = row < column
    cum_rows = cum.T
    first = column < 64
    grad_scores = jnp.zeros((128, 128), jnp.float32)
    own_steps = jnp.zeros((128, 128), jnp.float32)
    inside = []
    between(1)
    for pair in range(6):
        lanes = slice(pair * 128, (pair + 1) * 128)
        own = dyk[:, lanes]
        both = low(jnp.concatenate([jnp.where(first, own, 0.0), jnp.where(first, 0.0, own)], 0))
        grad_weights = mul_nt(low(x[:, lanes]), both)
        weights, moved, steps = [], [], []
        for side in range(2):
            h = 2 * pair + side
            faded = jnp.exp(cum_rows[h : h + 1, :] - cum[:, h : h + 1] + bias)
            pulled = grad_weights[:, side * 128 : (side + 1) * 128] * faded
            steps.append(step[:, h : h + 1])
            grad_scores = grad_scores + pulled * steps[side]
            moved.append(low(pulled * scores))
            weights.append(low(scores * faded))
        inside.append(mul(jnp.concatenate(weights, 1), both))
        later = mul(jnp.concatenate(moved, 0), tri)
        for side in range(2):
            h = 2 * pair + side
            part = later[side * 128 : (side + 1) * 128]
            own_steps = jnp.where(column == h, part[:, 0:1], own_steps)
            head_rows[h : h + 1, :] = jnp.sum(jnp.where(strict, part * steps[side], 0.0), 0, keepdims=True)
    between(2)
    grad_scores = low(grad_scores)
    grad_b = grad_b + mul(grad_scores, c_out)
    grad_c = grad_c + mul_tn(grad_scores, b_in)
    dxs = jnp.concatenate(inside, 1) + dxs_after
    dx = dxs * step_wide + bypass * dyk
    summed = head_sums(jnp.concatenate([dyk * outside, x * dxs_after], 0), expand[...])
    end = head_sums(jnp.broadcast_to(end, (16, 768)), expand[...])
    upper = (row <= column).astype(jnp.bfloat16)
    below = (row > column).astype(jnp.bfloat16)
    grad_decay = exact_sum(upper, summed[:128]) + exact_sum(below, step * summed[128:]) + end[0:1, :] + head_rows[...].T
    grad_step = own_steps + summed[128:] + heads[1:2, :] * grad_decay
    grad_raw = grad_step * sigmoid(step_raw[rows, :] + heads[0:1, :])
    step_low[rows, :] = low(jnp.where(column < 16, grad_raw, 0.0))
    acc_h[0:1, :] += jnp.sum(grad_raw, 0, keepdims=True)
    acc_h[1:2, :] += jnp.sum(step * grad_decay, 0, keepdims=True) * heads[1:2, :]
    between(3)
    for grad, grads, shifted, taps_ref, acc, result in (
        (dx * slope(pre, sig), du, values, taps, acc_v, value_low),
        (jnp.concatenate([grad_b, grad_c], 1) * slope(state_pre, state_sig), dus, state_values, state_taps, acc_s, state_low),
    ):
        grads[128:136, :] = grads[0:8, :]
        grads[0:128, :] = grad
        for lag in range(4):
            acc[lag : lag + 1, :] += jnp.sum(grad * shifted[lag], 0, keepdims=True)
        acc[4:5, :] += jnp.sum(grad, 0, keepdims=True)
        around = grads[...]
        count = around.shape[1] // 128
        total = grad * taps_ref[0:1, :]
        for lag, keep in zip((1, 2, 3), keeps):
            total = total + taps_ref[lag : lag + 1, :] * pltpu.roll(around * wide(keep, count), 136 - lag, 0)[:128, :]
        result[rows, :] = low(total)
    acc_v[6:7, :] += jnp.sum(dyk * x, 0, keepdims=True)


def put_small(small, acc_v, acc_h, step_grad):
    small[...] = jnp.zeros_like(small)
    rows = [acc_v[n : n + 1, j * 128 : (j + 1) * 128] for n in range(7) for j in range(6)] + [acc_h[0:1, :], acc_h[1:2, :]]
    place_in = iota((16, 128), 0)
    for j in range(12):
        block = jnp.where(place_in < 12, step_grad[:, j * 128 : (j + 1) * 128], 0.0)
        for n, row in enumerate(rows[4 * j : 4 * j + 4]):
            block = jnp.where(place_in == 12 + n, row, block)
        small[j // 4, j % 4] = low(block)


def put_shared(shared, acc_s, acc_n):
    shared[...] = jnp.zeros_like(shared)
    place_in = iota((16, 128), 0)
    for j, rows in enumerate(
        (
            [acc_n[:, n * 128 : (n + 1) * 128] for n in range(12)],
            [acc_s[n : n + 1, j * 128 : (j + 1) * 128] for n in range(5) for j in range(2)],
        )
    ):
        block = jnp.zeros((16, 128), jnp.float32)
        for n, row in enumerate(rows):
            block = jnp.where(place_in == n, row, block)
        shared[0, j] = low(block)


BRANCH_PLANS = {}
OUT_PLANS = {3: ("g0>",)}
VALUE_PLANS = {}
STATE_PLANS = {3: ("o1>",)}
SCAN_PLANS = (
    {4: ("g2>",), 6: ("o0>", "b1>"), 7: ("g4>",)},
    {},
    {0: ("b0>",), 2: ("g1>",), 4: ("o0",), 5: ("g3>",)},
    {},
)
DX_PLANS = ({3: ("g5>", "b2>")}, {0: ("v0>",), 1: ("o2>",), 3: ("d0>", "g6.", "o3>", "b3.")})
TAIL = (
    "v1>", "e0>", "s0>", "o4>", "d1>", "v2>", "s1>", "s2>", "o5>", "v3>", "s3>", "e1>",
    "s4>", "o6.", "v4>", "d2>", "s5>", "d3.", "e2>", "s6>", "e3.", "v5>", "s7.", "v6.",
)
RING = (0, 1, 2, 3, 5, 6, 7)


def head_row(values, lane, group):
    row = jnp.zeros(lane.shape, jnp.float32)
    for h in range(12):
        row = jnp.where(group(lane, h), values[h], row)
    return row


def layer_kernel(
    remote,
    tokens, cot_in, w_gate_in, w_value_in, w_state_in, w_out_in,
    seg, w_step_in, value_conv, value_bias, state_conv, state_bias, norm_gain, gated_gain, step_bias, log_rate, bypass_gain,
    res_gate, res_out, res_value, res_state, res_small, res_shared, res_branch, res_dx,
    normed, gate, y_ref, q_ref, vpad, spad, state_low, step_low, step_raw, segc, states, carried, du, dus, head_rows,
    acc_v, acc_s, acc_h, acc_n, taps, state_taps, heads, expand, gains,
    w_gate, w_value, w_state, w_step, w_out, cot, sums, landed,
    sum_gate, sum_out, sum_value, sum_state, small, shared, branch,
    *rest,
):
    scratch = [rest[n * 6 : (n + 1) * 6] for n in range(7)]
    value_scratch = [
        (early[0], own_ta2, early[2], own_ty, *early[4:])
        for early, own_ta2, own_ty in zip(scratch[0:2], rest[42:44], rest[44:46])
    ]
    branch_scratch = rest[46:48]
    own_tokens, own_cot, send, recv, local = rest[48:]
    at = place()
    dx = cot
    slots = branch.at[0]

    def fetch(k):
        return pltpu.make_async_copy(tokens.at[pl.ds(pl.multiple_of(k * 256, 256), 256)], slots.at[k % 2], local.at[k % 2])

    loads = [
        pltpu.make_async_copy(src, dst, local.at[2 + n])
        for n, (src, dst) in enumerate(
            (
                (w_gate_in, w_gate),
                (w_value_in, w_value),
                (w_state_in, w_state),
                (cot_in, cot),
                (w_out_in, w_out),
                (tokens.at[pl.ds(pl.multiple_of((at["t"] % 2 * 2 + at["t"] // 2) * 256, 256), 256)], own_tokens),
                (cot_in.at[at["t"] % 2, at["t"] // 2], own_cot),
            )
        )
    ]
    fetch(0).start()
    for cp in loads[:3]:
        cp.start()
    friends = dp_peers(at) + tensor_peers(at)
    if remote:
        greet(friends)

    orders = (("x", "z"), ("z", "x"))

    def pair(first, buf, res, scratch):
        return [
            (SumOverDp(at, order, buf.at[n], res.at[n], scratch[n], (send, recv, (first + n) * DP_SEMS)), RING)
            for n, order in enumerate(orders)
        ]

    last = 8 * DP_SEMS + STATE_SEMS
    dx_scratch = (w_out.at[pl.ds(0, 2)], w_out.at[2])
    upper, lower, all_rows = pl.ds(0, 128), pl.ds(128, 128), pl.ds(0, 256)

    def mixed_rows(total, rows):
        return low(own_tokens[rows].astype(jnp.float32) + total)

    def token_gradient(total, rows):
        hidden = own_tokens[rows].astype(jnp.float32)
        inverse = lax.rsqrt(jnp.sum(hidden * hidden, 1, keepdims=True) / 1536 + EPS)
        scaled = total * gains[0:1, :]
        along = jnp.sum(scaled * hidden, 1, keepdims=True) * (inverse * inverse * inverse / 1536)
        return low(own_cot[rows].astype(jnp.float32) + inverse * scaled - hidden * along)

    def over_tensor(n, rows, buf, res, scratch, ending):
        return [(SumOverTensor(at, rows, buf, res, scratch, (send, recv, last + n * TENSOR_SEMS), ending), range(4))]

    engines = {
        "g": pair(0, sum_gate, res_gate, scratch[0:2]),
        "o": pair(2, sum_out, res_out, scratch[2:4]),
        "v": pair(4, sum_value, res_value, value_scratch)
        + [(SumOverDp(at, orders[0], small, res_small, scratch[4], (send, recv, 6 * DP_SEMS)), RING)],
        "s": [
            (SumState(at, sum_state, res_state, scratch[6], (send, recv, 8 * DP_SEMS)), range(8)),
            (
                SumOverDp(at, orders[0], shared, res_shared, scratch[5], (send, recv, 7 * DP_SEMS), pl.ds(0, 16), True),
                (None, 0, 2, 3, 4, 5, 6, None),
            ),
        ],
        "b": over_tensor(0, all_rows, branch, res_branch, branch_scratch, mixed_rows),
        "d": over_tensor(1, upper, dx, res_dx, dx_scratch, token_gradient),
        "e": over_tensor(2, lower, dx, res_dx, dx_scratch, token_gradient),
    }

    def act(*plan):
        if not remote:
            return
        for word in plan:
            step = int(word[1])
            if word[2:]:
                for engine, stages in engines[word[0]]:
                    if stages[step] is not None:
                        engine.finish(stages[step])
                step += 1
            if word[2:] != ".":
                for engine, stages in engines[word[0]]:
                    if stages[step] is not None:
                        engine.start(stages[step])

    def act_at(i, plans):
        for n, plan in plans.items():

            @pl.when(i == n)
            def _():
                act(*plan)

    for ref in (du, dus, head_rows, carried, acc_v, acc_s, acc_h, acc_n, taps, state_taps, gains):
        ref[...] = jnp.zeros_like(ref)
    vpad[0:8, :] = jnp.zeros((8, 768), jnp.float32)
    spad[0:8, :] = jnp.zeros((8, 256), jnp.float32)
    columns_of_segments(seg, segc)
    taps[0:4, :] = value_conv[...]
    taps[4:5, :] = value_bias[...].reshape(1, 768)
    state_taps[0:4, :] = state_conv[...]
    state_taps[4:5, :] = state_bias[...].reshape(1, 256)
    lane = iota((8, 128), 1)
    heads[...] = head_row(step_bias, lane, lambda l, h: (l % 16 == h) & (l < 48))
    rate = head_row(log_rate, lane, lambda l, h: (l % 16 == h) & (l < 48))
    heads[1:2, :] = jnp.where((lane % 16 < 12) & (lane < 48), -jnp.exp(rate), 0.0)[0:1]
    gains[0:1, :] = norm_gain[...].reshape(1, 1536)
    gains[1:2, 0:768] = gated_gain[...].reshape(1, 768)
    gains[2:3, 0:768] = head_row(bypass_gain, iota((1, 768), 1), lambda l, h: l // 64 == h)
    expand[...] = expansion()
    chosen = ((iota((12, 128), 1) % 16 == iota((12, 128), 0)) & (iota((12, 128), 1) < 48)).astype(jnp.bfloat16)
    w_step[...] = low(mul_tn(chosen, w_step_in[...]))
    for cp in loads[:3]:
        cp.wait()
    for cp in loads[3:]:
        cp.start()

    def project(k, carry):
        rows = pl.ds(pl.multiple_of(k * 256, 256), 256)
        padded = pl.ds(pl.multiple_of(8 + k * 256, 8), 256)

        @pl.when(k < 3)
        def _():
            fetch(k + 1).start()

        fetch(k).wait()
        hidden = slots[k % 2].astype(jnp.float32)
        inverse = lax.rsqrt(jnp.sum(hidden * hidden, 1, keepdims=True) / 1536 + EPS)
        normal = low(hidden * inverse * gains[0:1, :])
        normed[rows, :] = normal
        gate[rows, :] = low(mul(normal, w_gate[...]))
        vpad[padded, :] = mul(normal, w_value[...])
        spad[padded, :] = mul(normal, w_state[...])
        step_raw[rows, :] = mul_nt(normal, w_step[...])
        return carry

    lax.fori_loop(0, 4, project, 0)
    for cp in loads[3:]:
        cp.wait()

    def project_back(k, carry):
        rows = pl.ds(pl.multiple_of(k * 256, 256), 256)
        q_ref[rows, :] = low(mul_nt(cot[k // 2, k % 2], w_out[...].reshape(768, 1536)) * gains[1:2, 0:768])
        return carry

    lax.fori_loop(0, 4, project_back, 0)

    def act_of(k):
        rows, columns = pl.ds(k // 2 % 2 * 128, 128), pl.ds(pl.multiple_of(k % 2 * 768, 128), 768)
        return branch.at[1, k // 4, rows, columns]

    def forward_block(k, carry):
        start = pl.multiple_of(k * 128, 128)
        rows = pl.ds(start, 128)
        keeps = kept(segc, start)
        pre = convolved(lagged(vpad, start, keeps), taps)
        x = pre * sigmoid(pre)
        pre = convolved(lagged(spad, start, keeps), state_taps)
        state = low(pre * sigmoid(pre))
        b_in, c_out = state[:, :128], state[:, 128:]
        step, cum, seg_column, seg_row, before, last, growth, tail = decay(k, start, segc, seg, step_raw, heads)
        spread = mul(jnp.concatenate([in_three(step), in_three(growth), in_three(tail)], 0), expand[...])
        xs = x * spread[:128]
        start_keep = (seg_column == before).astype(jnp.float32)
        entering = carried[...]
        states[k] = low(entering)
        outside = mul(c_out, low(entering)) * (spread[128:256] * wide(start_keep))
        through = spread[255:256] * wide((last == before).astype(jnp.float32))
        carried[...] = through * entering + mul_tn(b_in, low(xs * spread[256:]))
        scores = mul_nt(c_out, b_in)
        bias = jnp.where((seg_column == seg_row) & (iota((128, 128), 0) >= iota((128, 128), 1)), 0.0, -1e30)
        cum_rows = cum.T
        first = iota((128, 128), 1) < 64
        inside = []
        for pair in range(6):
            own = xs[:, pair * 128 : (pair + 1) * 128]
            right = low(jnp.concatenate([jnp.where(first, own, 0.0), jnp.where(first, 0.0, own)], 0))
            left = [
                low(scores * jnp.exp(cum[:, h : h + 1] - cum_rows[h : h + 1, :] + bias)) for h in (2 * pair, 2 * pair + 1)
            ]
            inside.append(mul(jnp.concatenate(left, 1), right))
        y = jnp.concatenate(inside, 1) + outside + gains[2:3, 0:768] * x
        raw = gate[rows, :].astype(jnp.float32)
        sig = sigmoid(raw)
        act = raw * sig
        gated = y * act
        y_ref[rows, :] = low(gated)
        gate[rows, :] = low(y * slope(raw, sig))
        act_of(k)[...] = low(act)
        squares = jnp.sum(gated * gated, 1, keepdims=True)
        cross = jnp.sum(q_ref[rows, :].astype(jnp.float32) * gated, 1, keepdims=True)
        lanes = iota((128, 128), 1)
        sums[k] = jnp.where(lanes == 0, squares, jnp.where(lanes == 1, cross, 0.0)).T[0:8, :]
        return carry

    def exchange(half):
        blocks, first = pl.ds(4 * half, 4), last + 3 * TENSOR_SEMS + 3 * half
        copies = [
            pltpu.make_async_remote_copy(
                src_ref=sums.at[blocks],
                dst_ref=landed.at[at["t"], blocks],
                send_sem=send.at[first + n],
                recv_sem=recv.at[first + n],
                device_id=peer,
                device_id_type=MESH_ID,
            )
            for n, peer in enumerate(tensor_peers(at))
        ]
        if not remote:
            for n in range(4):
                landed[n, blocks] = sums[blocks] * 0.75
            return []
        for cp in copies:
            cp.start()
        landed[at["t"], blocks] = sums[blocks]
        return copies

    def middle(k, carry):
        total = (landed[0, k] + landed[1, k]) + (landed[2, k] + landed[3, k])
        rows, scaled = middle_block(k, total, act_of(k), gate, y_ref, q_ref, acc_v)
        y_ref[rows, :] = low(scaled * gains[1:2, 0:768])
        return carry

    lax.fori_loop(0, 4, forward_block, 0)
    if remote:
        pl.semaphore_wait(pltpu.get_barrier_semaphore(), len(friends))
    first_sums = exchange(0)
    lax.fori_loop(4, 8, forward_block, 0)
    second_sums = exchange(1)
    for cp in first_sums:
        cp.wait()
    lax.fori_loop(0, 4, middle, 0)
    for cp in second_sums:
        cp.wait()
    lax.fori_loop(4, 8, middle, 0)
    acc_v[5:6, :] = acc_v[5:6, :] / gains[1:2, 0:768]
    gate_low, gate_normed, dy = gate, y_ref, q_ref
    value_low = y_ref

    def gate_weights(i, carry):
        put(sum_gate, i, mul_tn(normed[:, pl.ds(pl.multiple_of(i * 384, 128), 384)], gate_low[...]))
        return carry

    def out_weights(i, carry):
        out_rows = pl.ds(pl.multiple_of((i % 2) * 384, 128), 384)
        out_columns = pl.ds(pl.multiple_of((i // 2) * 768, 128), 768)
        put(sum_out, i, mul_tn(gate_normed[:, out_rows], cot[:, :, :, out_columns].reshape(1024, 768)))
        act_at(i, OUT_PLANS)
        return carry

    def branch_rows(i, carry):
        rows = pl.ds(pl.multiple_of(i * 256, 256), 256)
        branch[i // 2, i % 2] = low(mul(gate_normed[rows, :], w_out[...].reshape(768, 1536)))
        act_at(i, BRANCH_PLANS)
        return carry

    lax.fori_loop(0, 4, gate_weights, 0)
    act("g0")
    lax.fori_loop(0, 4, branch_rows, 0)
    act("b0")
    lax.fori_loop(0, 4, out_weights, 0)
    carried[...] = jnp.zeros((128, 768), jnp.float32)

    def scan(i, carry):
        act_at(i, SCAN_PLANS[0])
        backward_block(
            7 - i, vpad, spad, step_raw, seg, segc, taps, state_taps, heads, expand, gains[2:3, 0:768], states, dy,
            carried, du, dus, head_rows, value_low, state_low, step_low, acc_v, acc_s, acc_h,
            lambda point: act_at(i, SCAN_PLANS[point]),
        )
        return carry

    lax.fori_loop(0, 8, scan, 0)

    def value_weights(i, carry):
        put(sum_value, i, mul_tn(normed[:, pl.ds(pl.multiple_of(i * 384, 128), 384)], value_low[...]))
        act_at(i, VALUE_PLANS)
        return carry

    def state_weights(i, carry):
        thirds = [
            mul_tn(normed[:, pl.ds(pl.multiple_of(q * 512 + i * 128, 128), 128)], state_low[...]) for q in range(3)
        ]
        put(sum_state, i, jnp.concatenate(thirds, 1))
        act_at(i, STATE_PLANS)
        return carry

    lax.fori_loop(0, 4, value_weights, 0)
    put_small(small, acc_v, acc_h, mul_tn(step_low[...], normed[...])[0:16, :])
    act("v0")
    lax.fori_loop(0, 4, state_weights, 0)

    def dx_rows(half, i):
        firsts = [pl.ds(pl.multiple_of((i // 2 * 2 + n) * 256 + half * 128, 128), 128) for n in range(2)]
        columns = pl.ds(pl.multiple_of(i % 2 * 768, 128), 768)

        def both(ref, *lanes):
            return jnp.concatenate([ref[(rows, *lanes)] for rows in firsts], 0)

        part = mul_nt(both(gate_low), w_gate[columns, :]) + mul_nt(both(value_low), w_value[columns, :])
        part = part + mul_nt(both(state_low), w_state[columns, :]) + mul(both(step_low), w_step[:, columns])
        for n in range(2):
            dx[i // 2, n, half * 128 : half * 128 + 128, columns] = low(part[n * 128 : n * 128 + 128])
        acc_n[0:1, columns] += jnp.sum(part * both(normed, columns).astype(jnp.float32), 0, keepdims=True)
        act_at(i, DX_PLANS[half])

    for half in range(2):

        def dx_half(i, carry):
            dx_rows(half, i)
            return carry

        lax.fori_loop(0, 4, dx_half, 0)
        act("de"[half] + "0")
    put_shared(shared, acc_s, acc_n[0:1, :] / gains[0:1, :])
    act("s0", *TAIL)
    if not remote:
        results = (res_gate, res_out, res_value, res_state, res_small, res_shared, res_branch, res_dx)
        copies = [
            pltpu.make_async_copy(src, dst, local.at[n])
            for n, (src, dst) in enumerate(zip((sum_gate, sum_out, sum_value, sum_state, small, shared, branch, dx), results))
        ]
        for cp in copies:
            cp.start()
        for cp in copies:
            cp.wait()


def layer(*operands, remote=True):
    f32, bf16 = jnp.float32, jnp.bfloat16
    weight, rows = (2, 4, 4, 96, 384), (2, 2, 256, 1536)
    outs = [weight, weight, weight, (2, 4, 4, 32, 384), (4, 4, 16, 128), (4, 4, 16, 128), rows, rows]
    scratch = [
        ((1024, 1536), bf16), ((1024, 768), bf16), ((1024, 768), bf16), ((1024, 768), bf16), ((1032, 768), f32),
        ((1032, 256), f32), ((1024, 256), bf16), ((1024, 128), bf16), ((1024, 128), f32),
        ((1040, 128), f32), ((8, 128, 768), bf16), ((128, 768), f32), ((136, 768), f32), ((136, 256), f32), ((128, 128), f32),
        ((8, 768), f32), ((8, 256), f32), ((8, 128), f32), ((8, 1536), f32), ((8, 768), f32), ((8, 256), f32),
        ((8, 128), f32), ((128, 768), bf16), ((8, 1536), f32),
        ((1536, 768), bf16), ((1536, 768), bf16), ((1536, 256), bf16), ((128, 1536), bf16), ((3, 256, 1536), bf16),
        (rows, bf16), ((8, 8, 128), f32), ((4, 8, 8, 128), f32),
    ] + [(shape, bf16) for shape in outs[:7]]
    vmem, hbm, smem = [pl.BlockSpec(memory_space=space) for space in (pltpu.VMEM, pl.ANY, pltpu.SMEM)]
    count = 8 * DP_SEMS + STATE_SEMS + 3 * TENSOR_SEMS + 6
    return pl.pallas_call(
        functools.partial(layer_kernel, remote),
        out_shape=[jax.ShapeDtypeStruct(shape, bf16) for shape in outs],
        in_specs=[hbm] * 6 + [vmem] * 8 + [smem] * 3,
        out_specs=[hbm] * 8,
        scratch_shapes=[pltpu.VMEM(shape, kind) for shape, kind in scratch]
        + dp_scratch(96, 384) * 4
        + dp_scratch(16, 128)
        + dp_scratch(16, 128, 16, True)
        + state_scratch(32, 384)
        + [pltpu.VMEM((2, 4, 96, 384), bf16)] * 2
        + [pltpu.VMEM((96, 384), bf16)] * 2
        + [pltpu.VMEM((2, 256, 1536), bf16)] + [pltpu.VMEM((256, 1536), bf16)] * 3
        + [pltpu.SemaphoreType.DMA((count,)), pltpu.SemaphoreType.DMA((count,)), pltpu.SemaphoreType.DMA((9,))],
        compiler_params=pltpu.CompilerParams(
            collective_id=0 if remote else None, has_side_effects=True, vmem_limit_bytes=63 * 2**20
        ),
        name="layer",
    )(*operands)


def finish_kernel(
    gate_in, out_in, value_in, state_in, small, shared, branch_in, dx_in,
    mixed_out, tokens_out, gate_out, value_out, out_out, state_out, step, value_taps, value_bias, state_taps, state_bias, step_bias,
    log_rate, bypass, gain, mixer_gain,
    dx, sum_gate, sum_out, sum_value, sum_state, mixed, grad_tokens, gate, value, out, state, arrive, leave,
):
    loads = []
    for n, (src, dst) in enumerate(((gate_in, sum_gate), (value_in, sum_value), (out_in, sum_out), (state_in, sum_state))):
        loads.append([pltpu.make_async_copy(src, dst, arrive.at[n])])
    for n in range(4):
        loads.append([pltpu.make_async_copy(dx_in.at[n], dx.at[n], arrive.at[4 + n])])
    for group in loads:
        for cp in group:
            cp.start()
    stores = []

    def store(src, dst):
        stores.append(pltpu.make_async_copy(src, dst, leave.at[len(stores)]))
        stores[-1].start()

    mixed_load = pltpu.make_async_copy(branch_in, mixed, arrive.at[8])
    mixed_load.start()
    for n, (summed, result, home) in enumerate(
        ((sum_gate, gate, gate_out), (sum_value, value, value_out), (sum_out, out, out_out))
    ):
        loads[n][0].wait()
        for i in range(4):
            for stream in range(2):
                if n < 2:
                    rows, columns = pl.ds(i * 384, 384), pl.ds(stream * 384, 384)
                else:
                    rows, columns = pl.ds(i % 2 * 384, 384), pl.ds(i // 2 * 768 + stream * 384, 384)
                result[rows, columns] = summed[stream, i].astype(jnp.float32).reshape(384, 384)
            if n < 2:
                store(result.at[rows], home.at[rows])
            elif i > 1:
                store(result.at[rows], home.at[rows])
    blocks = [small[j // 4, j % 4].astype(jnp.float32) for j in range(12)]
    step[...] = jnp.concatenate([block[0:12] for block in blocks], 1)
    rows = [block[n : n + 1] for block in blocks for n in range(12, 16)]
    channels = [jnp.concatenate(rows[6 * n : 6 * n + 6], 1) for n in range(7)]
    value_taps[...] = jnp.concatenate(channels[0:4], 0)
    value_bias[...] = channels[4].reshape(768)
    mixer_gain[...] = channels[5].reshape(768)
    bypass[...] = mul_nt(low(jnp.broadcast_to(channels[6], (16, 768))), expansion())[0:1, 0:12].reshape(12)
    step_bias[...] = rows[42][:, 0:12].reshape(12)
    log_rate[...] = rows[43][:, 0:12].reshape(12)
    gains, convs = [shared[0, j].astype(jnp.float32) for j in range(2)]
    gain[...] = jnp.concatenate([gains[n : n + 1] for n in range(12)], 1).reshape(1536)
    taps = [jnp.concatenate([convs[2 * n : 2 * n + 1], convs[2 * n + 1 : 2 * n + 2]], 1) for n in range(5)]
    state_taps[...] = jnp.concatenate(taps[0:4], 0)
    state_bias[...] = taps[4].reshape(256)
    loads[3][0].wait()
    for i in range(4):
        rows = pl.ds(i * 128, 128)
        first, second = [sum_state[stream, i].astype(jnp.float32).reshape(128, 384) for stream in range(2)]
        state[0, rows, :] = first[:, 0:256]
        state[1, rows, 0:128] = first[:, 256:384]
        state[1, rows, 128:256] = second[:, 0:128]
        state[2, rows, :] = second[:, 128:384]
    store(state, state_out)
    mixed_load.wait()
    store(mixed, mixed_out)
    for n in range(4):
        loads[4 + n][0].wait()
        rows = pl.ds(n * 256, 256)
        grad_tokens[rows, :] = dx[n].astype(jnp.float32)
        store(grad_tokens.at[rows], tokens_out.at[rows])
    for cp in stores:
        cp.wait()


def finished(*sums):
    f32, bf16 = jnp.float32, jnp.bfloat16
    large = [((1024, 1536), bf16), ((1024, 1536), f32), ((1536, 768), f32), ((1536, 768), f32), ((768, 1536), f32), ((3, 512, 256), f32)]
    rest = [((12, 1536), f32), ((4, 768), f32), ((768,), f32), ((4, 256), f32), ((256,), f32)] + [((12,), f32)] * 3
    rest += [((1536,), f32), ((768,), f32)]
    scratch = [((4, 256, 1536), bf16)] + [((2, 4, 4, 96, 384), bf16)] * 3 + [((2, 4, 4, 32, 384), bf16)] + large
    vmem, hbm = pl.BlockSpec(memory_space=pltpu.VMEM), pl.BlockSpec(memory_space=pl.ANY)
    return pl.pallas_call(
        finish_kernel,
        out_shape=[jax.ShapeDtypeStruct(shape, kind) for shape, kind in large + rest],
        in_specs=[hbm, hbm, hbm, hbm, vmem, vmem, hbm, hbm],
        out_specs=[hbm] * len(large) + [vmem] * len(rest),
        scratch_shapes=[pltpu.VMEM(shape, kind) for shape, kind in scratch]
        + [pltpu.SemaphoreType.DMA((20,)), pltpu.SemaphoreType.DMA((19,))],
        compiler_params=pltpu.CompilerParams(vmem_limit_bytes=60 * 2**20),
        name="finish",
    )(*sums)


def local(
    tokens,
    segment,
    gate_proj,
    value_proj,
    state_proj,
    step_proj,
    value_conv,
    value_conv_bias,
    state_conv,
    state_conv_bias,
    step_bias,
    log_rate,
    bypass_gain,
    norm_gain,
    gated_norm_gain,
    out_proj,
    cotangent,
):
    sum_gate, sum_out, sum_value, sum_state, small, shared, branch, dx = layer(
        tokens, cotangent.reshape(2, 2, 256, 1536), gate_proj, value_proj, state_proj, out_proj.reshape(3, 256, 1536), segment, step_proj.T,
        value_conv, value_conv_bias, state_conv, state_conv_bias, norm_gain, gated_norm_gain, step_bias, log_rate, bypass_gain,
    )
    (
        mixed_out, grad_tokens, grad_gate, grad_value, grad_out, grad_state, grad_step, grad_value_conv, grad_value_bias,
        grad_state_conv, grad_state_bias, grad_step_bias, grad_log_rate, grad_bypass, grad_gain, grad_mixer_gain,
    ) = finished(
        sum_gate, sum_out, sum_value, sum_state, small, shared, branch.reshape(tokens.shape), dx.reshape(4, 256, 1536)
    )
    return (
        mixed_out,
        grad_tokens,
        grad_gate,
        grad_value,
        grad_state.reshape(state_proj.shape),
        grad_step.T,
        grad_value_conv,
        grad_value_bias,
        grad_state_conv,
        grad_state_bias,
        grad_step_bias,
        grad_log_rate,
        grad_bypass,
        grad_gain,
        grad_mixer_gain,
        grad_out,
    )


def solution(mesh):
    placed = (
        P("dp", None),
        P("dp", None),
        P(None, "tensor"),
        P(None, "tensor"),
        P(),
        P(None, "tensor"),
        P(None, "tensor"),
        P("tensor"),
        P(),
        P(),
        P("tensor"),
        P("tensor"),
        P("tensor"),
        P(),
        P("tensor"),
        P("tensor", None),
        P("dp", None),
    )
    return jax.shard_map(
        local,
        mesh=mesh,
        in_specs=placed,
        out_specs=(
            P("dp", None),
            P("dp", None),
            P(None, "tensor"),
            P(None, "tensor"),
            P(),
            P(None, "tensor"),
            P(None, "tensor"),
            P("tensor"),
            P(),
            P(),
            P("tensor"),
            P("tensor"),
            P("tensor"),
            P(),
            P("tensor"),
            P("tensor", None),
        ),
        check_vma=False,
    )
```

```python
import functools

import jax
import jax.numpy as jnp
from jax import lax
from jax.experimental import pallas as pl
from jax.experimental.pallas import tpu as pltpu
from jax.sharding import PartitionSpec as P

EPS = 1e-05
MESH_ID = pl.DeviceIdType.MESH


def place():
    dp = lax.axis_index("dp")
    tensor = lax.axis_index("tensor")
    return {"x": dp // 8, "y": (dp // 4) % 2, "z": dp % 4, "t": tensor}


def device_at(at, **moved):
    spot = dict(at, **moved)
    return (spot["x"] * 8 + spot["y"] * 4 + spot["z"], spot["t"])


def dp_peers(at):
    return [
        device_at(at, x=(at["x"] + 1) % 4),
        device_at(at, x=(at["x"] + 3) % 4),
        device_at(at, z=(at["z"] + 1) % 4),
        device_at(at, z=(at["z"] + 3) % 4),
        device_at(at, y=1 - at["y"]),
    ]


def tensor_peers(at):
    return [device_at(at, t=(at["t"] + step) % 4) for step in (1, 2, 3)]


def greet(peers):
    barrier = pltpu.get_barrier_semaphore()
    for peer in peers:
        pl.semaphore_signal(barrier, inc=1, device_id=peer, device_id_type=MESH_ID)


def added(*refs):
    total = refs[0][...].astype(jnp.float32)
    for ref in refs[1:]:
        total = total + ref[...].astype(jnp.float32)
    return total.astype(jnp.bfloat16)


class Staged:
    def __init__(self, send, recv, first):
        self.send, self.recv, self.first = send, recv, first

    def start(self, stage):
        send, recv = self.send.at[self.first + stage], self.recv.at[self.first + stage]
        for src, dst, peer in self.copies(stage):
            if peer is None:
                pltpu.make_async_copy(src, dst, recv).start()
            else:
                pltpu.make_async_remote_copy(
                    src_ref=src, dst_ref=dst, send_sem=send, recv_sem=recv, device_id=peer, device_id_type=MESH_ID
                ).start()

    def finish(self, stage):
        send, recv = self.send.at[self.first + stage], self.recv.at[self.first + stage]
        arrived, sent = self.totals(stage)
        peer = self.copies(stage)[0][2]
        for ref in (sent, arrived):
            copy = pltpu.make_async_remote_copy(
                src_ref=ref, dst_ref=ref, send_sem=send, recv_sem=recv, device_id=peer, device_id_type=MESH_ID
            )
            if ref is sent:
                copy.wait_send()
            if ref is arrived:
                copy.wait_recv()
            if sent is arrived:
                break
        self.settle(stage)


class SumOverDp(Staged):
    stages = 8

    def __init__(self, at, order, buf, res, scratch, sems, across=None, direct=False):
        super().__init__(*sems)
        self.at, self.buf, self.res, self.across, self.direct = at, buf, res, across, direct
        self.ta1, self.ta2, self.tb, self.ty, self.own, self.tt = scratch
        a_axis, b_axis = order
        self.a, self.b = at[a_axis], at[b_axis]
        self.a_up, self.a_down, self.a_far = [(self.a + n) % 4 for n in (1, 3, 2)]
        self.a_right, self.a_left = [device_at(at, **{a_axis: n}) for n in (self.a_up, self.a_down)]
        self.a_others = [(self.a + n) % 4 for n in (1, 2, 3)]
        self.a_peers = [device_at(at, **{a_axis: n}) for n in self.a_others]
        self.b_others = [(self.b + n) % 4 for n in (1, 2, 3)]
        self.b_peers = [device_at(at, **{b_axis: n}) for n in self.b_others]
        self.other = device_at(at, y=1 - at["y"])

    def copies(self, stage):
        buf, res, a, b, own = self.buf, self.res, self.a, self.b, self.own
        near, far = pl.ds(0, 2), pl.ds(2, 2)
        if stage == 0 and self.direct:
            return [(buf.at[i], self.ta1.at[n], peer) for n, (i, peer) in enumerate(zip(self.a_others, self.a_peers))]
        if stage == 6 and self.direct:
            return [(res.at[a], res.at[a], peer) for peer in self.a_peers]
        if stage == 0:
            return [(buf.at[self.a_far, near], self.ta1.at[0], self.a_right), (buf.at[self.a_far, far], self.ta1.at[1], self.a_left)]
        if stage == 1:
            return [(buf.at[self.a_up], self.ta2.at[0], self.a_right), (buf.at[self.a_down], self.ta2.at[1], self.a_left)]
        if stage == 2:
            return [(buf.at[a, j], self.tb.at[n], peer) for n, (j, peer) in enumerate(zip(self.b_others, self.b_peers))]
        if stage == 3:
            return [(buf.at[a, b], self.ty, self.other)]
        if stage == 4:
            return [(own.at[self.across], self.tt.at[self.at["t"]], peer) for peer in tensor_peers(self.at)]
        if stage == 5:
            home = res.at[a, b]
            return [(own, home, peer) for peer in self.b_peers] + [(own, home, None)]
        if stage == 6:
            return [(res.at[a], res.at[a], self.a_right), (res.at[a], res.at[a], self.a_left)]
        return [
            (res.at[self.a_down, near], res.at[self.a_down, near], self.a_right),
            (res.at[self.a_up, far], res.at[self.a_up, far], self.a_left),
        ]

    def totals(self, stage):
        res, a = self.res, self.a
        if stage == 5:
            return res.at[a], res.at[a, pl.ds(0, 3)]
        if stage == 6:
            both = res.at[pl.ds(0, 3 if self.direct else 2)]
        elif stage == 7:
            both = res.at[0]
        elif stage == 4:
            both = self.tt.at[pl.ds(0, 3)]
        else:
            both = (self.ta1, self.ta2, self.tb, self.ty)[stage]
        return both, both

    def settle(self, stage):
        buf, a, b, own = self.buf, self.a, self.b, self.own
        if stage == 0 and self.direct:
            for j in range(4):
                buf[a, j] = added(buf.at[a, j], *(self.ta1.at[n, j] for n in range(3)))
        elif stage == 0:
            for j in range(2):
                buf[self.a_up, j] = added(buf.at[self.a_up, j], self.ta1.at[0, j])
                buf[self.a_down, 2 + j] = added(buf.at[self.a_down, 2 + j], self.ta1.at[1, j])
        elif stage == 1:
            for j in range(4):
                buf[a, j] = added(buf.at[a, j], self.ta2.at[0, j], self.ta2.at[1, j])
        elif stage == 2:
            buf[a, b] = added(buf.at[a, b], *(self.tb.at[n] for n in range(3)))
        elif stage == 3:
            own[...] = added(buf.at[a, b], self.ty)
        elif stage == 4:
            self.tt[self.at["t"]] = own[self.across]
            own[self.across] = added(*(self.tt.at[n] for n in range(4)))


DP_SEMS = SumOverDp.stages


def dp_scratch(rows, width, across=16, direct=False):
    first = [(3, 4, rows, width), (1, 16, width)] if direct else [(2, 2, rows, width), (2, 4, rows, width)]
    shapes = first + [(3, rows, width), (rows, width), (rows, width), (4, across, width)]
    return [pltpu.VMEM(shape, jnp.bfloat16) for shape in shapes]


class SumOverTensor(Staged):
    stages = 4

    def __init__(self, at, rows, buf, res, scratch, sems, ending):
        super().__init__(*sems)
        self.buf, self.res, self.rows, self.ending = buf, res, rows, ending
        self.t0, self.t1 = scratch
        self.c, self.h = at["t"] % 2, at["t"] // 2
        self.sibling = device_at(at, t=self.h * 2 + 1 - self.c)
        self.partner = device_at(at, t=(1 - self.h) * 2 + self.c)

    def copies(self, stage):
        buf, res, c, h, rows = self.buf, self.res, self.c, self.h, self.rows
        if stage == 0:
            return [(buf.at[1 - c, :, rows], self.t0.at[:, rows], self.sibling)]
        if stage == 1:
            return [(buf.at[c, 1 - h, rows], self.t1.at[rows], self.partner)]
        if stage == 2:
            mine, theirs = buf.at[c, h, rows], res.at[c, h, rows]
            return [(mine, theirs, self.partner), (mine, theirs, None)]
        return [(res.at[c, :, rows], res.at[c, :, rows], self.sibling)]

    def totals(self, stage):
        res, c, h, rows = self.res, self.c, self.h, self.rows
        if stage == 2:
            return res.at[c, :, rows], res.at[c, h, rows]
        both = (self.t0.at[:, rows], self.t1.at[rows], None, res.at[c, :, rows])[stage]
        return both, both

    def settle(self, stage):
        buf, c, h, rows = self.buf, self.c, self.h, self.rows
        if stage == 0:
            for n in range(2):
                buf[c, n, rows] = added(buf.at[c, n, rows], self.t0.at[n, rows])
        elif stage == 1:
            total = buf[c, h, rows].astype(jnp.float32) + self.t1[rows].astype(jnp.float32)
            buf[c, h, rows] = self.ending(total, rows)


TENSOR_SEMS = SumOverTensor.stages


class SumState(Staged):
    stages = 8

    def __init__(self, at, buf, res, scratch, sems):
        super().__init__(*sems)
        self.buf, self.res = buf, res
        self.t0, self.ta, self.tb, self.ty, self.tt, self.own = scratch
        x, y, z, t = at["x"], at["y"], at["z"], at["t"]
        c = t % 2
        self.c, self.a, self.b = c, x * (1 - c) + z * c, z * (1 - c) + x * c
        self.sibling = device_at(at, t=t // 2 * 2 + 1 - c)
        self.partner = device_at(at, t=(1 - t // 2) * 2 + c)
        self.other = device_at(at, y=1 - y)
        self.a_peers = [device_at(at, x=(x + n * (1 - c)) % 4, z=(z + n * c) % 4) for n in (1, 2, 3)]
        self.b_peers = [device_at(at, x=(x + n * c) % 4, z=(z + n * (1 - c)) % 4) for n in (1, 2, 3)]

    def copies(self, stage):
        buf, res, a, b, c, own = self.buf, self.res, self.a, self.b, self.c, self.own
        if stage == 0:
            return [(buf.at[1 - c], self.t0, self.sibling)]
        if stage == 1:
            return [(buf.at[c, (a + n + 1) % 4], self.ta.at[n], peer) for n, peer in enumerate(self.a_peers)]
        if stage == 2:
            return [(buf.at[c, a, (b + n + 1) % 4], self.tb.at[n], peer) for n, peer in enumerate(self.b_peers)]
        if stage == 3:
            return [(buf.at[c, a, b], self.ty, self.other)]
        if stage == 4:
            return [(own, self.tt, self.partner)]
        if stage == 5:
            return [(own, res.at[c, a, b], peer) for peer in self.b_peers] + [(own, res.at[c, a, b], None)]
        if stage == 6:
            return [(res.at[c, a], res.at[c, a], peer) for peer in self.a_peers]
        return [(res.at[c], res.at[c], self.sibling)]

    def totals(self, stage):
        res, a, c = self.res, self.a, self.c
        if stage == 5:
            return res.at[c, a], res.at[c, a, pl.ds(0, 3)]
        if stage == 6:
            both = res.at[c, pl.ds(0, 3)]
        elif stage == 7:
            both = res.at[c]
        else:
            both = (self.t0, self.ta, self.tb, self.ty, self.tt)[stage]
        return both, both

    def settle(self, stage):
        buf, a, b, c = self.buf, self.a, self.b, self.c
        if stage == 0:
            for i in range(4):
                for j in range(4):
                    buf[c, i, j] = added(buf.at[c, i, j], self.t0.at[i, j])
        elif stage == 1:
            for j in range(4):
                buf[c, a, j] = added(buf.at[c, a, j], *(self.ta.at[n, j] for n in range(3)))
        elif stage == 2:
            buf[c, a, b] = added(buf.at[c, a, b], *(self.tb.at[n] for n in range(3)))
        elif stage == 3:
            self.own[...] = added(buf.at[c, a, b], self.ty)
        elif stage == 4:
            self.own[...] = added(self.own, self.tt)


STATE_SEMS = SumState.stages


def state_scratch(rows, width):
    block = (rows, width)
    shapes = [(4, 4) + block, (3, 4) + block, (3,) + block, block, block, block]
    return [pltpu.VMEM(shape, jnp.bfloat16) for shape in shapes]


def wide(tile, count=6):
    return jnp.concatenate([tile] * count, axis=1)


def mul(left, right):
    return jnp.dot(left, right, preferred_element_type=jnp.float32)


def mul_nt(left, right):
    return lax.dot_general(left, right, (((1,), (1,)), ((), ())), preferred_element_type=jnp.float32)


def mul_tn(left, right):
    return lax.dot_general(left, right, (((0,), (0,)), ((), ())), preferred_element_type=jnp.float32)


def low(value):
    return value.astype(jnp.bfloat16)


def iota(shape, dim):
    return lax.broadcasted_iota(jnp.int32, shape, dim)


def in_three(value):
    high = low(value).astype(jnp.float32)
    rest = value - high
    middle = low(rest).astype(jnp.float32)
    lane = iota(value.shape, 1)
    return low(jnp.where(lane < 16, high, jnp.where(lane < 32, middle, rest - middle)))


def exact_sum(ones, value):
    high = low(value)
    rest = value - high.astype(jnp.float32)
    middle = low(rest)
    return mul(ones, high) + mul(ones, middle) + mul(ones, low(rest - middle.astype(jnp.float32)))


def softplus(value):
    return jnp.maximum(value, 0.0) + jnp.log1p(jnp.exp(-jnp.abs(value)))


def sigmoid(value):
    return 1.0 / (1.0 + jnp.exp(-value))


def columns_of_segments(seg_ref, segc):
    segc[0:8, :] = jnp.full((8, 128), -1.0, jnp.float32)
    segc[1032:1040, :] = jnp.full((8, 128), -1.0, jnp.float32)

    def fill(k, carry):
        row = jnp.broadcast_to(seg_ref[:, pl.ds(pl.multiple_of(k * 128, 128), 128)].astype(jnp.float32), (128, 128))
        segc[pl.ds(pl.multiple_of(8 + k * 128, 8), 128), :] = row.T
        return carry

    lax.fori_loop(0, 8, fill, 0)


def kept(segc, start):
    around = segc[pl.ds(start, 144), :]
    here = around[8:, :]
    return [(pltpu.roll(around, lag, 0)[8:, :] == here).astype(jnp.float32) for lag in (1, 2, 3)]


def lagged(padded, start, keeps):
    around = padded[pl.ds(start, 136), :]
    count = around.shape[1] // 128
    return [around[8:, :]] + [pltpu.roll(around, lag, 0)[8:, :] * wide(keep[:128], count) for lag, keep in zip((1, 2, 3), keeps)]


def convolved(shifted, taps):
    total = taps[4:5, :] + taps[0:1, :] * shifted[0]
    for lag in (1, 2, 3):
        total = total + taps[lag : lag + 1, :] * shifted[lag]
    return total


def decay(k, start, segc, seg_ref, step_raw, heads):
    rows = pl.ds(start, 128)
    step = softplus(step_raw[rows, :] + heads[0:1, :])
    tri = (iota((128, 128), 0) >= iota((128, 128), 1)).astype(jnp.bfloat16)
    cum = exact_sum(tri, step * heads[1:2, :])
    seg_column = segc[pl.ds(start + 8, 128), :]
    seg_row = seg_ref[:, rows].astype(jnp.float32)
    before = segc[pl.ds(start, 8), :][7:8, :]
    last = seg_column[127:128, :]
    growth = jnp.exp(cum)
    tail = jnp.exp(cum[127:128, :] - cum) * (seg_column == last).astype(jnp.float32)
    return step, cum, seg_column, seg_row, before, last, growth, tail


def expansion():
    row, column = iota((128, 768), 0), iota((128, 768), 1)
    return ((row < 48) & (row % 16 == column // 64)).astype(jnp.bfloat16)


def head_sums(value, expand):
    return mul_nt(low(value), expand)


def slope(pre, sig):
    return sig * (1.0 + pre * (1.0 - sig))


def middle_block(k, total, kept_act, bent, gated_ref, pulled, acc_v):
    rows = pl.ds(pl.multiple_of(k * 128, 128), 128)
    columns = jnp.concatenate([total] * 16, 0).T
    scale = lax.rsqrt(columns[:, 0:1] / 3072 + EPS)
    pull = columns[:, 1:2] * scale * scale * scale / 3072
    gated, q, act, bend = [
        value.astype(jnp.float32) for value in (gated_ref[rows, :], pulled[rows, :], kept_act[...], bent[rows, :])
    ]
    scaled = gated * scale
    acc_v[5:6, :] += jnp.sum(q * scaled, 0, keepdims=True)
    grad_gated = scale * q - gated * pull
    pulled[rows, :] = low(grad_gated * act)
    bent[rows, :] = low(grad_gated * bend)
    return rows, scaled


def put(buf, i, value):
    pieces = low(value.reshape(4, value.shape[0] // 4, 768))
    for stream in range(2):
        buf[stream, i] = pieces[..., stream * 384 : (stream + 1) * 384]


def backward_block(
    k, vpad, spad, step_raw, seg_ref, segc, taps, state_taps, heads, expand, bypass, states, dy,
    dstate, du, dus, head_rows, value_low, state_low, step_low, acc_v, acc_s, acc_h, between,
):
    start = pl.multiple_of(k * 128, 128)
    rows = pl.ds(start, 128)
    keeps = kept(segc, start)
    values = lagged(vpad, start, keeps)
    pre = convolved(values, taps)
    sig = sigmoid(pre)
    x = pre * sig
    state_values = lagged(spad, start, keeps)
    state_pre = convolved(state_values, state_taps)
    state_sig = sigmoid(state_pre)
    state = low(state_pre * state_sig)
    b_in, c_out = state[:, :128], state[:, 128:]
    step, cum, seg_column, seg_row, before, last, growth, tail = decay(k, start, segc, seg_ref, step_raw, heads)
    spread = mul(jnp.concatenate([in_three(step), in_three(growth), in_three(tail)], 0), expand[...])
    step_wide, tail_wide = spread[:128], spread[256:]
    growth_wide = spread[128:256] * wide((seg_column == before).astype(jnp.float32))
    through = spread[255:256] * wide((last == before).astype(jnp.float32))
    xs = x * step_wide
    entering = states[k]
    grad_state = dstate[...]
    grad_state_low = low(grad_state)
    dyk = dy[rows, :].astype(jnp.float32)
    grown = low(dyk * growth_wide)
    outside = mul(c_out, entering) * growth_wide
    dxs_after = mul(b_in, grad_state_low) * tail_wide
    grad_c = mul_nt(grown, entering)
    grad_b = mul_nt(low(xs * tail_wide), grad_state_low)
    end = jnp.sum(entering.astype(jnp.float32) * grad_state, 0, keepdims=True) * through
    dstate[...] = through * grad_state + mul_tn(c_out, grown)
    scores = mul_nt(b_in, c_out)
    row, column = iota((128, 128), 0), iota((128, 128), 1)
    bias = jnp.where((seg_column == seg_row) & (row <= column), 0.0, -1e30)
    tri = (row >= column).astype(jnp.bfloat16)
    strict = row < column
    cum_rows = cum.T
    first = column < 64
    grad_scores = jnp.zeros((128, 128), jnp.float32)
    own_steps = jnp.zeros((128, 128), jnp.float32)
    inside = []
    between(1)
    for pair in range(6):
        lanes = slice(pair * 128, (pair + 1) * 128)
        own = dyk[:, lanes]
        both = low(jnp.concatenate([jnp.where(first, own, 0.0), jnp.where(first, 0.0, own)], 0))
        grad_weights = mul_nt(low(x[:, lanes]), both)
        weights, moved, steps = [], [], []
        for side in range(2):
            h = 2 * pair + side
            faded = jnp.exp(cum_rows[h : h + 1, :] - cum[:, h : h + 1] + bias)
            pulled = grad_weights[:, side * 128 : (side + 1) * 128] * faded
            steps.append(step[:, h : h + 1])
            grad_scores = grad_scores + pulled * steps[side]
            moved.append(low(pulled * scores))
            weights.append(low(scores * faded))
        inside.append(mul(jnp.concatenate(weights, 1), both))
        later = mul(jnp.concatenate(moved, 0), tri)
        for side in range(2):
            h = 2 * pair + side
            part = later[side * 128 : (side + 1) * 128]
            own_steps = jnp.where(column == h, part[:, 0:1], own_steps)
            head_rows[h : h + 1, :] = jnp.sum(jnp.where(strict, part * steps[side], 0.0), 0, keepdims=True)
    between(2)
    grad_scores = low(grad_scores)
    grad_b = grad_b + mul(grad_scores, c_out)
    grad_c = grad_c + mul_tn(grad_scores, b_in)
    dxs = jnp.concatenate(inside, 1) + dxs_after
    dx = dxs * step_wide + bypass * dyk
    summed = head_sums(jnp.concatenate([dyk * outside, x * dxs_after], 0), expand[...])
    end = head_sums(jnp.broadcast_to(end, (16, 768)), expand[...])
    upper = (row <= column).astype(jnp.bfloat16)
    below = (row > column).astype(jnp.bfloat16)
    grad_decay = exact_sum(upper, summed[:128]) + exact_sum(below, step * summed[128:]) + end[0:1, :] + head_rows[...].T
    grad_step = own_steps + summed[128:] + heads[1:2, :] * grad_decay
    grad_raw = grad_step * sigmoid(step_raw[rows, :] + heads[0:1, :])
    step_low[rows, :] = low(jnp.where(column < 16, grad_raw, 0.0))
    acc_h[0:1, :] += jnp.sum(grad_raw, 0, keepdims=True)
    acc_h[1:2, :] += jnp.sum(step * grad_decay, 0, keepdims=True) * heads[1:2, :]
    between(3)
    for grad, grads, shifted, taps_ref, acc, result in (
        (dx * slope(pre, sig), du, values, taps, acc_v, value_low),
        (jnp.concatenate([grad_b, grad_c], 1) * slope(state_pre, state_sig), dus, state_values, state_taps, acc_s, state_low),
    ):
        grads[128:136, :] = grads[0:8, :]
        grads[0:128, :] = grad
        for lag in range(4):
            acc[lag : lag + 1, :] += jnp.sum(grad * shifted[lag], 0, keepdims=True)
        acc[4:5, :] += jnp.sum(grad, 0, keepdims=True)
        around = grads[...]
        count = around.shape[1] // 128
        total = grad * taps_ref[0:1, :]
        for lag, keep in zip((1, 2, 3), keeps):
            total = total + taps_ref[lag : lag + 1, :] * pltpu.roll(around * wide(keep, count), 136 - lag, 0)[:128, :]
        result[rows, :] = low(total)
    acc_v[6:7, :] += jnp.sum(dyk * x, 0, keepdims=True)


def put_small(small, acc_v, acc_h, step_grad):
    small[...] = jnp.zeros_like(small)
    rows = [acc_v[n : n + 1, j * 128 : (j + 1) * 128] for n in range(7) for j in range(6)] + [acc_h[0:1, :], acc_h[1:2, :]]
    place_in = iota((16, 128), 0)
    for j in range(12):
        block = jnp.where(place_in < 12, step_grad[:, j * 128 : (j + 1) * 128], 0.0)
        for n, row in enumerate(rows[4 * j : 4 * j + 4]):
            block = jnp.where(place_in == 12 + n, row, block)
        small[j // 4, j % 4] = low(block)


def put_shared(shared, acc_s, acc_n):
    shared[...] = jnp.zeros_like(shared)
    place_in = iota((16, 128), 0)
    for j, rows in enumerate(
        (
            [acc_n[:, n * 128 : (n + 1) * 128] for n in range(12)],
            [acc_s[n : n + 1, j * 128 : (j + 1) * 128] for n in range(5) for j in range(2)],
        )
    ):
        block = jnp.zeros((16, 128), jnp.float32)
        for n, row in enumerate(rows):
            block = jnp.where(place_in == n, row, block)
        shared[0, j] = low(block)


BRANCH_PLANS = {}
OUT_PLANS = {3: ("g0>",)}
VALUE_PLANS = {}
STATE_PLANS = {3: ("o1>",)}
SCAN_PLANS = (
    {4: ("g2>",), 6: ("o0>", "b1>"), 7: ("g4>",)},
    {},
    {0: ("b0>",), 2: ("g1>",), 4: ("o0",), 5: ("g3>",)},
    {},
)
DX_PLANS = ({3: ("g5>", "b2>")}, {0: ("v0>",), 1: ("o2>",), 3: ("d0>", "g6.", "o3>", "b3.")})
TAIL = (
    "v1>", "e0>", "s0>", "o4>", "d1>", "v2>", "s1>", "s2>", "o5>", "v3>", "s3>", "e1>",
    "s4>", "o6.", "v4>", "d2>", "s5>", "d3.", "e2>", "s6>", "e3.", "v5>", "s7.", "v6.",
)
RING = (0, 1, 2, 3, 5, 6, 7)


def head_row(values, lane, group):
    row = jnp.zeros(lane.shape, jnp.float32)
    for h in range(12):
        row = jnp.where(group(lane, h), values[h], row)
    return row


def layer_kernel(
    remote,
    tokens, cot_in, w_gate_in, w_value_in, w_state_in, w_out_in,
    seg, w_step_in, value_conv, value_bias, state_conv, state_bias, norm_gain, gated_gain, step_bias, log_rate, bypass_gain,
    res_gate, res_out, res_value, res_state, res_small, res_shared, res_branch, res_dx,
    normed, gate, y_ref, q_ref, vpad, spad, state_low, step_low, step_raw, segc, states, carried, du, dus, head_rows,
    acc_v, acc_s, acc_h, acc_n, taps, state_taps, heads, expand, gains,
    w_gate, w_value, w_state, w_step, w_out, cot, sums, landed,
    sum_gate, sum_out, sum_value, sum_state, small, shared, branch,
    *rest,
):
    scratch = [rest[n * 6 : (n + 1) * 6] for n in range(7)]
    value_scratch = [
        (early[0], own_ta2, early[2], own_ty, *early[4:])
        for early, own_ta2, own_ty in zip(scratch[0:2], rest[42:44], rest[44:46])
    ]
    branch_scratch = rest[46:48]
    own_tokens, own_cot, send, recv, local = rest[48:]
    at = place()
    dx = cot
    slots = branch.at[0]

    def fetch(k):
        return pltpu.make_async_copy(tokens.at[pl.ds(pl.multiple_of(k * 256, 256), 256)], slots.at[k % 2], local.at[k % 2])

    loads = [
        pltpu.make_async_copy(src, dst, local.at[2 + n])
        for n, (src, dst) in enumerate(
            (
                (w_gate_in, w_gate),
                (w_value_in, w_value),
                (w_state_in, w_state),
                (cot_in, cot),
                (w_out_in, w_out),
                (tokens.at[pl.ds(pl.multiple_of((at["t"] % 2 * 2 + at["t"] // 2) * 256, 256), 256)], own_tokens),
                (cot_in.at[at["t"] % 2, at["t"] // 2], own_cot),
            )
        )
    ]
    fetch(0).start()
    for cp in loads[:3]:
        cp.start()
    friends = dp_peers(at) + tensor_peers(at)
    if remote:
        greet(friends)

    orders = (("x", "z"), ("z", "x"))

    def pair(first, buf, res, scratch):
        return [
            (SumOverDp(at, order, buf.at[n], res.at[n], scratch[n], (send, recv, (first + n) * DP_SEMS)), RING)
            for n, order in enumerate(orders)
        ]

    last = 8 * DP_SEMS + STATE_SEMS
    dx_scratch = (w_out.at[pl.ds(0, 2)], w_out.at[2])
    upper, lower, all_rows = pl.ds(0, 128), pl.ds(128, 128), pl.ds(0, 256)

    def mixed_rows(total, rows):
        return low(own_tokens[rows].astype(jnp.float32) + total)

    def token_gradient(total, rows):
        hidden = own_tokens[rows].astype(jnp.float32)
        inverse = lax.rsqrt(jnp.sum(hidden * hidden, 1, keepdims=True) / 1536 + EPS)
        scaled = total * gains[0:1, :]
        along = jnp.sum(scaled * hidden, 1, keepdims=True) * (inverse * inverse * inverse / 1536)
        return low(own_cot[rows].astype(jnp.float32) + inverse * scaled - hidden * along)

    def over_tensor(n, rows, buf, res, scratch, ending):
        return [(SumOverTensor(at, rows, buf, res, scratch, (send, recv, last + n * TENSOR_SEMS), ending), range(4))]

    engines = {
        "g": pair(0, sum_gate, res_gate, scratch[0:2]),
        "o": pair(2, sum_out, res_out, scratch[2:4]),
        "v": pair(4, sum_value, res_value, value_scratch)
        + [(SumOverDp(at, orders[0], small, res_small, scratch[4], (send, recv, 6 * DP_SEMS)), RING)],
        "s": [
            (SumState(at, sum_state, res_state, scratch[6], (send, recv, 8 * DP_SEMS)), range(8)),
            (
                SumOverDp(at, orders[0], shared, res_shared, scratch[5], (send, recv, 7 * DP_SEMS), pl.ds(0, 16), True),
                (None, 0, 2, 3, 4, 5, 6, None),
            ),
        ],
        "b": over_tensor(0, all_rows, branch, res_branch, branch_scratch, mixed_rows),
        "d": over_tensor(1, upper, dx, res_dx, dx_scratch, token_gradient),
        "e": over_tensor(2, lower, dx, res_dx, dx_scratch, token_gradient),
    }

    def act(*plan):
        if not remote:
            return
        for word in plan:
            step = int(word[1])
            if word[2:]:
                for engine, stages in engines[word[0]]:
                    if stages[step] is not None:
                        engine.finish(stages[step])
                step += 1
            if word[2:] != ".":
                for engine, stages in engines[word[0]]:
                    if stages[step] is not None:
                        engine.start(stages[step])

    def act_at(i, plans):
        for n, plan in plans.items():

            @pl.when(i == n)
            def _():
                act(*plan)

    for ref in (du, dus, head_rows, carried, acc_v, acc_s, acc_h, acc_n, taps, state_taps, gains):
        ref[...] = jnp.zeros_like(ref)
    vpad[0:8, :] = jnp.zeros((8, 768), jnp.float32)
    spad[0:8, :] = jnp.zeros((8, 256), jnp.float32)
    columns_of_segments(seg, segc)
    taps[0:4, :] = value_conv[...]
    taps[4:5, :] = value_bias[...].reshape(1, 768)
    state_taps[0:4, :] = state_conv[...]
    state_taps[4:5, :] = state_bias[...].reshape(1, 256)
    lane = iota((8, 128), 1)
    heads[...] = head_row(step_bias, lane, lambda l, h: (l % 16 == h) & (l < 48))
    rate = head_row(log_rate, lane, lambda l, h: (l % 16 == h) & (l < 48))
    heads[1:2, :] = jnp.where((lane % 16 < 12) & (lane < 48), -jnp.exp(rate), 0.0)[0:1]
    gains[0:1, :] = norm_gain[...].reshape(1, 1536)
    gains[1:2, 0:768] = gated_gain[...].reshape(1, 768)
    gains[2:3, 0:768] = head_row(bypass_gain, iota((1, 768), 1), lambda l, h: l // 64 == h)
    expand[...] = expansion()
    chosen = ((iota((12, 128), 1) % 16 == iota((12, 128), 0)) & (iota((12, 128), 1) < 48)).astype(jnp.bfloat16)
    w_step[...] = low(mul_tn(chosen, w_step_in[...]))
    for cp in loads[:3]:
        cp.wait()
    for cp in loads[3:]:
        cp.start()

    def project(k, carry):
        rows = pl.ds(pl.multiple_of(k * 256, 256), 256)
        padded = pl.ds(pl.multiple_of(8 + k * 256, 8), 256)

        @pl.when(k < 3)
        def _():
            fetch(k + 1).start()

        fetch(k).wait()
        hidden = slots[k % 2].astype(jnp.float32)
        inverse = lax.rsqrt(jnp.sum(hidden * hidden, 1, keepdims=True) / 1536 + EPS)
        normal = low(hidden * inverse * gains[0:1, :])
        normed[rows, :] = normal
        gate[rows, :] = low(mul(normal, w_gate[...]))
        vpad[padded, :] = mul(normal, w_value[...])
        spad[padded, :] = mul(normal, w_state[...])
        step_raw[rows, :] = mul_nt(normal, w_step[...])
        return carry

    lax.fori_loop(0, 4, project, 0)
    for cp in loads[3:]:
        cp.wait()

    def project_back(k, carry):
        rows = pl.ds(pl.multiple_of(k * 256, 256), 256)
        q_ref[rows, :] = low(mul_nt(cot[k // 2, k % 2], w_out[...].reshape(768, 1536)) * gains[1:2, 0:768])
        return carry

    lax.fori_loop(0, 4, project_back, 0)

    def act_of(k):
        rows, columns = pl.ds(k // 2 % 2 * 128, 128), pl.ds(pl.multiple_of(k % 2 * 768, 128), 768)
        return branch.at[1, k // 4, rows, columns]

    def forward_block(k, carry):
        start = pl.multiple_of(k * 128, 128)
        rows = pl.ds(start, 128)
        keeps = kept(segc, start)
        pre = convolved(lagged(vpad, start, keeps), taps)
        x = pre * sigmoid(pre)
        pre = convolved(lagged(spad, start, keeps), state_taps)
        state = low(pre * sigmoid(pre))
        b_in, c_out = state[:, :128], state[:, 128:]
        step, cum, seg_column, seg_row, before, last, growth, tail = decay(k, start, segc, seg, step_raw, heads)
        spread = mul(jnp.concatenate([in_three(step), in_three(growth), in_three(tail)], 0), expand[...])
        xs = x * spread[:128]
        start_keep = (seg_column == before).astype(jnp.float32)
        entering = carried[...]
        states[k] = low(entering)
        outside = mul(c_out, low(entering)) * (spread[128:256] * wide(start_keep))
        through = spread[255:256] * wide((last == before).astype(jnp.float32))
        carried[...] = through * entering + mul_tn(b_in, low(xs * spread[256:]))
        scores = mul_nt(c_out, b_in)
        bias = jnp.where((seg_column == seg_row) & (iota((128, 128), 0) >= iota((128, 128), 1)), 0.0, -1e30)
        cum_rows = cum.T
        first = iota((128, 128), 1) < 64
        inside = []
        for pair in range(6):
            own = xs[:, pair * 128 : (pair + 1) * 128]
            right = low(jnp.concatenate([jnp.where(first, own, 0.0), jnp.where(first, 0.0, own)], 0))
            left = [
                low(scores * jnp.exp(cum[:, h : h + 1] - cum_rows[h : h + 1, :] + bias)) for h in (2 * pair, 2 * pair + 1)
            ]
            inside.append(mul(jnp.concatenate(left, 1), right))
        y = jnp.concatenate(inside, 1) + outside + gains[2:3, 0:768] * x
        raw = gate[rows, :].astype(jnp.float32)
        sig = sigmoid(raw)
        act = raw * sig
        gated = y * act
        y_ref[rows, :] = low(gated)
        gate[rows, :] = low(y * slope(raw, sig))
        act_of(k)[...] = low(act)
        squares = jnp.sum(gated * gated, 1, keepdims=True)
        cross = jnp.sum(q_ref[rows, :].astype(jnp.float32) * gated, 1, keepdims=True)
        lanes = iota((128, 128), 1)
        sums[k] = jnp.where(lanes == 0, squares, jnp.where(lanes == 1, cross, 0.0)).T[0:8, :]
        return carry

    def exchange(half):
        blocks, first = pl.ds(4 * half, 4), last + 3 * TENSOR_SEMS + 3 * half
        copies = [
            pltpu.make_async_remote_copy(
                src_ref=sums.at[blocks],
                dst_ref=landed.at[at["t"], blocks],
                send_sem=send.at[first + n],
                recv_sem=recv.at[first + n],
                device_id=peer,
                device_id_type=MESH_ID,
            )
            for n, peer in enumerate(tensor_peers(at))
        ]
        if not remote:
            for n in range(4):
                landed[n, blocks] = sums[blocks] * 0.75
            return []
        for cp in copies:
            cp.start()
        landed[at["t"], blocks] = sums[blocks]
        return copies

    def middle(k, carry):
        total = (landed[0, k] + landed[1, k]) + (landed[2, k] + landed[3, k])
        rows, scaled = middle_block(k, total, act_of(k), gate, y_ref, q_ref, acc_v)
        y_ref[rows, :] = low(scaled * gains[1:2, 0:768])
        return carry

    lax.fori_loop(0, 4, forward_block, 0)
    if remote:
        pl.semaphore_wait(pltpu.get_barrier_semaphore(), len(friends))
    first_sums = exchange(0)
    lax.fori_loop(4, 8, forward_block, 0)
    second_sums = exchange(1)
    for cp in first_sums:
        cp.wait()
    lax.fori_loop(0, 4, middle, 0)
    for cp in second_sums:
        cp.wait()
    lax.fori_loop(4, 8, middle, 0)
    acc_v[5:6, :] = acc_v[5:6, :] / gains[1:2, 0:768]
    gate_low, gate_normed, dy = gate, y_ref, q_ref
    value_low = y_ref

    def gate_weights(i, carry):
        put(sum_gate, i, mul_tn(normed[:, pl.ds(pl.multiple_of(i * 384, 128), 384)], gate_low[...]))
        return carry

    def out_weights(i, carry):
        out_rows = pl.ds(pl.multiple_of((i % 2) * 384, 128), 384)
        out_columns = pl.ds(pl.multiple_of((i // 2) * 768, 128), 768)
        put(sum_out, i, mul_tn(gate_normed[:, out_rows], cot[:, :, :, out_columns].reshape(1024, 768)))
        act_at(i, OUT_PLANS)
        return carry

    def branch_rows(i, carry):
        rows = pl.ds(pl.multiple_of(i * 256, 256), 256)
        branch[i // 2, i % 2] = low(mul(gate_normed[rows, :], w_out[...].reshape(768, 1536)))
        act_at(i, BRANCH_PLANS)
        return carry

    lax.fori_loop(0, 4, gate_weights, 0)
    act("g0")
    lax.fori_loop(0, 4, branch_rows, 0)
    act("b0")
    lax.fori_loop(0, 4, out_weights, 0)
    carried[...] = jnp.zeros((128, 768), jnp.float32)

    def scan(i, carry):
        act_at(i, SCAN_PLANS[0])
        backward_block(
            7 - i, vpad, spad, step_raw, seg, segc, taps, state_taps, heads, expand, gains[2:3, 0:768], states, dy,
            carried, du, dus, head_rows, value_low, state_low, step_low, acc_v, acc_s, acc_h,
            lambda point: act_at(i, SCAN_PLANS[point]),
        )
        return carry

    lax.fori_loop(0, 8, scan, 0)

    def value_weights(i, carry):
        put(sum_value, i, mul_tn(normed[:, pl.ds(pl.multiple_of(i * 384, 128), 384)], value_low[...]))
        act_at(i, VALUE_PLANS)
        return carry

    def state_weights(i, carry):
        thirds = [
            mul_tn(normed[:, pl.ds(pl.multiple_of(q * 512 + i * 128, 128), 128)], state_low[...]) for q in range(3)
        ]
        put(sum_state, i, jnp.concatenate(thirds, 1))
        act_at(i, STATE_PLANS)
        return carry

    lax.fori_loop(0, 4, value_weights, 0)
    put_small(small, acc_v, acc_h, mul_tn(step_low[...], normed[...])[0:16, :])
    act("v0")
    lax.fori_loop(0, 4, state_weights, 0)

    def dx_rows(half, i):
        firsts = [pl.ds(pl.multiple_of((i // 2 * 2 + n) * 256 + half * 128, 128), 128) for n in range(2)]
        columns = pl.ds(pl.multiple_of(i % 2 * 768, 128), 768)

        def both(ref, *lanes):
            return jnp.concatenate([ref[(rows, *lanes)] for rows in firsts], 0)

        part = mul_nt(both(gate_low), w_gate[columns, :]) + mul_nt(both(value_low), w_value[columns, :])
        part = part + mul_nt(both(state_low), w_state[columns, :]) + mul(both(step_low), w_step[:, columns])
        for n in range(2):
            dx[i // 2, n, half * 128 : half * 128 + 128, columns] = low(part[n * 128 : n * 128 + 128])
        acc_n[0:1, columns] += jnp.sum(part * both(normed, columns).astype(jnp.float32), 0, keepdims=True)
        act_at(i, DX_PLANS[half])

    for half in range(2):

        def dx_half(i, carry):
            dx_rows(half, i)
            return carry

        lax.fori_loop(0, 4, dx_half, 0)
        act("de"[half] + "0")
    put_shared(shared, acc_s, acc_n[0:1, :] / gains[0:1, :])
    act("s0", *TAIL)
    if not remote:
        results = (res_gate, res_out, res_value, res_state, res_small, res_shared, res_branch, res_dx)
        copies = [
            pltpu.make_async_copy(src, dst, local.at[n])
            for n, (src, dst) in enumerate(zip((sum_gate, sum_out, sum_value, sum_state, small, shared, branch, dx), results))
        ]
        for cp in copies:
            cp.start()
        for cp in copies:
            cp.wait()


def layer(*operands, remote=True):
    f32, bf16 = jnp.float32, jnp.bfloat16
    weight, rows = (2, 4, 4, 96, 384), (2, 2, 256, 1536)
    outs = [weight, weight, weight, (2, 4, 4, 32, 384), (4, 4, 16, 128), (4, 4, 16, 128), rows, rows]
    scratch = [
        ((1024, 1536), bf16), ((1024, 768), bf16), ((1024, 768), bf16), ((1024, 768), bf16), ((1032, 768), f32),
        ((1032, 256), f32), ((1024, 256), bf16), ((1024, 128), bf16), ((1024, 128), f32),
        ((1040, 128), f32), ((8, 128, 768), bf16), ((128, 768), f32), ((136, 768), f32), ((136, 256), f32), ((128, 128), f32),
        ((8, 768), f32), ((8, 256), f32), ((8, 128), f32), ((8, 1536), f32), ((8, 768), f32), ((8, 256), f32),
        ((8, 128), f32), ((128, 768), bf16), ((8, 1536), f32),
        ((1536, 768), bf16), ((1536, 768), bf16), ((1536, 256), bf16), ((128, 1536), bf16), ((3, 256, 1536), bf16),
        (rows, bf16), ((8, 8, 128), f32), ((4, 8, 8, 128), f32),
    ] + [(shape, bf16) for shape in outs[:7]]
    vmem, hbm, smem = [pl.BlockSpec(memory_space=space) for space in (pltpu.VMEM, pl.ANY, pltpu.SMEM)]
    count = 8 * DP_SEMS + STATE_SEMS + 3 * TENSOR_SEMS + 6
    return pl.pallas_call(
        functools.partial(layer_kernel, remote),
        out_shape=[jax.ShapeDtypeStruct(shape, bf16) for shape in outs],
        in_specs=[hbm] * 6 + [vmem] * 8 + [smem] * 3,
        out_specs=[hbm] * 8,
        scratch_shapes=[pltpu.VMEM(shape, kind) for shape, kind in scratch]
        + dp_scratch(96, 384) * 4
        + dp_scratch(16, 128)
        + dp_scratch(16, 128, 16, True)
        + state_scratch(32, 384)
        + [pltpu.VMEM((2, 4, 96, 384), bf16)] * 2
        + [pltpu.VMEM((96, 384), bf16)] * 2
        + [pltpu.VMEM((2, 256, 1536), bf16)] + [pltpu.VMEM((256, 1536), bf16)] * 3
        + [pltpu.SemaphoreType.DMA((count,)), pltpu.SemaphoreType.DMA((count,)), pltpu.SemaphoreType.DMA((9,))],
        compiler_params=pltpu.CompilerParams(
            collective_id=0 if remote else None, has_side_effects=True, vmem_limit_bytes=63 * 2**20
        ),
        name="layer",
    )(*operands)


def finish_kernel(
    gate_in, out_in, value_in, state_in, small, shared, branch_in, dx_in,
    mixed_out, tokens_out, gate_out, value_out, out_out, state_out, step, value_taps, value_bias, state_taps, state_bias, step_bias,
    log_rate, bypass, gain, mixer_gain,
    dx, sum_gate, sum_out, sum_value, sum_state, mixed, grad_tokens, gate, value, out, state, arrive, leave,
):
    loads = []
    for n, (src, dst) in enumerate(((gate_in, sum_gate), (value_in, sum_value), (out_in, sum_out), (state_in, sum_state))):
        loads.append([pltpu.make_async_copy(src, dst, arrive.at[n])])
    for n in range(4):
        loads.append([pltpu.make_async_copy(dx_in.at[n], dx.at[n], arrive.at[4 + n])])
    for group in loads:
        for cp in group:
            cp.start()
    stores = []

    def store(src, dst):
        stores.append(pltpu.make_async_copy(src, dst, leave.at[len(stores)]))
        stores[-1].start()

    mixed_load = pltpu.make_async_copy(branch_in, mixed, arrive.at[8])
    mixed_load.start()
    for n, (summed, result, home) in enumerate(
        ((sum_gate, gate, gate_out), (sum_value, value, value_out), (sum_out, out, out_out))
    ):
        loads[n][0].wait()
        for i in range(4):
            for stream in range(2):
                if n < 2:
                    rows, columns = pl.ds(i * 384, 384), pl.ds(stream * 384, 384)
                else:
                    rows, columns = pl.ds(i % 2 * 384, 384), pl.ds(i // 2 * 768 + stream * 384, 384)
                result[rows, columns] = summed[stream, i].astype(jnp.float32).reshape(384, 384)
            if n < 2:
                store(result.at[rows], home.at[rows])
            elif i > 1:
                store(result.at[rows], home.at[rows])
    blocks = [small[j // 4, j % 4].astype(jnp.float32) for j in range(12)]
    step[...] = jnp.concatenate([block[0:12] for block in blocks], 1)
    rows = [block[n : n + 1] for block in blocks for n in range(12, 16)]
    channels = [jnp.concatenate(rows[6 * n : 6 * n + 6], 1) for n in range(7)]
    value_taps[...] = jnp.concatenate(channels[0:4], 0)
    value_bias[...] = channels[4].reshape(768)
    mixer_gain[...] = channels[5].reshape(768)
    bypass[...] = mul_nt(low(jnp.broadcast_to(channels[6], (16, 768))), expansion())[0:1, 0:12].reshape(12)
    step_bias[...] = rows[42][:, 0:12].reshape(12)
    log_rate[...] = rows[43][:, 0:12].reshape(12)
    gains, convs = [shared[0, j].astype(jnp.float32) for j in range(2)]
    gain[...] = jnp.concatenate([gains[n : n + 1] for n in range(12)], 1).reshape(1536)
    taps = [jnp.concatenate([convs[2 * n : 2 * n + 1], convs[2 * n + 1 : 2 * n + 2]], 1) for n in range(5)]
    state_taps[...] = jnp.concatenate(taps[0:4], 0)
    state_bias[...] = taps[4].reshape(256)
    loads[3][0].wait()
    for i in range(4):
        rows = pl.ds(i * 128, 128)
        first, second = [sum_state[stream, i].astype(jnp.float32).reshape(128, 384) for stream in range(2)]
        state[0, rows, :] = first[:, 0:256]
        state[1, rows, 0:128] = first[:, 256:384]
        state[1, rows, 128:256] = second[:, 0:128]
        state[2, rows, :] = second[:, 128:384]
    store(state, state_out)
    mixed_load.wait()
    store(mixed, mixed_out)
    for n in range(4):
        loads[4 + n][0].wait()
        rows = pl.ds(n * 256, 256)
        grad_tokens[rows, :] = dx[n].astype(jnp.float32)
        store(grad_tokens.at[rows], tokens_out.at[rows])
    for cp in stores:
        cp.wait()


def finished(*sums):
    f32, bf16 = jnp.float32, jnp.bfloat16
    large = [((1024, 1536), bf16), ((1024, 1536), f32), ((1536, 768), f32), ((1536, 768), f32), ((768, 1536), f32), ((3, 512, 256), f32)]
    rest = [((12, 1536), f32), ((4, 768), f32), ((768,), f32), ((4, 256), f32), ((256,), f32)] + [((12,), f32)] * 3
    rest += [((1536,), f32), ((768,), f32)]
    scratch = [((4, 256, 1536), bf16)] + [((2, 4, 4, 96, 384), bf16)] * 3 + [((2, 4, 4, 32, 384), bf16)] + large
    vmem, hbm = pl.BlockSpec(memory_space=pltpu.VMEM), pl.BlockSpec(memory_space=pl.ANY)
    return pl.pallas_call(
        finish_kernel,
        out_shape=[jax.ShapeDtypeStruct(shape, kind) for shape, kind in large + rest],
        in_specs=[hbm, hbm, hbm, hbm, vmem, vmem, hbm, hbm],
        out_specs=[hbm] * len(large) + [vmem] * len(rest),
        scratch_shapes=[pltpu.VMEM(shape, kind) for shape, kind in scratch]
        + [pltpu.SemaphoreType.DMA((20,)), pltpu.SemaphoreType.DMA((19,))],
        compiler_params=pltpu.CompilerParams(vmem_limit_bytes=60 * 2**20),
        name="finish",
    )(*sums)


def local(
    tokens,
    segment,
    gate_proj,
    value_proj,
    state_proj,
    step_proj,
    value_conv,
    value_conv_bias,
    state_conv,
    state_conv_bias,
    step_bias,
    log_rate,
    bypass_gain,
    norm_gain,
    gated_norm_gain,
    out_proj,
    cotangent,
):
    sum_gate, sum_out, sum_value, sum_state, small, shared, branch, dx = layer(
        tokens, cotangent.reshape(2, 2, 256, 1536), gate_proj, value_proj, state_proj, out_proj.reshape(3, 256, 1536), segment, step_proj.T,
        value_conv, value_conv_bias, state_conv, state_conv_bias, norm_gain, gated_norm_gain, step_bias, log_rate, bypass_gain,
    )
    (
        mixed_out, grad_tokens, grad_gate, grad_value, grad_out, grad_state, grad_step, grad_value_conv, grad_value_bias,
        grad_state_conv, grad_state_bias, grad_step_bias, grad_log_rate, grad_bypass, grad_gain, grad_mixer_gain,
    ) = finished(
        sum_gate, sum_out, sum_value, sum_state, small, shared, branch.reshape(tokens.shape), dx.reshape(4, 256, 1536)
    )
    return (
        mixed_out,
        grad_tokens,
        grad_gate,
        grad_value,
        grad_state.reshape(state_proj.shape),
        grad_step.T,
        grad_value_conv,
        grad_value_bias,
        grad_state_conv,
        grad_state_bias,
        grad_step_bias,
        grad_log_rate,
        grad_bypass,
        grad_gain,
        grad_mixer_gain,
        grad_out,
    )


def solution(mesh):
    placed = (
        P("dp", None),
        P("dp", None),
        P(None, "tensor"),
        P(None, "tensor"),
        P(),
        P(None, "tensor"),
        P(None, "tensor"),
        P("tensor"),
        P(),
        P(),
        P("tensor"),
        P("tensor"),
        P("tensor"),
        P(),
        P("tensor"),
        P("tensor", None),
        P("dp", None),
    )
    return jax.shard_map(
        local,
        mesh=mesh,
        in_specs=placed,
        out_specs=(
            P("dp", None),
            P("dp", None),
            P(None, "tensor"),
            P(None, "tensor"),
            P(),
            P(None, "tensor"),
            P(None, "tensor"),
            P("tensor"),
            P(),
            P(),
            P("tensor"),
            P("tensor"),
            P("tensor"),
            P(),
            P("tensor"),
            P("tensor", None),
        ),
        check_vma=False,
    )
```

```python
import functools

import jax
import jax.numpy as jnp
from jax import lax
from jax.experimental import pallas as pl
from jax.experimental.pallas import tpu as pltpu
from jax.sharding import PartitionSpec as P

EPS = 1e-05
MESH_ID = pl.DeviceIdType.MESH


def place():
    dp = lax.axis_index("dp")
    tensor = lax.axis_index("tensor")
    return {"x": dp // 8, "y": (dp // 4) % 2, "z": dp % 4, "t": tensor}


def device_at(at, **moved):
    spot = dict(at, **moved)
    return (spot["x"] * 8 + spot["y"] * 4 + spot["z"], spot["t"])


def dp_peers(at):
    return [
        device_at(at, x=(at["x"] + 1) % 4),
        device_at(at, x=(at["x"] + 3) % 4),
        device_at(at, z=(at["z"] + 1) % 4),
        device_at(at, z=(at["z"] + 3) % 4),
        device_at(at, y=1 - at["y"]),
    ]


def tensor_peers(at):
    return [device_at(at, t=(at["t"] + step) % 4) for step in (1, 2, 3)]


def greet(peers):
    barrier = pltpu.get_barrier_semaphore()
    for peer in peers:
        pl.semaphore_signal(barrier, inc=1, device_id=peer, device_id_type=MESH_ID)


def added(*refs):
    if len(refs) == 2:
        return refs[0][...] + refs[1][...]
    total = refs[0][...].astype(jnp.float32)
    for ref in refs[1:]:
        total = total + ref[...].astype(jnp.float32)
    return total.astype(jnp.bfloat16)


class Staged:
    def __init__(self, send, recv, first):
        self.send, self.recv, self.first = send, recv, first

    def start(self, stage):
        send, recv = self.send.at[self.first + stage], self.recv.at[self.first + stage]
        for src, dst, peer in self.copies(stage):
            if peer is None:
                pltpu.make_async_copy(src, dst, recv).start()
            else:
                pltpu.make_async_remote_copy(
                    src_ref=src, dst_ref=dst, send_sem=send, recv_sem=recv, device_id=peer, device_id_type=MESH_ID
                ).start()

    def finish(self, stage):
        send, recv = self.send.at[self.first + stage], self.recv.at[self.first + stage]
        arrived, sent = self.totals(stage)
        peer = self.copies(stage)[0][2]
        for ref in (sent, arrived):
            copy = pltpu.make_async_remote_copy(
                src_ref=ref, dst_ref=ref, send_sem=send, recv_sem=recv, device_id=peer, device_id_type=MESH_ID
            )
            if ref is sent:
                copy.wait_send()
            if ref is arrived:
                copy.wait_recv()
            if sent is arrived:
                break
        self.settle(stage)


class SumOverDp(Staged):
    stages = 8

    def __init__(self, at, order, buf, res, scratch, sems, across=None, direct=False):
        super().__init__(*sems)
        self.at, self.buf, self.res, self.across, self.direct = at, buf, res, across, direct
        self.ta1, self.ta2, self.tb, self.ty, self.own, self.tt = scratch
        a_axis, b_axis = order
        self.a, self.b = at[a_axis], at[b_axis]
        self.a_up, self.a_down, self.a_far = [(self.a + n) % 4 for n in (1, 3, 2)]
        self.a_right, self.a_left = [device_at(at, **{a_axis: n}) for n in (self.a_up, self.a_down)]
        self.a_others = [(self.a + n) % 4 for n in (1, 2, 3)]
        self.a_peers = [device_at(at, **{a_axis: n}) for n in self.a_others]
        self.b_others = [(self.b + n) % 4 for n in (1, 2, 3)]
        self.b_peers = [device_at(at, **{b_axis: n}) for n in self.b_others]
        self.other = device_at(at, y=1 - at["y"])

    def copies(self, stage):
        buf, res, a, b, own = self.buf, self.res, self.a, self.b, self.own
        near, far = pl.ds(0, 2), pl.ds(2, 2)
        if stage == 0 and self.direct:
            return [(buf.at[i], self.ta1.at[n], peer) for n, (i, peer) in enumerate(zip(self.a_others, self.a_peers))]
        if stage == 6 and self.direct:
            return [(res.at[a], res.at[a], peer) for peer in self.a_peers]
        if stage == 0:
            return [(buf.at[self.a_far, near], self.ta1.at[0], self.a_right), (buf.at[self.a_far, far], self.ta1.at[1], self.a_left)]
        if stage == 1:
            return [(buf.at[self.a_up], self.ta2.at[0], self.a_right), (buf.at[self.a_down], self.ta2.at[1], self.a_left)]
        if stage == 2:
            return [(buf.at[a, j], self.tb.at[n], peer) for n, (j, peer) in enumerate(zip(self.b_others, self.b_peers))]
        if stage == 3:
            return [(buf.at[a, b], self.ty, self.other)]
        if stage == 4:
            return [(own.at[self.across], self.tt.at[self.at["t"]], peer) for peer in tensor_peers(self.at)]
        if stage == 5:
            home = res.at[a, b]
            return [(own, home, peer) for peer in self.b_peers] + [(own, home, None)]
        if stage == 6:
            return [(res.at[a], res.at[a], self.a_right), (res.at[a], res.at[a], self.a_left)]
        return [
            (res.at[self.a_down, near], res.at[self.a_down, near], self.a_right),
            (res.at[self.a_up, far], res.at[self.a_up, far], self.a_left),
        ]

    def totals(self, stage):
        res, a = self.res, self.a
        if stage == 5:
            return res.at[a], res.at[a, pl.ds(0, 3)]
        if stage == 6:
            both = res.at[pl.ds(0, 3 if self.direct else 2)]
        elif stage == 7:
            both = res.at[0]
        elif stage == 4:
            both = self.tt.at[pl.ds(0, 3)]
        else:
            both = (self.ta1, self.ta2, self.tb, self.ty)[stage]
        return both, both

    def settle(self, stage):
        buf, a, b, own = self.buf, self.a, self.b, self.own
        if stage == 0 and self.direct:
            for j in range(4):
                buf[a, j] = added(buf.at[a, j], *(self.ta1.at[n, j] for n in range(3)))
        elif stage == 0:
            for j in range(2):
                buf[self.a_up, j] = added(buf.at[self.a_up, j], self.ta1.at[0, j])
                buf[self.a_down, 2 + j] = added(buf.at[self.a_down, 2 + j], self.ta1.at[1, j])
        elif stage == 1:
            for j in range(4):
                buf[a, j] = added(buf.at[a, j], self.ta2.at[0, j], self.ta2.at[1, j])
        elif stage == 2:
            buf[a, b] = added(buf.at[a, b], *(self.tb.at[n] for n in range(3)))
        elif stage == 3:
            own[...] = added(buf.at[a, b], self.ty)
        elif stage == 4:
            self.tt[self.at["t"]] = own[self.across]
            own[self.across] = added(*(self.tt.at[n] for n in range(4)))


DP_SEMS = SumOverDp.stages


def dp_scratch(rows, width, across=16, direct=False):
    first = [(3, 4, rows, width), (1, 16, width)] if direct else [(2, 2, rows, width), (2, 4, rows, width)]
    shapes = first + [(3, rows, width), (rows, width), (rows, width), (4, across, width)]
    return [pltpu.VMEM(shape, jnp.bfloat16) for shape in shapes]


class SumOverTensor(Staged):
    stages = 4

    def __init__(self, at, rows, buf, res, scratch, sems, ending):
        super().__init__(*sems)
        self.buf, self.res, self.rows, self.ending = buf, res, rows, ending
        self.t0, self.t1 = scratch
        self.c, self.h = at["t"] % 2, at["t"] // 2
        self.sibling = device_at(at, t=self.h * 2 + 1 - self.c)
        self.partner = device_at(at, t=(1 - self.h) * 2 + self.c)

    def copies(self, stage):
        buf, res, c, h, rows = self.buf, self.res, self.c, self.h, self.rows
        if stage == 0:
            return [(buf.at[1 - c, :, rows], self.t0.at[:, rows], self.sibling)]
        if stage == 1:
            return [(buf.at[c, 1 - h, rows], self.t1.at[rows], self.partner)]
        if stage == 2:
            mine, theirs = buf.at[c, h, rows], res.at[c, h, rows]
            return [(mine, theirs, self.partner), (mine, theirs, None)]
        return [(res.at[c, :, rows], res.at[c, :, rows], self.sibling)]

    def totals(self, stage):
        res, c, h, rows = self.res, self.c, self.h, self.rows
        if stage == 2:
            return res.at[c, :, rows], res.at[c, h, rows]
        both = (self.t0.at[:, rows], self.t1.at[rows], None, res.at[c, :, rows])[stage]
        return both, both

    def settle(self, stage):
        buf, c, h, rows = self.buf, self.c, self.h, self.rows
        if stage == 0:
            for n in range(2):
                buf[c, n, rows] = added(buf.at[c, n, rows], self.t0.at[n, rows])
        elif stage == 1:
            total = buf[c, h, rows].astype(jnp.float32) + self.t1[rows].astype(jnp.float32)
            buf[c, h, rows] = self.ending(total, rows)


TENSOR_SEMS = SumOverTensor.stages


class SumState(Staged):
    stages = 8

    def __init__(self, at, buf, res, scratch, sems):
        super().__init__(*sems)
        self.buf, self.res = buf, res
        self.t0, self.ta, self.tb, self.ty, self.tt, self.own = scratch
        x, y, z, t = at["x"], at["y"], at["z"], at["t"]
        c = t % 2
        self.c, self.a, self.b = c, x * (1 - c) + z * c, z * (1 - c) + x * c
        self.sibling = device_at(at, t=t // 2 * 2 + 1 - c)
        self.partner = device_at(at, t=(1 - t // 2) * 2 + c)
        self.other = device_at(at, y=1 - y)
        self.a_peers = [device_at(at, x=(x + n * (1 - c)) % 4, z=(z + n * c) % 4) for n in (1, 2, 3)]
        self.b_peers = [device_at(at, x=(x + n * c) % 4, z=(z + n * (1 - c)) % 4) for n in (1, 2, 3)]

    def copies(self, stage):
        buf, res, a, b, c, own = self.buf, self.res, self.a, self.b, self.c, self.own
        if stage == 0:
            return [(buf.at[1 - c], self.t0, self.sibling)]
        if stage == 1:
            return [(buf.at[c, (a + n + 1) % 4], self.ta.at[n], peer) for n, peer in enumerate(self.a_peers)]
        if stage == 2:
            return [(buf.at[c, a, (b + n + 1) % 4], self.tb.at[n], peer) for n, peer in enumerate(self.b_peers)]
        if stage == 3:
            return [(buf.at[c, a, b], self.ty, self.other)]
        if stage == 4:
            return [(own, self.tt, self.partner)]
        if stage == 5:
            return [(own, res.at[c, a, b], peer) for peer in self.b_peers] + [(own, res.at[c, a, b], None)]
        if stage == 6:
            return [(res.at[c, a], res.at[c, a], peer) for peer in self.a_peers]
        return [(res.at[c], res.at[c], self.sibling)]

    def totals(self, stage):
        res, a, c = self.res, self.a, self.c
        if stage == 5:
            return res.at[c, a], res.at[c, a, pl.ds(0, 3)]
        if stage == 6:
            both = res.at[c, pl.ds(0, 3)]
        elif stage == 7:
            both = res.at[c]
        else:
            both = (self.t0, self.ta, self.tb, self.ty, self.tt)[stage]
        return both, both

    def settle(self, stage):
        buf, a, b, c = self.buf, self.a, self.b, self.c
        if stage == 0:
            for i in range(4):
                for j in range(4):
                    buf[c, i, j] = added(buf.at[c, i, j], self.t0.at[i, j])
        elif stage == 1:
            for j in range(4):
                buf[c, a, j] = added(buf.at[c, a, j], *(self.ta.at[n, j] for n in range(3)))
        elif stage == 2:
            buf[c, a, b] = added(buf.at[c, a, b], *(self.tb.at[n] for n in range(3)))
        elif stage == 3:
            self.own[...] = added(buf.at[c, a, b], self.ty)
        elif stage == 4:
            self.own[...] = added(self.own, self.tt)


STATE_SEMS = SumState.stages


def state_scratch(rows, width):
    block = (rows, width)
    shapes = [(4, 4) + block, (3, 4) + block, (3,) + block, block, block, block]
    return [pltpu.VMEM(shape, jnp.bfloat16) for shape in shapes]


def wide(tile, count=6):
    return jnp.concatenate([tile] * count, axis=1)


def mul(left, right):
    return jnp.dot(left, right, preferred_element_type=jnp.float32)


def mul_nt(left, right):
    return lax.dot_general(left, right, (((1,), (1,)), ((), ())), preferred_element_type=jnp.float32)


def mul_tn(left, right):
    return lax.dot_general(left, right, (((0,), (0,)), ((), ())), preferred_element_type=jnp.float32)


def low(value):
    return value.astype(jnp.bfloat16)


def iota(shape, dim):
    return lax.broadcasted_iota(jnp.int32, shape, dim)


def in_three(value):
    high = low(value).astype(jnp.float32)
    rest = value - high
    middle = low(rest).astype(jnp.float32)
    lane = iota(value.shape, 1)
    return low(jnp.where(lane < 16, high, jnp.where(lane < 32, middle, rest - middle)))


def exact_sum(ones, value):
    high = low(value)
    rest = value - high.astype(jnp.float32)
    middle = low(rest)
    return mul(ones, high) + mul(ones, middle) + mul(ones, low(rest - middle.astype(jnp.float32)))


def softplus(value):
    return jnp.maximum(value, 0.0) + jnp.log1p(jnp.exp(-jnp.abs(value)))


def sigmoid(value):
    return 1.0 / (1.0 + jnp.exp(-value))


def columns_of_segments(seg_ref, segc):
    segc[0:8, :] = jnp.full((8, 128), -1.0, jnp.float32)
    segc[1032:1040, :] = jnp.full((8, 128), -1.0, jnp.float32)

    def fill(k, carry):
        row = jnp.broadcast_to(seg_ref[:, pl.ds(pl.multiple_of(k * 128, 128), 128)].astype(jnp.float32), (128, 128))
        segc[pl.ds(pl.multiple_of(8 + k * 128, 8), 128), :] = row.T
        return carry

    lax.fori_loop(0, 8, fill, 0)


def kept(segc, start):
    around = segc[pl.ds(start, 144), :]
    here = around[8:, :]
    return [(pltpu.roll(around, lag, 0)[8:, :] == here).astype(jnp.float32) for lag in (1, 2, 3)]


def lagged(padded, start, keeps):
    around = padded[pl.ds(start, 136), :]
    count = around.shape[1] // 128
    return [around[8:, :]] + [pltpu.roll(around, lag, 0)[8:, :] * wide(keep[:128], count) for lag, keep in zip((1, 2, 3), keeps)]


def convolved(shifted, taps):
    total = taps[4:5, :] + taps[0:1, :] * shifted[0]
    for lag in (1, 2, 3):
        total = total + taps[lag : lag + 1, :] * shifted[lag]
    return total


def decay(k, start, segc, seg_ref, step_raw, heads):
    rows = pl.ds(start, 128)
    step = softplus(step_raw[rows, :] + heads[0:1, :])
    tri = (iota((128, 128), 0) >= iota((128, 128), 1)).astype(jnp.bfloat16)
    cum = exact_sum(tri, step * heads[1:2, :])
    seg_column = segc[pl.ds(start + 8, 128), :]
    seg_row = seg_ref[:, rows].astype(jnp.float32)
    before = segc[pl.ds(start, 8), :][7:8, :]
    last = seg_column[127:128, :]
    growth = jnp.exp(cum)
    tail = jnp.exp(cum[127:128, :] - cum) * (seg_column == last).astype(jnp.float32)
    return step, cum, seg_column, seg_row, before, last, growth, tail


def expansion():
    row, column = iota((128, 768), 0), iota((128, 768), 1)
    return ((row < 48) & (row % 16 == column // 64)).astype(jnp.bfloat16)


def head_sums(value, expand):
    return mul_nt(low(value), expand)


def slope(pre, sig):
    return sig * (1.0 + pre * (1.0 - sig))


def middle_block(k, total, kept_act, bent, gated_ref, pulled, acc_v):
    rows = pl.ds(pl.multiple_of(k * 128, 128), 128)
    columns = jnp.concatenate([total] * 16, 0).T
    scale = lax.rsqrt(columns[:, 0:1] / 3072 + EPS)
    pull = columns[:, 1:2] * scale * scale * scale / 3072
    gated, q, act, bend = [
        value.astype(jnp.float32) for value in (gated_ref[rows, :], pulled[rows, :], kept_act[...], bent[rows, :])
    ]
    scaled = gated * scale
    acc_v[5:6, :] += jnp.sum(q * scaled, 0, keepdims=True)
    grad_gated = scale * q - gated * pull
    pulled[rows, :] = low(grad_gated * act)
    bent[rows, :] = low(grad_gated * bend)
    return rows, scaled


def put(buf, i, value):
    pieces = low(value.reshape(4, value.shape[0] // 4, 768))
    for stream in range(2):
        buf[stream, i] = pieces[..., stream * 384 : (stream + 1) * 384]


def backward_block(
    k, vpad, spad, step_raw, seg_ref, segc, taps, state_taps, heads, expand, bypass, states, dy,
    dstate, du, dus, head_rows, value_low, state_low, step_low, acc_v, acc_s, acc_h, between,
):
    start = pl.multiple_of(k * 128, 128)
    rows = pl.ds(start, 128)
    keeps = kept(segc, start)
    values = lagged(vpad, start, keeps)
    pre = convolved(values, taps)
    sig = sigmoid(pre)
    x = pre * sig
    state_values = lagged(spad, start, keeps)
    state_pre = convolved(state_values, state_taps)
    state_sig = sigmoid(state_pre)
    state = low(state_pre * state_sig)
    b_in, c_out = state[:, :128], state[:, 128:]
    step, cum, seg_column, seg_row, before, last, growth, tail = decay(k, start, segc, seg_ref, step_raw, heads)
    spread = mul(jnp.concatenate([in_three(step), in_three(growth), in_three(tail)], 0), expand[...])
    step_wide, tail_wide = spread[:128], spread[256:]
    growth_wide = spread[128:256] * wide((seg_column == before).astype(jnp.float32))
    through = spread[255:256] * wide((last == before).astype(jnp.float32))
    xs = x * step_wide
    entering = states[k]
    grad_state = dstate[...]
    grad_state_low = low(grad_state)
    dyk = dy[rows, :].astype(jnp.float32)
    grown = low(dyk * growth_wide)
    outside = mul(c_out, entering) * growth_wide
    dxs_after = mul(b_in, grad_state_low) * tail_wide
    grad_c = mul_nt(grown, entering)
    grad_b = mul_nt(low(xs * tail_wide), grad_state_low)
    end = jnp.sum(entering.astype(jnp.float32) * grad_state, 0, keepdims=True) * through
    dstate[...] = through * grad_state + mul_tn(c_out, grown)
    scores = mul_nt(b_in, c_out)
    row, column = iota((128, 128), 0), iota((128, 128), 1)
    bias = jnp.where((seg_column == seg_row) & (row <= column), 0.0, -1e30)
    tri = (row >= column).astype(jnp.bfloat16)
    strict = row < column
    cum_rows = cum.T
    first = column < 64
    grad_scores = jnp.zeros((128, 128), jnp.float32)
    own_steps = jnp.zeros((128, 128), jnp.float32)
    inside = []
    between(1)
    for pair in range(6):
        lanes = slice(pair * 128, (pair + 1) * 128)
        own = dyk[:, lanes]
        both = low(jnp.concatenate([jnp.where(first, own, 0.0), jnp.where(first, 0.0, own)], 0))
        grad_weights = mul_nt(low(x[:, lanes]), both)
        weights, moved, steps = [], [], []
        for side in range(2):
            h = 2 * pair + side
            faded = jnp.exp(cum_rows[h : h + 1, :] - cum[:, h : h + 1] + bias)
            pulled = grad_weights[:, side * 128 : (side + 1) * 128] * faded
            steps.append(step[:, h : h + 1])
            grad_scores = grad_scores + pulled * steps[side]
            moved.append(low(pulled * scores))
            weights.append(low(scores * faded))
        inside.append(mul(jnp.concatenate(weights, 1), both))
        later = mul(jnp.concatenate(moved, 0), tri)
        for side in range(2):
            h = 2 * pair + side
            part = later[side * 128 : (side + 1) * 128]
            own_steps = jnp.where(column == h, part[:, 0:1], own_steps)
            head_rows[h : h + 1, :] = jnp.sum(jnp.where(strict, part * steps[side], 0.0), 0, keepdims=True)
    between(2)
    grad_scores = low(grad_scores)
    grad_b = grad_b + mul(grad_scores, c_out)
    grad_c = grad_c + mul_tn(grad_scores, b_in)
    dxs = jnp.concatenate(inside, 1) + dxs_after
    dx = dxs * step_wide + bypass * dyk
    summed = head_sums(jnp.concatenate([dyk * outside, x * dxs_after], 0), expand[...])
    end = head_sums(jnp.broadcast_to(end, (16, 768)), expand[...])
    upper = (row <= column).astype(jnp.bfloat16)
    below = (row > column).astype(jnp.bfloat16)
    grad_decay = exact_sum(upper, summed[:128]) + exact_sum(below, step * summed[128:]) + end[0:1, :] + head_rows[...].T
    grad_step = own_steps + summed[128:] + heads[1:2, :] * grad_decay
    grad_raw = grad_step * sigmoid(step_raw[rows, :] + heads[0:1, :])
    step_low[rows, :] = low(jnp.where(column < 16, grad_raw, 0.0))
    acc_h[0:1, :] += jnp.sum(grad_raw, 0, keepdims=True)
    acc_h[1:2, :] += jnp.sum(step * grad_decay, 0, keepdims=True) * heads[1:2, :]
    between(3)
    for grad, grads, shifted, taps_ref, acc, result in (
        (dx * slope(pre, sig), du, values, taps, acc_v, value_low),
        (jnp.concatenate([grad_b, grad_c], 1) * slope(state_pre, state_sig), dus, state_values, state_taps, acc_s, state_low),
    ):
        grads[128:136, :] = grads[0:8, :]
        grads[0:128, :] = grad
        for lag in range(4):
            acc[lag : lag + 1, :] += jnp.sum(grad * shifted[lag], 0, keepdims=True)
        acc[4:5, :] += jnp.sum(grad, 0, keepdims=True)
        around = grads[...]
        count = around.shape[1] // 128
        total = grad * taps_ref[0:1, :]
        for lag, keep in zip((1, 2, 3), keeps):
            total = total + taps_ref[lag : lag + 1, :] * pltpu.roll(around * wide(keep, count), 136 - lag, 0)[:128, :]
        result[rows, :] = low(total)
    acc_v[6:7, :] += jnp.sum(dyk * x, 0, keepdims=True)


def put_small(small, acc_v, acc_h, step_grad):
    small[...] = jnp.zeros_like(small)
    rows = [acc_v[n : n + 1, j * 128 : (j + 1) * 128] for n in range(7) for j in range(6)] + [acc_h[0:1, :], acc_h[1:2, :]]
    place_in = iota((16, 128), 0)
    for j in range(12):
        block = jnp.where(place_in < 12, step_grad[:, j * 128 : (j + 1) * 128], 0.0)
        for n, row in enumerate(rows[4 * j : 4 * j + 4]):
            block = jnp.where(place_in == 12 + n, row, block)
        small[j // 4, j % 4] = low(block)


def put_shared(shared, acc_s, acc_n):
    shared[...] = jnp.zeros_like(shared)
    place_in = iota((16, 128), 0)
    for j, rows in enumerate(
        (
            [acc_n[:, n * 128 : (n + 1) * 128] for n in range(12)],
            [acc_s[n : n + 1, j * 128 : (j + 1) * 128] for n in range(5) for j in range(2)],
        )
    ):
        block = jnp.zeros((16, 128), jnp.float32)
        for n, row in enumerate(rows):
            block = jnp.where(place_in == n, row, block)
        shared[0, j] = low(block)


BRANCH_PLANS = {}
OUT_PLANS = {3: ("g0>",)}
VALUE_PLANS = {}
STATE_PLANS = {3: ("o1>",)}
SCAN_PLANS = (
    {4: ("g2>",), 6: ("o0>", "b1>"), 7: ("g4>",)},
    {},
    {0: ("b0>",), 2: ("g1>",), 4: ("o0",), 5: ("g3>",)},
    {},
)
DX_PLANS = ({3: ("g5>", "b2>")}, {0: ("v0>",), 1: ("o2>",), 3: ("d0>", "g6.", "o3>", "b3.")})
TAIL = (
    "v1>", "e0>", "s0>", "o4>", "d1>", "v2>", "s1>", "s2>", "o5>", "v3>", "s3>", "e1>",
    "s4>", "o6.", "v4>", "d2>", "s5>", "d3.", "e2>", "s6>", "e3.", "v5>", "s7.", "v6.",
)
RING = (0, 1, 2, 3, 5, 6, 7)


def head_row(values, lane, group):
    row = jnp.zeros(lane.shape, jnp.float32)
    for h in range(12):
        row = jnp.where(group(lane, h), values[h], row)
    return row


def layer_kernel(
    remote,
    tokens, cot_in, w_gate_in, w_value_in, w_state_in, w_out_in,
    seg, w_step_in, value_conv, value_bias, state_conv, state_bias, norm_gain, gated_gain, step_bias, log_rate, bypass_gain,
    res_gate, res_out, res_value, res_state, res_small, res_shared, res_branch, res_dx,
    normed, gate, y_ref, q_ref, vpad, spad, state_low, step_low, step_raw, segc, states, carried, du, dus, head_rows,
    acc_v, acc_s, acc_h, acc_n, taps, state_taps, heads, expand, gains,
    w_gate, w_value, w_state, w_step, w_out, cot, sums, landed,
    sum_gate, sum_out, sum_value, sum_state, small, shared, branch,
    *rest,
):
    scratch = [rest[n * 6 : (n + 1) * 6] for n in range(7)]
    value_scratch = [
        (early[0], own_ta2, early[2], own_ty, *early[4:])
        for early, own_ta2, own_ty in zip(scratch[0:2], rest[42:44], rest[44:46])
    ]
    branch_scratch = rest[46:48]
    own_tokens, own_cot, send, recv, local = rest[48:]
    at = place()
    dx = cot
    slots = branch.at[0]

    def fetch(k):
        return pltpu.make_async_copy(tokens.at[pl.ds(pl.multiple_of(k * 256, 256), 256)], slots.at[k % 2], local.at[k % 2])

    loads = [
        pltpu.make_async_copy(src, dst, local.at[2 + n])
        for n, (src, dst) in enumerate(
            (
                (w_gate_in, w_gate),
                (w_value_in, w_value),
                (w_state_in, w_state),
                (cot_in, cot),
                (w_out_in, w_out),
                (tokens.at[pl.ds(pl.multiple_of((at["t"] % 2 * 2 + at["t"] // 2) * 256, 256), 256)], own_tokens),
                (cot_in.at[at["t"] % 2, at["t"] // 2], own_cot),
            )
        )
    ]
    fetch(0).start()
    for cp in loads[:3]:
        cp.start()
    friends = dp_peers(at) + tensor_peers(at)
    if remote:
        greet(friends)

    orders = (("x", "z"), ("z", "x"))

    def pair(first, buf, res, scratch):
        return [
            (SumOverDp(at, order, buf.at[n], res.at[n], scratch[n], (send, recv, (first + n) * DP_SEMS)), RING)
            for n, order in enumerate(orders)
        ]

    last = 8 * DP_SEMS + STATE_SEMS
    dx_scratch = (w_out.at[pl.ds(0, 2)], w_out.at[2])
    upper, lower, all_rows = pl.ds(0, 128), pl.ds(128, 128), pl.ds(0, 256)

    def mixed_rows(total, rows):
        return low(own_tokens[rows].astype(jnp.float32) + total)

    def token_gradient(total, rows):
        hidden = own_tokens[rows].astype(jnp.float32)
        inverse = lax.rsqrt(jnp.sum(hidden * hidden, 1, keepdims=True) / 1536 + EPS)
        scaled = total * gains[0:1, :]
        along = jnp.sum(scaled * hidden, 1, keepdims=True) * (inverse * inverse * inverse / 1536)
        return low(own_cot[rows].astype(jnp.float32) + inverse * scaled - hidden * along)

    def over_tensor(n, rows, buf, res, scratch, ending):
        return [(SumOverTensor(at, rows, buf, res, scratch, (send, recv, last + n * TENSOR_SEMS), ending), range(4))]

    engines = {
        "g": pair(0, sum_gate, res_gate, scratch[0:2]),
        "o": pair(2, sum_out, res_out, scratch[2:4]),
        "v": pair(4, sum_value, res_value, value_scratch)
        + [(SumOverDp(at, orders[0], small, res_small, scratch[4], (send, recv, 6 * DP_SEMS)), RING)],
        "s": [
            (SumState(at, sum_state, res_state, scratch[6], (send, recv, 8 * DP_SEMS)), range(8)),
            (
                SumOverDp(at, orders[0], shared, res_shared, scratch[5], (send, recv, 7 * DP_SEMS), pl.ds(0, 16), True),
                (None, 0, 2, 3, 4, 5, 6, None),
            ),
        ],
        "b": over_tensor(0, all_rows, branch, res_branch, branch_scratch, mixed_rows),
        "d": over_tensor(1, upper, dx, res_dx, dx_scratch, token_gradient),
        "e": over_tensor(2, lower, dx, res_dx, dx_scratch, token_gradient),
    }

    def act(*plan):
        if not remote:
            return
        for word in plan:
            step = int(word[1])
            if word[2:]:
                for engine, stages in engines[word[0]]:
                    if stages[step] is not None:
                        engine.finish(stages[step])
                step += 1
            if word[2:] != ".":
                for engine, stages in engines[word[0]]:
                    if stages[step] is not None:
                        engine.start(stages[step])

    def act_at(i, plans):
        for n, plan in plans.items():

            @pl.when(i == n)
            def _():
                act(*plan)

    for ref in (du, dus, head_rows, carried, acc_v, acc_s, acc_h, acc_n, taps, state_taps, gains):
        ref[...] = jnp.zeros_like(ref)
    vpad[0:8, :] = jnp.zeros((8, 768), jnp.float32)
    spad[0:8, :] = jnp.zeros((8, 256), jnp.float32)
    columns_of_segments(seg, segc)
    taps[0:4, :] = value_conv[...]
    taps[4:5, :] = value_bias[...].reshape(1, 768)
    state_taps[0:4, :] = state_conv[...]
    state_taps[4:5, :] = state_bias[...].reshape(1, 256)
    lane = iota((8, 128), 1)
    heads[...] = head_row(step_bias, lane, lambda l, h: (l % 16 == h) & (l < 48))
    rate = head_row(log_rate, lane, lambda l, h: (l % 16 == h) & (l < 48))
    heads[1:2, :] = jnp.where((lane % 16 < 12) & (lane < 48), -jnp.exp(rate), 0.0)[0:1]
    gains[0:1, :] = norm_gain[...].reshape(1, 1536)
    gains[1:2, 0:768] = gated_gain[...].reshape(1, 768)
    gains[2:3, 0:768] = head_row(bypass_gain, iota((1, 768), 1), lambda l, h: l // 64 == h)
    expand[...] = expansion()
    chosen = ((iota((12, 128), 1) % 16 == iota((12, 128), 0)) & (iota((12, 128), 1) < 48)).astype(jnp.bfloat16)
    w_step[...] = low(mul_tn(chosen, w_step_in[...]))
    for cp in loads[:3]:
        cp.wait()
    for cp in loads[3:]:
        cp.start()

    def project(k, carry):
        rows = pl.ds(pl.multiple_of(k * 256, 256), 256)
        padded = pl.ds(pl.multiple_of(8 + k * 256, 8), 256)

        @pl.when(k < 3)
        def _():
            fetch(k + 1).start()

        fetch(k).wait()
        hidden = slots[k % 2].astype(jnp.float32)
        inverse = lax.rsqrt(jnp.sum(hidden * hidden, 1, keepdims=True) / 1536 + EPS)
        normal = low(hidden * inverse * gains[0:1, :])
        normed[rows, :] = normal
        gate[rows, :] = low(mul(normal, w_gate[...]))
        vpad[padded, :] = mul(normal, w_value[...])
        spad[padded, :] = mul(normal, w_state[...])
        step_raw[rows, :] = mul_nt(normal, w_step[...])
        return carry

    lax.fori_loop(0, 4, project, 0)
    for cp in loads[3:]:
        cp.wait()

    def project_back(k, carry):
        rows = pl.ds(pl.multiple_of(k * 256, 256), 256)
        q_ref[rows, :] = low(mul_nt(cot[k // 2, k % 2], w_out[...].reshape(768, 1536)) * gains[1:2, 0:768])
        return carry

    lax.fori_loop(0, 4, project_back, 0)

    def act_of(k):
        rows, columns = pl.ds(k // 2 % 2 * 128, 128), pl.ds(pl.multiple_of(k % 2 * 768, 128), 768)
        return branch.at[1, k // 4, rows, columns]

    def forward_block(k, carry):
        start = pl.multiple_of(k * 128, 128)
        rows = pl.ds(start, 128)
        keeps = kept(segc, start)
        pre = convolved(lagged(vpad, start, keeps), taps)
        x = pre * sigmoid(pre)
        pre = convolved(lagged(spad, start, keeps), state_taps)
        state = low(pre * sigmoid(pre))
        b_in, c_out = state[:, :128], state[:, 128:]
        step, cum, seg_column, seg_row, before, last, growth, tail = decay(k, start, segc, seg, step_raw, heads)
        spread = mul(jnp.concatenate([in_three(step), in_three(growth), in_three(tail)], 0), expand[...])
        xs = x * spread[:128]
        start_keep = (seg_column == before).astype(jnp.float32)
        entering = carried[...]
        states[k] = low(entering)
        outside = mul(c_out, low(entering)) * (spread[128:256] * wide(start_keep))
        through = spread[255:256] * wide((last == before).astype(jnp.float32))
        carried[...] = through * entering + mul_tn(b_in, low(xs * spread[256:]))
        scores = mul_nt(c_out, b_in)
        bias = jnp.where((seg_column == seg_row) & (iota((128, 128), 0) >= iota((128, 128), 1)), 0.0, -1e30)
        cum_rows = cum.T
        first = iota((128, 128), 1) < 64
        inside = []
        for pair in range(6):
            own = xs[:, pair * 128 : (pair + 1) * 128]
            right = low(jnp.concatenate([jnp.where(first, own, 0.0), jnp.where(first, 0.0, own)], 0))
            left = [
                low(scores * jnp.exp(cum[:, h : h + 1] - cum_rows[h : h + 1, :] + bias)) for h in (2 * pair, 2 * pair + 1)
            ]
            inside.append(mul(jnp.concatenate(left, 1), right))
        y = jnp.concatenate(inside, 1) + outside + gains[2:3, 0:768] * x
        raw = gate[rows, :].astype(jnp.float32)
        sig = sigmoid(raw)
        act = raw * sig
        gated = y * act
        y_ref[rows, :] = low(gated)
        gate[rows, :] = low(y * slope(raw, sig))
        act_of(k)[...] = low(act)
        squares = jnp.sum(gated * gated, 1, keepdims=True)
        cross = jnp.sum(q_ref[rows, :].astype(jnp.float32) * gated, 1, keepdims=True)
        lanes = iota((128, 128), 1)
        sums[k] = jnp.where(lanes == 0, squares, jnp.where(lanes == 1, cross, 0.0)).T[0:8, :]
        return carry

    def exchange(half):
        blocks, first = pl.ds(4 * half, 4), last + 3 * TENSOR_SEMS + 3 * half
        copies = [
            pltpu.make_async_remote_copy(
                src_ref=sums.at[blocks],
                dst_ref=landed.at[at["t"], blocks],
                send_sem=send.at[first + n],
                recv_sem=recv.at[first + n],
                device_id=peer,
                device_id_type=MESH_ID,
            )
            for n, peer in enumerate(tensor_peers(at))
        ]
        if not remote:
            for n in range(4):
                landed[n, blocks] = sums[blocks] * 0.75
            return []
        for cp in copies:
            cp.start()
        landed[at["t"], blocks] = sums[blocks]
        return copies

    def middle(k, carry):
        total = (landed[0, k] + landed[1, k]) + (landed[2, k] + landed[3, k])
        rows, scaled = middle_block(k, total, act_of(k), gate, y_ref, q_ref, acc_v)
        y_ref[rows, :] = low(scaled * gains[1:2, 0:768])
        return carry

    lax.fori_loop(0, 4, forward_block, 0)
    if remote:
        pl.semaphore_wait(pltpu.get_barrier_semaphore(), len(friends))
    first_sums = exchange(0)
    lax.fori_loop(4, 8, forward_block, 0)
    second_sums = exchange(1)
    for cp in first_sums:
        cp.wait()
    lax.fori_loop(0, 4, middle, 0)
    for cp in second_sums:
        cp.wait()
    lax.fori_loop(4, 8, middle, 0)
    acc_v[5:6, :] = acc_v[5:6, :] / gains[1:2, 0:768]
    gate_low, gate_normed, dy = gate, y_ref, q_ref
    value_low = y_ref

    def gate_weights(i, carry):
        put(sum_gate, i, mul_tn(normed[:, pl.ds(pl.multiple_of(i * 384, 128), 384)], gate_low[...]))
        return carry

    def out_weights(i, carry):
        out_rows = pl.ds(pl.multiple_of((i % 2) * 384, 128), 384)
        out_columns = pl.ds(pl.multiple_of((i // 2) * 768, 128), 768)
        put(sum_out, i, mul_tn(gate_normed[:, out_rows], cot[:, :, :, out_columns].reshape(1024, 768)))
        act_at(i, OUT_PLANS)
        return carry

    def branch_rows(i, carry):
        rows = pl.ds(pl.multiple_of(i * 256, 256), 256)
        branch[i // 2, i % 2] = low(mul(gate_normed[rows, :], w_out[...].reshape(768, 1536)))
        act_at(i, BRANCH_PLANS)
        return carry

    lax.fori_loop(0, 4, gate_weights, 0)
    act("g0")
    lax.fori_loop(0, 4, branch_rows, 0)
    act("b0")
    lax.fori_loop(0, 4, out_weights, 0)
    carried[...] = jnp.zeros((128, 768), jnp.float32)

    def scan(i, carry):
        act_at(i, SCAN_PLANS[0])
        backward_block(
            7 - i, vpad, spad, step_raw, seg, segc, taps, state_taps, heads, expand, gains[2:3, 0:768], states, dy,
            carried, du, dus, head_rows, value_low, state_low, step_low, acc_v, acc_s, acc_h,
            lambda point: act_at(i, SCAN_PLANS[point]),
        )
        return carry

    lax.fori_loop(0, 8, scan, 0)

    def value_weights(i, carry):
        put(sum_value, i, mul_tn(normed[:, pl.ds(pl.multiple_of(i * 384, 128), 384)], value_low[...]))
        act_at(i, VALUE_PLANS)
        return carry

    def state_weights(i, carry):
        thirds = [
            mul_tn(normed[:, pl.ds(pl.multiple_of(q * 512 + i * 128, 128), 128)], state_low[...]) for q in range(3)
        ]
        put(sum_state, i, jnp.concatenate(thirds, 1))
        act_at(i, STATE_PLANS)
        return carry

    lax.fori_loop(0, 4, value_weights, 0)
    put_small(small, acc_v, acc_h, mul_tn(step_low[...], normed[...])[0:16, :])
    act("v0")
    lax.fori_loop(0, 4, state_weights, 0)

    def dx_rows(half, i):
        firsts = [pl.ds(pl.multiple_of((i // 2 * 2 + n) * 256 + half * 128, 128), 128) for n in range(2)]
        columns = pl.ds(pl.multiple_of(i % 2 * 768, 128), 768)

        def both(ref, *lanes):
            return jnp.concatenate([ref[(rows, *lanes)] for rows in firsts], 0)

        part = mul_nt(both(gate_low), w_gate[columns, :]) + mul_nt(both(value_low), w_value[columns, :])
        part = part + mul_nt(both(state_low), w_state[columns, :]) + mul(both(step_low), w_step[:, columns])
        for n in range(2):
            dx[i // 2, n, half * 128 : half * 128 + 128, columns] = low(part[n * 128 : n * 128 + 128])
        acc_n[0:1, columns] += jnp.sum(part * both(normed, columns).astype(jnp.float32), 0, keepdims=True)
        act_at(i, DX_PLANS[half])

    for half in range(2):

        def dx_half(i, carry):
            dx_rows(half, i)
            return carry

        lax.fori_loop(0, 4, dx_half, 0)
        act("de"[half] + "0")
    put_shared(shared, acc_s, acc_n[0:1, :] / gains[0:1, :])
    act("s0", *TAIL)
    if not remote:
        results = (res_gate, res_out, res_value, res_state, res_small, res_shared, res_branch, res_dx)
        copies = [
            pltpu.make_async_copy(src, dst, local.at[n])
            for n, (src, dst) in enumerate(zip((sum_gate, sum_out, sum_value, sum_state, small, shared, branch, dx), results))
        ]
        for cp in copies:
            cp.start()
        for cp in copies:
            cp.wait()


def layer(*operands, remote=True):
    f32, bf16 = jnp.float32, jnp.bfloat16
    weight, rows = (2, 4, 4, 96, 384), (2, 2, 256, 1536)
    outs = [weight, weight, weight, (2, 4, 4, 32, 384), (4, 4, 16, 128), (4, 4, 16, 128), rows, rows]
    scratch = [
        ((1024, 1536), bf16), ((1024, 768), bf16), ((1024, 768), bf16), ((1024, 768), bf16), ((1032, 768), f32),
        ((1032, 256), f32), ((1024, 256), bf16), ((1024, 128), bf16), ((1024, 128), f32),
        ((1040, 128), f32), ((8, 128, 768), bf16), ((128, 768), f32), ((136, 768), f32), ((136, 256), f32), ((128, 128), f32),
        ((8, 768), f32), ((8, 256), f32), ((8, 128), f32), ((8, 1536), f32), ((8, 768), f32), ((8, 256), f32),
        ((8, 128), f32), ((128, 768), bf16), ((8, 1536), f32),
        ((1536, 768), bf16), ((1536, 768), bf16), ((1536, 256), bf16), ((128, 1536), bf16), ((3, 256, 1536), bf16),
        (rows, bf16), ((8, 8, 128), f32), ((4, 8, 8, 128), f32),
    ] + [(shape, bf16) for shape in outs[:7]]
    vmem, hbm, smem = [pl.BlockSpec(memory_space=space) for space in (pltpu.VMEM, pl.ANY, pltpu.SMEM)]
    count = 8 * DP_SEMS + STATE_SEMS + 3 * TENSOR_SEMS + 6
    return pl.pallas_call(
        functools.partial(layer_kernel, remote),
        out_shape=[jax.ShapeDtypeStruct(shape, bf16) for shape in outs],
        in_specs=[hbm] * 6 + [vmem] * 8 + [smem] * 3,
        out_specs=[hbm] * 8,
        scratch_shapes=[pltpu.VMEM(shape, kind) for shape, kind in scratch]
        + dp_scratch(96, 384) * 4
        + dp_scratch(16, 128)
        + dp_scratch(16, 128, 16, True)
        + state_scratch(32, 384)
        + [pltpu.VMEM((2, 4, 96, 384), bf16)] * 2
        + [pltpu.VMEM((96, 384), bf16)] * 2
        + [pltpu.VMEM((2, 256, 1536), bf16)] + [pltpu.VMEM((256, 1536), bf16)] * 3
        + [pltpu.SemaphoreType.DMA((count,)), pltpu.SemaphoreType.DMA((count,)), pltpu.SemaphoreType.DMA((9,))],
        compiler_params=pltpu.CompilerParams(
            collective_id=0 if remote else None, has_side_effects=True, vmem_limit_bytes=63 * 2**20
        ),
        name="layer",
    )(*operands)


def finish_kernel(
    gate_in, out_in, value_in, state_in, small, shared, branch_in, dx_in,
    mixed_out, tokens_out, gate_out, value_out, out_out, state_out, step, value_taps, value_bias, state_taps, state_bias, step_bias,
    log_rate, bypass, gain, mixer_gain,
    dx, sum_gate, sum_out, sum_value, sum_state, mixed, grad_tokens, gate, value, out, state, arrive, leave,
):
    loads = []
    for n, (src, dst) in enumerate(((gate_in, sum_gate), (value_in, sum_value), (out_in, sum_out), (state_in, sum_state))):
        loads.append([pltpu.make_async_copy(src, dst, arrive.at[n])])
    for n in range(4):
        loads.append([pltpu.make_async_copy(dx_in.at[n], dx.at[n], arrive.at[4 + n])])
    for group in loads:
        for cp in group:
            cp.start()
    stores = []

    def store(src, dst):
        stores.append(pltpu.make_async_copy(src, dst, leave.at[len(stores)]))
        stores[-1].start()

    mixed_load = pltpu.make_async_copy(branch_in, mixed, arrive.at[8])
    mixed_load.start()
    for n, (summed, result, home) in enumerate(
        ((sum_gate, gate, gate_out), (sum_value, value, value_out), (sum_out, out, out_out))
    ):
        loads[n][0].wait()
        for i in range(4):
            for stream in range(2):
                if n < 2:
                    rows, columns = pl.ds(i * 384, 384), pl.ds(stream * 384, 384)
                else:
                    rows, columns = pl.ds(i % 2 * 384, 384), pl.ds(i // 2 * 768 + stream * 384, 384)
                result[rows, columns] = summed[stream, i].astype(jnp.float32).reshape(384, 384)
            if n < 2:
                store(result.at[rows], home.at[rows])
            elif i > 1:
                store(result.at[rows], home.at[rows])
    blocks = [small[j // 4, j % 4].astype(jnp.float32) for j in range(12)]
    step[...] = jnp.concatenate([block[0:12] for block in blocks], 1)
    rows = [block[n : n + 1] for block in blocks for n in range(12, 16)]
    channels = [jnp.concatenate(rows[6 * n : 6 * n + 6], 1) for n in range(7)]
    value_taps[...] = jnp.concatenate(channels[0:4], 0)
    value_bias[...] = channels[4].reshape(768)
    mixer_gain[...] = channels[5].reshape(768)
    bypass[...] = mul_nt(low(jnp.broadcast_to(channels[6], (16, 768))), expansion())[0:1, 0:12].reshape(12)
    step_bias[...] = rows[42][:, 0:12].reshape(12)
    log_rate[...] = rows[43][:, 0:12].reshape(12)
    gains, convs = [shared[0, j].astype(jnp.float32) for j in range(2)]
    gain[...] = jnp.concatenate([gains[n : n + 1] for n in range(12)], 1).reshape(1536)
    taps = [jnp.concatenate([convs[2 * n : 2 * n + 1], convs[2 * n + 1 : 2 * n + 2]], 1) for n in range(5)]
    state_taps[...] = jnp.concatenate(taps[0:4], 0)
    state_bias[...] = taps[4].reshape(256)
    loads[3][0].wait()
    for i in range(4):
        rows = pl.ds(i * 128, 128)
        first, second = [sum_state[stream, i].astype(jnp.float32).reshape(128, 384) for stream in range(2)]
        state[0, rows, :] = first[:, 0:256]
        state[1, rows, 0:128] = first[:, 256:384]
        state[1, rows, 128:256] = second[:, 0:128]
        state[2, rows, :] = second[:, 128:384]
    store(state, state_out)
    mixed_load.wait()
    store(mixed, mixed_out)
    for n in range(4):
        loads[4 + n][0].wait()
        rows = pl.ds(n * 256, 256)
        grad_tokens[rows, :] = dx[n].astype(jnp.float32)
        store(grad_tokens.at[rows], tokens_out.at[rows])
    for cp in stores:
        cp.wait()


def finished(*sums):
    f32, bf16 = jnp.float32, jnp.bfloat16
    large = [((1024, 1536), bf16), ((1024, 1536), f32), ((1536, 768), f32), ((1536, 768), f32), ((768, 1536), f32), ((3, 512, 256), f32)]
    rest = [((12, 1536), f32), ((4, 768), f32), ((768,), f32), ((4, 256), f32), ((256,), f32)] + [((12,), f32)] * 3
    rest += [((1536,), f32), ((768,), f32)]
    scratch = [((4, 256, 1536), bf16)] + [((2, 4, 4, 96, 384), bf16)] * 3 + [((2, 4, 4, 32, 384), bf16)] + large
    vmem, hbm = pl.BlockSpec(memory_space=pltpu.VMEM), pl.BlockSpec(memory_space=pl.ANY)
    return pl.pallas_call(
        finish_kernel,
        out_shape=[jax.ShapeDtypeStruct(shape, kind) for shape, kind in large + rest],
        in_specs=[hbm, hbm, hbm, hbm, vmem, vmem, hbm, hbm],
        out_specs=[hbm] * len(large) + [vmem] * len(rest),
        scratch_shapes=[pltpu.VMEM(shape, kind) for shape, kind in scratch]
        + [pltpu.SemaphoreType.DMA((20,)), pltpu.SemaphoreType.DMA((19,))],
        compiler_params=pltpu.CompilerParams(vmem_limit_bytes=60 * 2**20),
        name="finish",
    )(*sums)


def local(
    tokens,
    segment,
    gate_proj,
    value_proj,
    state_proj,
    step_proj,
    value_conv,
    value_conv_bias,
    state_conv,
    state_conv_bias,
    step_bias,
    log_rate,
    bypass_gain,
    norm_gain,
    gated_norm_gain,
    out_proj,
    cotangent,
):
    sum_gate, sum_out, sum_value, sum_state, small, shared, branch, dx = layer(
        tokens, cotangent.reshape(2, 2, 256, 1536), gate_proj, value_proj, state_proj, out_proj.reshape(3, 256, 1536), segment, step_proj.T,
        value_conv, value_conv_bias, state_conv, state_conv_bias, norm_gain, gated_norm_gain, step_bias, log_rate, bypass_gain,
    )
    (
        mixed_out, grad_tokens, grad_gate, grad_value, grad_out, grad_state, grad_step, grad_value_conv, grad_value_bias,
        grad_state_conv, grad_state_bias, grad_step_bias, grad_log_rate, grad_bypass, grad_gain, grad_mixer_gain,
    ) = finished(
        sum_gate, sum_out, sum_value, sum_state, small, shared, branch.reshape(tokens.shape), dx.reshape(4, 256, 1536)
    )
    return (
        mixed_out,
        grad_tokens,
        grad_gate,
        grad_value,
        grad_state.reshape(state_proj.shape),
        grad_step.T,
        grad_value_conv,
        grad_value_bias,
        grad_state_conv,
        grad_state_bias,
        grad_step_bias,
        grad_log_rate,
        grad_bypass,
        grad_gain,
        grad_mixer_gain,
        grad_out,
    )


def solution(mesh):
    placed = (
        P("dp", None),
        P("dp", None),
        P(None, "tensor"),
        P(None, "tensor"),
        P(),
        P(None, "tensor"),
        P(None, "tensor"),
        P("tensor"),
        P(),
        P(),
        P("tensor"),
        P("tensor"),
        P("tensor"),
        P(),
        P("tensor"),
        P("tensor", None),
        P("dp", None),
    )
    return jax.shard_map(
        local,
        mesh=mesh,
        in_specs=placed,
        out_specs=(
            P("dp", None),
            P("dp", None),
            P(None, "tensor"),
            P(None, "tensor"),
            P(),
            P(None, "tensor"),
            P(None, "tensor"),
            P("tensor"),
            P(),
            P(),
            P("tensor"),
            P("tensor"),
            P("tensor"),
            P(),
            P("tensor"),
            P("tensor", None),
        ),
        check_vma=False,
    )
```
